32 devices in a mesh: dp: 16 (over z, y, x), fsdp: 2 (over core).
Axes of the slice: x: 2, y: 2, z: 4, core: 2. Of those that a mesh axis runs over, the one named last changes fastest.
Arguments:
- tokens: bfloat16 [64, 256, 1024], P(('dp', 'fsdp')), may hold values from -6 to 6
- lengths: int32 [64], P(('dp', 'fsdp')), may hold values from 64 to 256, as said below
- cotangent: bfloat16 [64, 256, 1024], P(('dp', 'fsdp')), may hold values from -6 to 6
- query_weight: float32 [1024, 1024], P(('dp', 'fsdp')), may hold values from -0.25 to 0.25
- key_weight: float32 [1024, 1024], P(('dp', 'fsdp')), may hold values from -0.25 to 0.25
- value_weight: float32 [1024, 1024], P(('dp', 'fsdp')), may hold values from -0.1875 to 0.1875
- output_weight: float32 [1024, 1024], P(('dp', 'fsdp')), may hold values from -0.5 to 0.5
- query_bias: float32 [1024], P(('dp', 'fsdp')), may hold values from -3 to 3
- value_bias: float32 [1024], P(('dp', 'fsdp')), may hold values from -3 to 3
- output_bias: float32 [1024], P(('dp', 'fsdp')), may hold values from -3 to 3
- first_gain: float32 [1024], P(('dp', 'fsdp')), may hold values from 0.1 to 1.9
- first_shift: float32 [1024], P(('dp', 'fsdp')), may hold values from -3 to 3
- inner_weight: float32 [1024, 4096], P(('dp', 'fsdp')), may hold values from -0.1875 to 0.1875
- inner_bias: float32 [4096], P(('dp', 'fsdp')), may hold values from -3 to 3
- outer_weight: float32 [4096, 1024], P(('dp', 'fsdp')), may hold values from -0.09375 to 0.09375
- outer_bias: float32 [1024], P(('dp', 'fsdp')), may hold values from -3 to 3
- second_gain: float32 [1024], P(('dp', 'fsdp')), may hold values from 0.1 to 1.9
- second_shift: float32 [1024], P(('dp', 'fsdp')), may hold values from -3 to 3
Outputs:
- layer_out: bfloat16 [64, 256, 1024], P(('dp', 'fsdp'))
- tokens_gradient: bfloat16 [64, 256, 1024], P(('dp', 'fsdp'))
- query_weight_gradient: float32 [1024, 1024], P(('dp', 'fsdp'))
- key_weight_gradient: float32 [1024, 1024], P(('dp', 'fsdp'))
- value_weight_gradient: float32 [1024, 1024], P(('dp', 'fsdp'))
- output_weight_gradient: float32 [1024, 1024], P(('dp', 'fsdp'))
- query_bias_gradient: float32 [1024], P(('dp', 'fsdp'))
- value_bias_gradient: float32 [1024], P(('dp', 'fsdp'))
- output_bias_gradient: float32 [1024], P(('dp', 'fsdp'))
- first_gain_gradient: float32 [1024], P(('dp', 'fsdp'))
- first_shift_gradient: float32 [1024], P(('dp', 'fsdp'))
- inner_weight_gradient: float32 [1024, 4096], P(('dp', 'fsdp'))
- inner_bias_gradient: float32 [4096], P(('dp', 'fsdp'))
- outer_weight_gradient: float32 [4096, 1024], P(('dp', 'fsdp'))
- outer_bias_gradient: float32 [1024], P(('dp', 'fsdp'))
- second_gain_gradient: float32 [1024], P(('dp', 'fsdp'))
- second_shift_gradient: float32 [1024], P(('dp', 'fsdp'))
The draws below stay inside these ranges and needn't reach their ends.
Inputs may be any that keep to these rules, and one draw needn't show every extreme that they name: `lengths`: in each aligned group of 2 sequences (those of one device) one, chosen by the seed, has length 256.
All inputs are finite; a program needn't handle non-finite values.
Results may differ from the reference program's by a relative error of at most 0.015.
The reference program's roundings to bfloat16 on the way count: a program that leaves them out, or rounds other values in their place, can miss the bound.
Values may be sent and summed in bfloat16 or wider, within the bound.
A program may use at most 256 MiB of HBM per device.

```python
import math
import jax
import jax.numpy as jnp
from jax import lax

D = 1024
HEADS = 16
HD = 64
FF = 4096
SEQ = 256
MB = 2
SEQS = 64


def draw_lengths(key, part):
    key = jax.random.fold_in(key, 5)
    first_key, second_key = jax.random.split(key)
    drawn = jax.random.randint(first_key, (SEQS,), SEQ // 4, SEQ + 1)
    groups = SEQS // MB
    chosen = jax.random.randint(second_key, (groups,), 0, MB)
    slot_index = jnp.arange(SEQS, dtype=jnp.int32)
    picked = jnp.repeat(chosen, MB, total_repeat_length=SEQS)
    return jnp.where(slot_index % MB == picked, SEQ, drawn).astype(jnp.int32)


def with_spikes(values, own_key, source, target, parts, factor):
    owner, partner = [(jnp.arange(values.shape[axis_at]) // (values.shape[axis_at] // parts)).reshape([-1 if axis == axis_at else 1 for axis in range(values.ndim)]) for axis_at in (source, target)]
    chosen = jax.random.permutation(own_key, parts)[partner]
    strong = (owner == chosen) | (owner == (partner + parts // 2) % parts)
    return jnp.where(strong, factor * values, values)


def steps_of(stream_key, dims, shards, least, largest):
    factor_of = 1.0
    for dim, shards_of in shards:
        steps = jax.random.uniform(jax.random.fold_in(jax.random.fold_in(stream_key, 6), dim), (shards_of,), jnp.float32, least / len(shards), largest / len(shards))
        factor_of = factor_of * jnp.repeat(jnp.exp(steps), dims[dim] // shards_of).reshape((-1,) + (1,) * (len(dims) - 1 - dim))
    return factor_of


def scatter_about(key, shape, scale, bound, cuts=(), kind=jnp.bfloat16):
    values = scale * jax.random.normal(key, shape, jnp.float32)
    if cuts:
        values = values * steps_of(key, shape, cuts, -0.22, 0.18)
    return jnp.clip(values, -bound, bound).astype(kind)


def noise_with(key, extent, scale, limit, shards, heavy, held_as=jnp.bfloat16):
    values = scale * jax.random.normal(key, extent, jnp.float32)
    if shards:
        values = values * steps_of(key, extent, shards, -0.22, 0.18)
    return jnp.clip(with_spikes(values, jax.random.fold_in(key, 3), *heavy), -limit, limit).astype(held_as)


def setup_inputs(seed: int = 0) -> dict:
    splits = jax.random.split(jax.random.key(seed), 19)
    tokens = noise_with(splits[0], (SEQS, SEQ, D), 1.0, 6.0, ((0, 32),), (0, 2, 32, 2.75))
    lengths = draw_lengths(jax.random.fold_in(splits[18], 71), 0)
    cotangent = scatter_about(splits[2], (SEQS, SEQ, D), 1.0, 6.0, ((0, 32),))
    query_weight = scatter_about(splits[3], (D, D), (D // 2) ** -0.5, 0.25, ((0, 32),), jnp.float32)
    key_weight = scatter_about(splits[4], (D, D), (D // 2) ** -0.5, 0.25, ((0, 32),), jnp.float32)
    value_weight = scatter_about(splits[5], (D, D), D ** -0.5, 0.1875, ((0, 32),), jnp.float32)
    output_weight = scatter_about(splits[6], (D, D), (D // 8) ** -0.5, 0.5, ((0, 32),), jnp.float32)
    query_bias = scatter_about(splits[7], (D,), 0.5, 3.0, ((0, 32),), jnp.float32)
    value_bias = scatter_about(splits[8], (D,), 0.5, 3.0, ((0, 32),), jnp.float32)
    output_bias = scatter_about(splits[9], (D,), 0.5, 3.0, ((0, 32),), jnp.float32)
    first_gain = jnp.clip(1.0 + 0.18 * jax.random.normal(splits[10], (D,), jnp.float32), 0.1, 1.9)
    first_shift = scatter_about(splits[11], (D,), 0.5, 3.0, ((0, 32),), jnp.float32)
    inner_weight = scatter_about(splits[12], (D, FF), D ** -0.5, 0.1875, ((0, 32),), jnp.float32)
    inner_bias = scatter_about(splits[13], (FF,), 0.5, 3.0, ((0, 32),), jnp.float32)
    outer_weight = scatter_about(splits[14], (FF, D), FF ** -0.5, 0.09375, ((0, 32),), jnp.float32)
    outer_bias = scatter_about(splits[15], (D,), 0.5, 3.0, ((0, 32),), jnp.float32)
    second_gain = jnp.clip(1.0 + 0.18 * jax.random.normal(splits[16], (D,), jnp.float32), 0.1, 1.9)
    second_shift = scatter_about(splits[17], (D,), 0.5, 3.0, ((0, 32),), jnp.float32)
    return {"tokens": tokens, "lengths": lengths, "cotangent": cotangent, "query_weight": query_weight, "key_weight": key_weight, "value_weight": value_weight, "output_weight": output_weight, "query_bias": query_bias, "value_bias": value_bias, "output_bias": output_bias, "first_gain": first_gain, "first_shift": first_shift, "inner_weight": inner_weight, "inner_bias": inner_bias, "outer_weight": outer_weight, "outer_bias": outer_bias, "second_gain": second_gain, "second_shift": second_shift}


@jax.custom_vjp
def low(v):
    return lax.optimization_barrier(v.astype(jnp.bfloat16)).astype(jnp.float32)

@jax.custom_vjp
def low_back(v):
    return v

def low_keep(v):
    return (low(v), None)

def low_pass(kept, grad):
    return (grad,)

def back_keep(v):
    return (v, None)

def back_low(kept, grad):
    return (low(grad),)
low.defvjp(low_keep, low_pass)
low_back.defvjp(back_keep, back_low)
epsilon = 1e-12
highest = lax.Precision.HIGHEST

def rounded(value):
    return low(low_back(value))

def normalize(hidden, gain, shift):
    center = hidden - lax.optimization_barrier(jnp.mean(hidden, axis=-1, keepdims=True))
    spread = lax.optimization_barrier(jnp.mean(center * center, axis=-1, keepdims=True))
    return center * lax.rsqrt(spread + epsilon) * gain + shift

def project(left, right):
    return jnp.einsum('gsd,de->gse', left, right, precision=highest)

def forward(tokens, params, valid_keys):
    query_weight, key_weight, value_weight, output_weight, query_bias, value_bias, output_bias, first_gain, first_shift, inner_weight, inner_bias, outer_weight, outer_bias, second_gain, second_shift = [low(param) for param in params]
    groups, length, width = tokens.shape
    queries = rounded(project(tokens, query_weight) + query_bias).reshape(groups, length, HEADS, HD)
    keys_all = rounded(project(tokens, key_weight)).reshape(groups, length, HEADS, HD)
    values_all = rounded(project(tokens, value_weight) + value_bias).reshape(groups, length, HEADS, HD)
    scores = low_back(jnp.einsum('gqhd,gkhd->ghqk', queries, keys_all, precision=highest) * (1.0 / math.sqrt(HD)))
    scores = jnp.where(valid_keys[:, None, None, :], scores, -1000000000.0)
    probs = low(jax.nn.softmax(scores, axis=-1))
    mixed = rounded(jnp.einsum('ghqk,gkhd->gqhd', probs, values_all, precision=highest).reshape(groups, length, width))
    branch = low_back(project(mixed, output_weight) + output_bias)
    first = normalize(tokens + branch, first_gain, first_shift)
    inner = low_back(project(low(first), inner_weight) + inner_bias)
    active = low(jax.nn.gelu(inner, approximate=False))
    outer = low_back(project(active, outer_weight) + outer_bias)
    return normalize(first + outer, second_gain, second_shift)

def add_pair(running, addend):
    return running + addend

def reference(tokens, lengths, cotangent, query_weight, key_weight, value_weight, output_weight, query_bias, value_bias, output_bias, first_gain, first_shift, inner_weight, inner_bias, outer_weight, outer_bias, second_gain, second_shift):
    params = (query_weight, key_weight, value_weight, output_weight, query_bias, value_bias, output_bias, first_gain, first_shift, inner_weight, inner_bias, outer_weight, outer_bias, second_gain, second_shift)
    group_size = math.gcd(SEQS, max(1, 4096 // SEQ))
    step_count = SEQS // group_size
    token_blocks = tokens.astype(jnp.float32).reshape(step_count, group_size, SEQ, D)
    cot_blocks = cotangent.astype(jnp.float32).reshape(step_count, group_size, SEQ, D)
    length_blocks = lengths.astype(jnp.int32).reshape(step_count, group_size)
    positions = jnp.arange(SEQ, dtype=jnp.int32)

    def accumulate(totals, block_item):
        token_block, cot_block, length_block = block_item
        valid_keys = positions[None, :] < length_block[:, None]

        def local_pass(inputs, weights):
            return forward(inputs, weights, valid_keys)
        result, pullback = jax.vjp(local_pass, token_block, params)
        token_grad, weight_grads = pullback(cot_block)
        totals = jax.tree.map(add_pair, totals, tuple(weight_grads))
        return (totals, (result.astype(jnp.bfloat16), token_grad.astype(jnp.bfloat16)))
    initial = tuple((jnp.zeros(param.shape, jnp.float32) for param in params))
    totals, (outputs, token_grads) = lax.scan(accumulate, initial, (token_blocks, cot_blocks, length_blocks))
    return (outputs.reshape(SEQS, SEQ, D), token_grads.reshape(SEQS, SEQ, D), totals[0], totals[1], totals[2], totals[3], totals[4], totals[5], totals[6], totals[7], totals[8], totals[9], totals[10], totals[11], totals[12], totals[13], totals[14])
```

```python
import functools
import math

import jax
import jax.numpy as jnp
from jax import lax
from jax.experimental import pallas as pl
from jax.experimental.pallas import tpu as pltpu
from jax.sharding import PartitionSpec as P

MESH = pl.DeviceIdType.MESH
COPIES = 15


class Place:
    def __init__(self):
        self.me = lax.axis_index("dp")
        self.core = lax.axis_index("fsdp")
        x, y, self.z = lax.rem(self.me, 2), lax.rem(self.me // 2, 2), self.me // 4
        self.a = x + self.core * (y - x)
        self.b = y + self.core * (x - y)
        odd = lax.rem(self.z, 2)
        self.pair, self.other = 3 - 2 * odd, 1 + 2 * odd
        self.z_pair = self.z + 1 - 2 * odd

    def chip(self, z, a, b):
        return z * 4 + (b + self.core * (a - b)) * 2 + (a + self.core * (b - a))

    def back(self, j):
        return lax.rem(self.z - j + 4, 4)

    def peers(self):
        along_z = [self.chip(lax.rem(self.z + k, 4), self.a, self.b) for k in (1, 2, 3)]
        return along_z + [self.chip(self.z, 1 - self.a, self.b), self.chip(self.z, self.a, 1 - self.b)]

    def meet(self):
        sem = pltpu.get_barrier_semaphore()
        peers = self.peers()
        for chip in peers:
            pl.semaphore_signal(sem, inc=1, device_id=(chip, self.core), device_id_type=MESH)
        pl.semaphore_signal(sem, inc=1, device_id=(self.me, 1 - self.core), device_id_type=MESH)
        pl.semaphore_wait(sem, len(peers) + 1)


class Hops:
    def __init__(self, place, send_sem, recv_sem, base):
        self.place, self.send_sem, self.recv_sem, self.base = place, send_sem, recv_sem, base
        self.started = []

    def send(self, k, source, target, chip):
        copy = pltpu.make_async_remote_copy(
            src_ref=source,
            dst_ref=target,
            send_sem=self.send_sem.at[self.base + k],
            recv_sem=self.recv_sem.at[self.base + k],
            device_id=(chip, self.place.core),
            device_id_type=MESH,
        )
        copy.start()
        self.started.append(copy)

    def arrived(self, k, block):
        pltpu.make_async_remote_copy(
            src_ref=block,
            dst_ref=block,
            send_sem=self.send_sem.at[self.base + k],
            recv_sem=self.recv_sem.at[self.base + k],
            device_id=(self.place.me, self.place.core),
            device_id_type=MESH,
        ).wait_recv()

    def finish(self):
        for copy in self.started:
            copy.wait_send()


class Gather(Hops):
    def __init__(self, place, held, *rest):
        super().__init__(place, *rest)
        self.held = held

    def pass_on(self, k, block, chip):
        self.send(k, self.held.at[block], self.held.at[block], chip)

    def along_z(self, k):
        p = self.place
        self.pass_on(k - 1, p.me, p.chip(lax.rem(p.z + k, 4), p.a, p.b))

    def along_a(self, j):
        p = self.place
        self.pass_on(3 + j, p.chip(p.back(j), p.a, p.b), p.chip(p.z, 1 - p.a, p.b))

    def along_b(self, i):
        p = self.place
        j = (0, 0, 2, 2, p.other, p.other)[i]
        a = (p.a, 1 - p.a)[i % 2]
        self.pass_on(7 + i, p.chip(p.back(j), a, p.b), p.chip(p.z, p.a, 1 - p.b))

    def to_pair(self, i):
        p = self.place
        a = (p.a, 1 - p.a)[i]
        self.pass_on(13 + i, p.chip(p.z, a, 1 - p.b), p.chip(p.z_pair, p.a, p.b))

    def wait(self, k):
        self.arrived(k, self.held.at[self.place.me])

    def step0(self):
        self.along_z(2)
        self.along_a(0)
        self.along_b(0)
        self.along_z(1)
        self.along_z(3)

    def step1(self):
        p = self.place
        self.wait(3)
        self.along_b(1)
        self.wait(7)
        self.to_pair(0)
        self.wait(1)
        self.along_a(2)
        self.along_b(2)
        self.wait(p.other - 1)
        self.along_a(p.other)
        self.along_b(4)
        self.wait(p.pair - 1)
        self.along_a(p.pair)

    def step2(self):
        p = self.place
        self.wait(8)
        self.to_pair(1)
        self.wait(5)
        self.along_b(3)
        self.wait(3 + p.other)
        self.along_b(5)

    def step3(self):
        self.wait(3 + self.place.pair)
        for k in (9, 10, 11, 12, 13, 14):
            self.wait(k)


class Reduce(Hops):
    def __init__(self, place, terms, landed, *rest):
        super().__init__(place, *rest)
        self.terms, self.landed = terms, landed

    def add(self, block, ks):
        for k in ks:
            self.arrived(k, self.landed.at[k])
        total = self.terms[block].astype(jnp.float32)
        for k in ks:
            total += self.landed[k].astype(jnp.float32)
        return total

    def add_and_send(self, k, block, ks, chip):
        if ks:
            self.terms[block] = self.add(block, ks).astype(self.terms.dtype)
        self.send(k, self.terms.at[block], self.landed.at[k], chip)

    def to_pair(self, i):
        p = self.place
        a = (p.a, 1 - p.a)[i]
        self.add_and_send(13 + i, p.chip(p.z_pair, a, 1 - p.b), (), p.chip(p.z_pair, p.a, p.b))

    def along_b(self, i):
        p = self.place
        j = (0, 0, 2, 2, p.other, p.other)[i]
        a = (p.a, 1 - p.a)[i % 2]
        ks = (13 + i,) if i < 2 else ()
        self.add_and_send(7 + i, p.chip(p.back(j), a, 1 - p.b), ks, p.chip(p.z, p.a, 1 - p.b))

    def along_a(self, j, ks):
        p = self.place
        self.add_and_send(3 + j, p.chip(p.back(j), 1 - p.a, p.b), ks, p.chip(p.z, 1 - p.a, p.b))

    def along_z(self, j, ks):
        p = self.place
        owner = p.chip(p.back(j), p.a, p.b)
        self.add_and_send(3 - j, owner, ks, owner)

    def step0(self):
        self.to_pair(0)
        self.to_pair(1)
        for i in (3, 5, 2, 4):
            self.along_b(i)
        self.along_a(self.place.pair, ())

    def step1(self):
        self.along_b(1)
        self.along_b(0)

    def step2(self):
        p = self.place
        self.along_a(2, (10,))
        self.along_a(p.other, (12,))
        self.along_a(0, (8,))

    def step3(self):
        p = self.place
        self.along_z(p.pair, (3 + p.pair,))
        self.along_z(2, (9, 5))
        self.along_z(p.other, (11, 3 + p.other))

    def result(self):
        return self.add(self.place.me, (7, 3, 0, 1, 2))


ORDER = ((0, 0), (0, 1), (1, 0), (0, 2), (1, 1), (0, 3), (2, 0), (1, 2), (2, 1), (1, 3), (2, 2), (2, 3))


def gather_kernel(
    units, vecs, out_units, out_vecs, local_sem, core_send, core_recv, send_sem, recv_sem
):
    place = Place()
    me, core = place.me, place.core
    local = [
        pltpu.make_async_copy(units.at[u], out_units.at[u, core, me], local_sem.at[u])
        for u in range(3)
    ] + [pltpu.make_async_copy(vecs, out_vecs.at[core, me], local_sem.at[3])]
    for copy in local:
        copy.start()
    place.meet()
    for copy in local:
        copy.wait()
    gathers = [
        Gather(place, out_units.at[u, core], send_sem, recv_sem, COPIES * u) for u in range(3)
    ]
    small = Gather(place, out_vecs.at[core], send_sem, recv_sem, COPIES * 3)

    def to_core(u, ref):
        return pltpu.make_async_remote_copy(
            src_ref=ref.at[core],
            dst_ref=ref.at[core],
            send_sem=core_send.at[u],
            recv_sem=core_recv.at[u],
            device_id=(me, 1 - core),
            device_id_type=MESH,
        )

    across = []
    for u, step in ORDER:
        getattr(gathers[u], f"step{step}")()
        if u == 0:
            getattr(small, f"step{step}")()
        if step == 3:
            across.append(to_core(u, out_units.at[u]))
            across[-1].start()
            if u == 0:
                across.append(to_core(3, out_vecs))
                across[-1].start()
    for each in gathers + [small]:
        each.finish()
    for copy in across:
        copy.wait()


def gather(units, vecs):
    return pl.pallas_call(
        gather_kernel,
        out_shape=(
            jax.ShapeDtypeStruct((3, 2, 16, 128, 1024), jnp.bfloat16),
            jax.ShapeDtypeStruct((2, 16, 16, 128), jnp.bfloat16),
        ),
        in_specs=[pl.BlockSpec(memory_space=pltpu.VMEM)] * 2,
        out_specs=(
            pl.BlockSpec(memory_space=pltpu.HBM),
            pl.BlockSpec(memory_space=pltpu.HBM),
        ),
        scratch_shapes=[
            pltpu.SemaphoreType.DMA((4,)),
            pltpu.SemaphoreType.DMA((4,)),
            pltpu.SemaphoreType.DMA((4,)),
            pltpu.SemaphoreType.DMA((4 * COPIES,)),
            pltpu.SemaphoreType.DMA((4 * COPIES,)),
        ],
        compiler_params=pltpu.CompilerParams(
            collective_id=0, has_side_effects=True, vmem_limit_bytes=56 << 20
        ),
    )(units, vecs)


def reduce_kernel(
    units,
    vecs,
    out_units,
    out_vecs,
    terms,
    across,
    vec_terms,
    vec_across,
    landed,
    vec_landed,
    local_sem,
    core_send,
    core_recv,
    send_sem,
    recv_sem,
):
    place = Place()
    me, core = place.me, place.core
    local = [
        pltpu.make_async_copy(units.at[core, u], terms.at[u], local_sem.at[u]) for u in range(3)
    ] + [pltpu.make_async_copy(vecs.at[core], vec_terms, local_sem.at[3])]
    for copy in local:
        copy.start()
    place.meet()
    swaps = []
    for u in (2, 1, 0, 3):
        source, target = (vecs.at[1 - core], vec_across) if u == 3 else (units.at[1 - core, u], across.at[u])
        swaps.append(
            pltpu.make_async_remote_copy(
                src_ref=source,
                dst_ref=target,
                send_sem=core_send.at[u],
                recv_sem=core_recv.at[u],
                device_id=(me, 1 - core),
                device_id_type=MESH,
            )
        )
        swaps[-1].start()
    for copy in local:
        copy.wait()
    reduces = [
        Reduce(place, terms.at[u], landed.at[u], send_sem, recv_sem, COPIES * u) for u in range(3)
    ]
    small = Reduce(place, vec_terms, vec_landed, send_sem, recv_sem, COPIES * 3)
    for n, step in ORDER:
        u = 2 - n
        if step == 0:
            swaps[n].wait_recv()

            @pl.loop(0, 16)
            def _(i):
                terms[u, i] += across[u, i]

            if u == 0:
                swaps[3].wait_recv()
                vec_terms[...] += vec_across[...]
        getattr(reduces[u], f"step{step}")()
        if u == 0:
            getattr(small, f"step{step}")()
    for u in (2, 1, 0):
        out_units[u] = reduces[u].result()
    out_vecs[...] = small.result()
    for each in reduces + [small]:
        each.finish()
    for copy in swaps:
        copy.wait_send()


def reduce(units, vecs):
    return pl.pallas_call(
        reduce_kernel,
        out_shape=(
            jax.ShapeDtypeStruct((3, 128, 1024), jnp.float32),
            jax.ShapeDtypeStruct((8, 128), jnp.float32),
        ),
        in_specs=[pl.BlockSpec(memory_space=pltpu.HBM)] * 2,
        out_specs=(
            pl.BlockSpec(memory_space=pltpu.VMEM),
            pl.BlockSpec(memory_space=pltpu.VMEM),
        ),
        scratch_shapes=[
            pltpu.VMEM((3, 16, 128, 1024), jnp.bfloat16),
            pltpu.VMEM((3, 16, 128, 1024), jnp.bfloat16),
            pltpu.VMEM((16, 8, 128), jnp.float32),
            pltpu.VMEM((16, 8, 128), jnp.float32),
            pltpu.VMEM((3, COPIES, 128, 1024), jnp.bfloat16),
            pltpu.VMEM((COPIES, 8, 128), jnp.float32),
            pltpu.SemaphoreType.DMA((4,)),
            pltpu.SemaphoreType.DMA((4,)),
            pltpu.SemaphoreType.DMA((4,)),
            pltpu.SemaphoreType.DMA((4 * COPIES,)),
            pltpu.SemaphoreType.DMA((4 * COPIES,)),
        ],
        compiler_params=pltpu.CompilerParams(
            collective_id=1, has_side_effects=True, vmem_limit_bytes=56 << 20
        ),
    )(units, vecs)


HD = 64
epsilon = 1e-12


def pieces_of(vectors):
    return jnp.concatenate(vectors).reshape(-1, 128)


def fast_device(
    tokens,
    lengths,
    cotangent,
    query_weight,
    key_weight,
    value_weight,
    output_weight,
    query_bias,
    value_bias,
    output_bias,
    first_gain,
    first_shift,
    inner_weight,
    inner_bias,
    outer_weight,
    outer_bias,
    second_gain,
    second_shift,
):
    low = jnp.bfloat16
    count, seq, width = tokens.shape
    rows = count * seq
    heads = width // HD
    scale = 1.0 / math.sqrt(HD)
    units = jnp.stack(
        [
            jnp.concatenate([query_weight, key_weight, value_weight, output_weight]).astype(low),
            inner_weight.astype(low).reshape(128, 1024),
            outer_weight.astype(low),
        ]
    )
    short = (query_bias, value_bias, output_bias, first_gain, first_shift, outer_bias, second_gain, second_shift)
    vecs = jnp.pad(jnp.concatenate(short + (inner_bias,)).astype(low).reshape(3, 128), ((0, 13), (0, 0)))
    units, vecs = gather(units, vecs)
    attn = units[0].transpose(1, 0, 2, 3).reshape(32, 4, 32, 1024).transpose(1, 0, 2, 3).reshape(4, 1024, 1024)
    query_use, key_use, value_use, output_use = attn[0], attn[1], attn[2], attn[3]
    inner_use = units[1].transpose(1, 0, 2, 3).reshape(1024, 4096)
    outer_use = units[2].transpose(1, 0, 2, 3).reshape(4096, 1024)
    flat = vecs.transpose(1, 0, 2, 3)[:, :, :3].reshape(32, 384).astype(jnp.float32)
    full = flat[:, :256].reshape(32, 8, 32).transpose(1, 0, 2).reshape(8, 1024)
    bias_query, bias_value, bias_output, gain_first, shift_first, bias_outer, gain_second, shift_second = [full[i] for i in range(8)]
    bias_inner = flat[:, 256:].reshape(4096)

    token_rows = tokens.reshape(rows, width)
    cot_rows = cotangent.reshape(rows, width).astype(jnp.float32)
    valid = jnp.arange(seq, dtype=jnp.int32)[None, :] < lengths[:, None]

    def split(array):
        return array.reshape(count, seq, heads, HD)

    queries = split((matmul(token_rows, query_use) + bias_query).astype(low))
    keys = split(matmul(token_rows, key_use).astype(low))
    values = split((matmul(token_rows, value_use) + bias_value).astype(low))
    scores = jnp.einsum("sqhd,skhd->shqk", queries, keys, preferred_element_type=jnp.float32) * scale
    scores = jnp.where(valid[:, None, None, :], scores, -1000000000.0)
    probs = jax.nn.softmax(scores, axis=-1)
    probs_low = probs.astype(low)
    mixed = (
        jnp.einsum("shqk,skhd->sqhd", probs_low, values, preferred_element_type=jnp.float32)
        .reshape(rows, width)
        .astype(low)
    )
    residual = token_rows.astype(jnp.float32) + matmul(mixed, output_use) + bias_output
    first, pull_first = jax.vjp(normalize, residual, gain_first, shift_first)
    first_low = first.astype(low)
    inner = matmul(first_low, inner_use) + bias_inner
    active, pull_gelu = jax.vjp(gelu_exact, inner)
    active = active.astype(low)
    second_in = first + matmul(active, outer_use) + bias_outer
    layer_rows, pull_second = jax.vjp(normalize, second_in, gain_second, shift_second)
    d_second, d_gain_second, d_shift_second = pull_second(cot_rows)
    d_outer = d_second.astype(low)
    outer_grad = matmul_left_t(active, d_outer)
    (d_inner,) = pull_gelu(matmul_right_t(d_outer, outer_use))
    d_inner = d_inner.astype(low)
    inner_grad = matmul_left_t(first_low, d_inner)
    d_first = matmul_right_t(d_inner, inner_use) + d_second
    d_residual, d_gain_first, d_shift_first = pull_first(d_first)
    d_branch = d_residual.astype(low)
    output_grad = matmul_left_t(mixed, d_branch)
    d_mixed = split(matmul_right_t(d_branch, output_use).astype(low))
    d_probs = jnp.einsum("sqhd,skhd->shqk", d_mixed, values, preferred_element_type=jnp.float32)
    d_values = jnp.einsum("shqk,sqhd->skhd", probs_low, d_mixed, preferred_element_type=jnp.float32)
    delta = jnp.sum(probs * d_probs, axis=-1, keepdims=True)
    d_scores = (probs * (d_probs - delta)).astype(low)
    d_queries = jnp.einsum("shqk,skhd->sqhd", d_scores, keys, preferred_element_type=jnp.float32) * scale
    d_keys = jnp.einsum("shqk,sqhd->skhd", d_scores, queries, preferred_element_type=jnp.float32) * scale
    d_queries, d_keys, d_values = [
        each.reshape(rows, width).astype(low) for each in (d_queries, d_keys, d_values)
    ]
    token_grad = (
        d_residual
        + matmul_right_t(d_queries, query_use)
        + matmul_right_t(d_keys, key_use)
        + matmul_right_t(d_values, value_use)
    )
    attn_grad = [matmul_left_t(token_rows, each) for each in (d_queries, d_keys, d_values)] + [output_grad]
    attn_grad = jnp.stack([each.astype(low) for each in attn_grad])

    def by_core(grads):
        return grads.reshape(16, 2, 128, 1024).transpose(1, 0, 2, 3)

    units = jnp.stack(
        [
            by_core(attn_grad.reshape(4, 32, 32, 1024).transpose(1, 0, 2, 3)),
            by_core(inner_grad.astype(low)),
            by_core(outer_grad.astype(low)),
        ],
        axis=1,
    )
    vectors = jnp.stack(
        [
            row_sum(d_queries),
            row_sum(d_values),
            row_sum(d_branch),
            d_gain_first,
            d_shift_first,
            row_sum(d_outer),
            d_gain_second,
            d_shift_second,
        ]
    )
    flat = jnp.concatenate(
        [vectors.reshape(8, 32, 32).transpose(1, 0, 2).reshape(32, 256), row_sum(d_inner).reshape(32, 128)], axis=1
    )
    vecs = jnp.pad(flat.reshape(16, 2, 3, 128).transpose(1, 0, 2, 3), ((0, 0), (0, 0), (0, 5), (0, 0)))
    units, vecs = reduce(units, vecs)
    flat = vecs[:3].reshape(384)
    part = [flat[32 * i : 32 * i + 32] for i in range(8)]
    return (
        layer_rows.astype(low).reshape(count, seq, width),
        token_grad.astype(low).reshape(count, seq, width),
        units[0, 0:32],
        units[0, 32:64],
        units[0, 64:96],
        units[0, 96:128],
        part[0],
        part[1],
        part[2],
        part[3],
        part[4],
        units[1].reshape(32, 4096),
        flat[256:384],
        units[2],
        part[5],
        part[6],
        part[7],
    )

def normalize(hidden, gain, shift):
    center = hidden - jnp.mean(hidden, axis=-1, keepdims=True)
    spread = jnp.mean(center * center, axis=-1, keepdims=True)
    return center * lax.rsqrt(spread + epsilon) * gain + shift


def gelu_exact(inner):
    return jax.nn.gelu(inner, approximate=False)


def matmul(left, right):
    return jnp.dot(left, right, preferred_element_type=jnp.float32)


def matmul_left_t(left, right):
    return lax.dot_general(
        left, right, (((0,), (0,)), ((), ())), preferred_element_type=jnp.float32
    )


def matmul_right_t(left, right):
    return lax.dot_general(
        left, right, (((1,), (1,)), ((), ())), preferred_element_type=jnp.float32
    )


def row_sum(values):
    return jnp.sum(values.astype(jnp.float32), axis=0)


def per_device(
    tokens,
    lengths,
    cotangent,
    query_weight,
    key_weight,
    value_weight,
    output_weight,
    query_bias,
    value_bias,
    output_bias,
    first_gain,
    first_shift,
    inner_weight,
    inner_bias,
    outer_weight,
    outer_bias,
    second_gain,
    second_shift,
):
    attn_master = (
        query_weight,
        key_weight,
        value_weight,
        output_weight,
        query_bias,
        value_bias,
        output_bias,
        first_gain,
        first_shift,
    )
    ffn_master = (inner_weight, inner_bias, outer_weight, outer_bias, second_gain, second_shift)
    attn_half = [param.astype(jnp.bfloat16) for param in attn_master]
    ffn_half = [param.astype(jnp.bfloat16) for param in ffn_master]
    micro_count, rows, width = tokens.shape
    heads = width // HD
    owners = lax.axis_size(("dp", "fsdp"))
    scale = 1.0 / math.sqrt(HD)
    positions = jnp.arange(rows, dtype=jnp.int32)
    attn_totals = [
        jnp.zeros((param.shape[0] * owners,) + param.shape[1:], jnp.float32)
        for param in attn_master
    ]
    ffn_totals = [
        jnp.zeros((param.shape[0] * owners,) + param.shape[1:], jnp.float32) for param in ffn_master
    ]
    outputs_list = []
    token_grads_list = []
    for micro in range(micro_count):
        token_rows = tokens[micro]
        cot_rows = cotangent[micro].astype(jnp.float32)
        valid_keys = positions < lengths[micro]
        attn_full = (
            lax.all_gather(attn_half[0], ("dp", "fsdp"), axis=0, tiled=True),
            lax.all_gather(attn_half[1], ("dp", "fsdp"), axis=0, tiled=True),
            lax.all_gather(attn_half[2], ("dp", "fsdp"), axis=0, tiled=True),
            lax.all_gather(attn_half[3], ("dp", "fsdp"), axis=0, tiled=True),
            lax.all_gather(attn_half[4], ("dp", "fsdp"), axis=0, tiled=True),
            lax.all_gather(attn_half[5], ("dp", "fsdp"), axis=0, tiled=True),
            lax.all_gather(attn_half[6], ("dp", "fsdp"), axis=0, tiled=True),
            lax.all_gather(attn_half[7], ("dp", "fsdp"), axis=0, tiled=True),
            lax.all_gather(attn_half[8], ("dp", "fsdp"), axis=0, tiled=True),
        )
        query_use, key_use, value_use, output_use = (
            attn_full[0],
            attn_full[1],
            attn_full[2],
            attn_full[3],
        )
        bias_query = attn_full[4].astype(jnp.float32)
        bias_value = attn_full[5].astype(jnp.float32)
        bias_output = attn_full[6].astype(jnp.float32)
        gain_first = attn_full[7].astype(jnp.float32)
        shift_first = attn_full[8].astype(jnp.float32)
        query_rows = (matmul(token_rows, query_use) + bias_query).astype(jnp.bfloat16)
        key_rows = matmul(token_rows, key_use).astype(jnp.bfloat16)
        value_rows = (matmul(token_rows, value_use) + bias_value).astype(jnp.bfloat16)
        query_heads = query_rows.reshape(rows, heads, HD)
        key_heads = key_rows.reshape(rows, heads, HD)
        value_heads = value_rows.reshape(rows, heads, HD)

        def attention_scores():
            raw_scores = (
                jnp.einsum(
                    "qhd,khd->hqk", query_heads, key_heads, preferred_element_type=jnp.float32
                )
                * scale
            )
            return jnp.where(valid_keys[None, None, :], raw_scores, -1000000000.0)

        scores = attention_scores()
        peak = jnp.max(scores, axis=-1, keepdims=True)
        log_total = peak + jnp.log(jnp.sum(jnp.exp(scores - peak), axis=-1, keepdims=True))
        probs_low = jnp.exp(scores - log_total).astype(jnp.bfloat16)
        mixed = (
            jnp.einsum("hqk,khd->qhd", probs_low, value_heads, preferred_element_type=jnp.float32)
            .reshape(rows, width)
            .astype(jnp.bfloat16)
        )
        residual = token_rows.astype(jnp.float32) + matmul(mixed, output_use) + bias_output
        first = normalize(residual, gain_first, shift_first)
        first_low = first.astype(jnp.bfloat16)
        ffn_full = (
            lax.all_gather(ffn_half[0], ("dp", "fsdp"), axis=0, tiled=True),
            lax.all_gather(ffn_half[1], ("dp", "fsdp"), axis=0, tiled=True),
            lax.all_gather(ffn_half[2], ("dp", "fsdp"), axis=0, tiled=True),
            lax.all_gather(ffn_half[3], ("dp", "fsdp"), axis=0, tiled=True),
            lax.all_gather(ffn_half[4], ("dp", "fsdp"), axis=0, tiled=True),
            lax.all_gather(ffn_half[5], ("dp", "fsdp"), axis=0, tiled=True),
        )
        inner = matmul(first_low, ffn_full[0]) + ffn_full[1].astype(jnp.float32)
        active = gelu_exact(inner).astype(jnp.bfloat16)
        second_in = first + matmul(active, ffn_full[2]) + ffn_full[3].astype(jnp.float32)
        gain_second = ffn_full[4].astype(jnp.float32)
        shift_second = ffn_full[5].astype(jnp.float32)
        layer_rows, pull_second = jax.vjp(normalize, second_in, gain_second, shift_second)
        outputs_list.append(layer_rows.astype(jnp.bfloat16))
        ffn_full = (
            lax.all_gather(ffn_half[0], ("dp", "fsdp"), axis=0, tiled=True),
            lax.all_gather(ffn_half[1], ("dp", "fsdp"), axis=0, tiled=True),
            lax.all_gather(ffn_half[2], ("dp", "fsdp"), axis=0, tiled=True),
            lax.all_gather(ffn_half[3], ("dp", "fsdp"), axis=0, tiled=True),
            lax.all_gather(ffn_half[4], ("dp", "fsdp"), axis=0, tiled=True),
            lax.all_gather(ffn_half[5], ("dp", "fsdp"), axis=0, tiled=True),
        )
        d_second, d_gain_second, d_shift_second = pull_second(cot_rows)
        d_outer = d_second.astype(jnp.bfloat16)
        ffn_totals[2] = ffn_totals[2] + matmul_left_t(active, d_outer)
        ffn_totals[3] = ffn_totals[3] + row_sum(d_outer)
        ffn_totals[4] = ffn_totals[4] + d_gain_second
        ffn_totals[5] = ffn_totals[5] + d_shift_second
        d_active = matmul_right_t(d_outer, ffn_full[2])
        gelu_value, pull_gelu = jax.vjp(gelu_exact, inner)
        (d_inner,) = pull_gelu(d_active)
        d_inner_low = d_inner.astype(jnp.bfloat16)
        ffn_totals[0] = ffn_totals[0] + matmul_left_t(first_low, d_inner_low)
        ffn_totals[1] = ffn_totals[1] + row_sum(d_inner_low)
        d_first = matmul_right_t(d_inner_low, ffn_full[0]) + d_second
        attn_full = (
            lax.all_gather(attn_half[0], ("dp", "fsdp"), axis=0, tiled=True),
            lax.all_gather(attn_half[1], ("dp", "fsdp"), axis=0, tiled=True),
            lax.all_gather(attn_half[2], ("dp", "fsdp"), axis=0, tiled=True),
            lax.all_gather(attn_half[3], ("dp", "fsdp"), axis=0, tiled=True),
            lax.all_gather(attn_half[4], ("dp", "fsdp"), axis=0, tiled=True),
            lax.all_gather(attn_half[5], ("dp", "fsdp"), axis=0, tiled=True),
            lax.all_gather(attn_half[6], ("dp", "fsdp"), axis=0, tiled=True),
            lax.all_gather(attn_half[7], ("dp", "fsdp"), axis=0, tiled=True),
            lax.all_gather(attn_half[8], ("dp", "fsdp"), axis=0, tiled=True),
        )
        query_use, key_use, value_use, output_use = (
            attn_full[0],
            attn_full[1],
            attn_full[2],
            attn_full[3],
        )
        norm_value, pull_first = jax.vjp(
            normalize, residual, attn_full[7].astype(jnp.float32), attn_full[8].astype(jnp.float32)
        )
        d_residual, d_gain_first, d_shift_first = pull_first(d_first)
        attn_totals[7] = attn_totals[7] + d_gain_first
        attn_totals[8] = attn_totals[8] + d_shift_first
        d_branch = d_residual.astype(jnp.bfloat16)
        attn_totals[3] = attn_totals[3] + matmul_left_t(mixed, d_branch)
        attn_totals[6] = attn_totals[6] + row_sum(d_branch)
        d_mixed = matmul_right_t(d_branch, output_use).astype(jnp.bfloat16).reshape(rows, heads, HD)
        scores = attention_scores()
        probs = jnp.exp(scores - log_total)
        probs_low = probs.astype(jnp.bfloat16)
        d_probs = jnp.einsum(
            "qhd,khd->hqk", d_mixed, value_heads, preferred_element_type=jnp.float32
        )
        d_values = jnp.einsum(
            "hqk,qhd->khd", probs_low, d_mixed, preferred_element_type=jnp.float32
        ).reshape(rows, width)
        delta_rows = jnp.sum(probs * d_probs, axis=-1, keepdims=True)
        d_scores = (probs * (d_probs - delta_rows)).astype(jnp.bfloat16)
        d_queries = (
            (
                jnp.einsum("hqk,khd->qhd", d_scores, key_heads, preferred_element_type=jnp.float32)
                * scale
            )
            .reshape(rows, width)
            .astype(jnp.bfloat16)
        )
        d_keys = (
            jnp.einsum(
                "hqk,qhd->khd", d_scores, query_heads, preferred_element_type=jnp.float32
            ).reshape(rows, width)
            * scale
        )
        key_low = d_keys.astype(jnp.bfloat16)
        value_low = d_values.astype(jnp.bfloat16)
        attn_totals[0] = attn_totals[0] + matmul_left_t(token_rows, d_queries)
        attn_totals[1] = attn_totals[1] + matmul_left_t(token_rows, key_low)
        attn_totals[2] = attn_totals[2] + matmul_left_t(token_rows, value_low)
        attn_totals[4] = attn_totals[4] + row_sum(d_queries)
        attn_totals[5] = attn_totals[5] + row_sum(value_low)
        token_grad = (
            d_residual
            + matmul_right_t(d_queries, query_use)
            + matmul_right_t(key_low, key_use)
            + matmul_right_t(value_low, value_use)
        )
        token_grads_list.append(token_grad.astype(jnp.bfloat16))
    attn_shards = (
        lax.psum_scatter(attn_totals[0], ("dp", "fsdp"), scatter_dimension=0, tiled=True),
        lax.psum_scatter(attn_totals[1], ("dp", "fsdp"), scatter_dimension=0, tiled=True),
        lax.psum_scatter(attn_totals[2], ("dp", "fsdp"), scatter_dimension=0, tiled=True),
        lax.psum_scatter(attn_totals[3], ("dp", "fsdp"), scatter_dimension=0, tiled=True),
        lax.psum_scatter(attn_totals[4], ("dp", "fsdp"), scatter_dimension=0, tiled=True),
        lax.psum_scatter(attn_totals[5], ("dp", "fsdp"), scatter_dimension=0, tiled=True),
        lax.psum_scatter(attn_totals[6], ("dp", "fsdp"), scatter_dimension=0, tiled=True),
        lax.psum_scatter(attn_totals[7], ("dp", "fsdp"), scatter_dimension=0, tiled=True),
        lax.psum_scatter(attn_totals[8], ("dp", "fsdp"), scatter_dimension=0, tiled=True),
    )
    ffn_shards = (
        lax.psum_scatter(ffn_totals[0], ("dp", "fsdp"), scatter_dimension=0, tiled=True),
        lax.psum_scatter(ffn_totals[1], ("dp", "fsdp"), scatter_dimension=0, tiled=True),
        lax.psum_scatter(ffn_totals[2], ("dp", "fsdp"), scatter_dimension=0, tiled=True),
        lax.psum_scatter(ffn_totals[3], ("dp", "fsdp"), scatter_dimension=0, tiled=True),
        lax.psum_scatter(ffn_totals[4], ("dp", "fsdp"), scatter_dimension=0, tiled=True),
        lax.psum_scatter(ffn_totals[5], ("dp", "fsdp"), scatter_dimension=0, tiled=True),
    )
    return (
        jnp.stack(outputs_list),
        jnp.stack(token_grads_list),
        attn_shards[0],
        attn_shards[1],
        attn_shards[2],
        attn_shards[3],
        attn_shards[4],
        attn_shards[5],
        attn_shards[6],
        attn_shards[7],
        attn_shards[8],
        ffn_shards[0],
        ffn_shards[1],
        ffn_shards[2],
        ffn_shards[3],
        ffn_shards[4],
        ffn_shards[5],
    )


def solution(mesh):
    in_specs = (
        P(("dp", "fsdp"), None, None),
        P(("dp", "fsdp")),
        P(("dp", "fsdp"), None, None),
        P(("dp", "fsdp"), None),
        P(("dp", "fsdp"), None),
        P(("dp", "fsdp"), None),
        P(("dp", "fsdp"), None),
        P(("dp", "fsdp")),
        P(("dp", "fsdp")),
        P(("dp", "fsdp")),
        P(("dp", "fsdp")),
        P(("dp", "fsdp")),
        P(("dp", "fsdp"), None),
        P(("dp", "fsdp")),
        P(("dp", "fsdp"), None),
        P(("dp", "fsdp")),
        P(("dp", "fsdp")),
        P(("dp", "fsdp")),
    )
    out_specs = (
        P(("dp", "fsdp"), None, None),
        P(("dp", "fsdp"), None, None),
        P(("dp", "fsdp"), None),
        P(("dp", "fsdp"), None),
        P(("dp", "fsdp"), None),
        P(("dp", "fsdp"), None),
        P(("dp", "fsdp")),
        P(("dp", "fsdp")),
        P(("dp", "fsdp")),
        P(("dp", "fsdp")),
        P(("dp", "fsdp")),
        P(("dp", "fsdp"), None),
        P(("dp", "fsdp")),
        P(("dp", "fsdp"), None),
        P(("dp", "fsdp")),
        P(("dp", "fsdp")),
        P(("dp", "fsdp")),
    )
    dims = dict(mesh.shape)
    device = fast_device if dims == {"dp": 16, "fsdp": 2} else per_device
    return jax.shard_map(
        device, mesh=mesh, in_specs=in_specs, out_specs=out_specs, check_vma=False
    )
```

```python
import functools
import math

import jax
import jax.numpy as jnp
from jax import lax
from jax.experimental import pallas as pl
from jax.experimental.pallas import tpu as pltpu
from jax.sharding import PartitionSpec as P

MESH = pl.DeviceIdType.MESH
COPIES = 15
HD = 64
LOW = jnp.bfloat16
F32 = jnp.float32


class Place:
    def __init__(self):
        self.me = lax.axis_index("dp")
        self.core = lax.axis_index("fsdp")
        x, y, self.z = lax.rem(self.me, 2), lax.rem(self.me // 2, 2), self.me // 4
        self.a = x + self.core * (y - x)
        self.b = y + self.core * (x - y)
        odd = lax.rem(self.z, 2)
        self.pair, self.other = 3 - 2 * odd, 1 + 2 * odd
        self.z_pair = self.z + 1 - 2 * odd

    def chip(self, z, a, b):
        return z * 4 + (b + self.core * (a - b)) * 2 + (a + self.core * (b - a))

    def back(self, j):
        return lax.rem(self.z - j + 4, 4)

    def peers(self):
        along_z = [self.chip(lax.rem(self.z + k, 4), self.a, self.b) for k in (1, 2, 3)]
        return along_z + [self.chip(self.z, 1 - self.a, self.b), self.chip(self.z, self.a, 1 - self.b)]

    def signal_peers(self, sem):
        for chip in self.peers():
            pl.semaphore_signal(sem, inc=1, device_id=(chip, self.core), device_id_type=MESH)

    def meet(self):
        sem = pltpu.get_barrier_semaphore()
        self.signal_peers(sem)
        pl.semaphore_signal(sem, inc=1, device_id=(self.me, 1 - self.core), device_id_type=MESH)
        pl.semaphore_wait(sem, 6)


class Hops:
    def __init__(self, place, send_sem, recv_sem, base):
        self.place, self.send_sem, self.recv_sem, self.base = place, send_sem, recv_sem, base
        self.started = []

    def send(self, k, source, target, chip):
        copy = pltpu.make_async_remote_copy(
            src_ref=source,
            dst_ref=target,
            send_sem=self.send_sem.at[self.base + k],
            recv_sem=self.recv_sem.at[self.base + k],
            device_id=(chip, self.place.core),
            device_id_type=MESH,
        )
        copy.start()
        self.started.append(copy)

    def arrived(self, k, block):
        pltpu.make_async_remote_copy(
            src_ref=block,
            dst_ref=block,
            send_sem=self.send_sem.at[self.base + k],
            recv_sem=self.recv_sem.at[self.base + k],
            device_id=(self.place.me, self.place.core),
            device_id_type=MESH,
        ).wait_recv()

    def finish(self):
        for copy in self.started:
            copy.wait_send()
        self.started = []


class Gather(Hops):
    STEPS = 10

    def __init__(self, place, held, *rest):
        super().__init__(place, *rest)
        self.held = held

    def pass_on(self, k, block, chip):
        self.send(k, self.held.at[block], self.held.at[block], chip)

    def along_z(self, k):
        p = self.place
        self.pass_on(k - 1, p.me, p.chip(lax.rem(p.z + k, 4), p.a, p.b))

    def along_a(self, j):
        p = self.place
        self.pass_on(3 + j, p.chip(p.back(j), p.a, p.b), p.chip(p.z, 1 - p.a, p.b))

    def along_b(self, i):
        p = self.place
        j = (0, 0, 2, 2, p.other, p.other)[i]
        a = (p.a, 1 - p.a)[i % 2]
        self.pass_on(7 + i, p.chip(p.back(j), a, p.b), p.chip(p.z, p.a, 1 - p.b))

    def to_pair(self, i):
        p = self.place
        a = (p.a, 1 - p.a)[i]
        self.pass_on(13 + i, p.chip(p.z, a, 1 - p.b), p.chip(p.z_pair, p.a, p.b))

    def wait(self, k):
        self.arrived(k, self.held.at[self.place.me])

    def step(self, n):
        p = self.place
        if n == 0:
            self.along_z(2)
            self.along_a(0)
            self.along_b(0)
            self.along_z(1)
            self.along_z(3)
        elif n == 1:
            self.wait(3)
            self.along_b(1)
        elif n == 2:
            self.wait(7)
            self.to_pair(0)
        elif n == 3:
            self.wait(1)
            self.along_a(2)
            self.along_b(2)
        elif n == 4:
            self.wait(p.other - 1)
            self.along_a(p.other)
            self.along_b(4)
        elif n == 5:
            self.wait(p.pair - 1)
            self.along_a(p.pair)
        elif n == 6:
            self.wait(8)
            self.to_pair(1)
        elif n == 7:
            self.wait(5)
            self.along_b(3)
        elif n == 8:
            self.wait(3 + p.other)
            self.along_b(5)
        elif n == 9:
            self.wait(3 + p.pair)
        elif n == 10:
            self.wait(9)
            self.wait(10)
        elif n == 11:
            for k in (11, 12, 13, 14):
                self.wait(k)


class Reduce(Hops):
    def __init__(self, place, terms, landed, chunk, *rest):
        super().__init__(place, *rest)
        self.terms, self.landed, self.chunk = terms, landed, chunk

    def sum_into(self, block, ks, store):
        for k in ks:
            self.arrived(k, self.landed(k))
        term = self.terms(block)
        landed = [self.landed(k) for k in ks]
        rows = term.shape[0]

        def some(n):
            at = rows_at(n, self.chunk)
            total = term[at].astype(F32)
            for each in landed:
                total += each[at].astype(F32)
            store(n, total)

        if rows == self.chunk:
            some(0)
        else:
            pl.loop(0, rows // self.chunk)(some)

    def add_and_send(self, k, block, ks, chip):
        term = self.terms(block)
        if ks:

            def store(n, total):
                term[rows_at(n, self.chunk)] = total.astype(term.dtype)

            self.sum_into(block, ks, store)
        self.send(k, term, self.landed(k), chip)

    def to_pair(self, i):
        p = self.place
        a = (p.a, 1 - p.a)[i]
        self.add_and_send(13 + i, p.chip(p.z_pair, a, 1 - p.b), (), p.chip(p.z_pair, p.a, p.b))

    def along_b(self, i):
        p = self.place
        j = (0, 0, 2, 2, p.other, p.other)[i]
        a = (p.a, 1 - p.a)[i % 2]
        ks = (13 + i,) if i < 2 else ()
        self.add_and_send(7 + i, p.chip(p.back(j), a, 1 - p.b), ks, p.chip(p.z, p.a, 1 - p.b))

    def along_a(self, j, ks):
        p = self.place
        self.add_and_send(3 + j, p.chip(p.back(j), 1 - p.a, p.b), ks, p.chip(p.z, 1 - p.a, p.b))

    def along_z(self, j, ks):
        p = self.place
        owner = p.chip(p.back(j), p.a, p.b)
        self.add_and_send(3 - j, owner, ks, owner)

    def step(self, n):
        p = self.place
        if n == 0:
            self.to_pair(0)
            self.to_pair(1)
            self.along_a(p.pair, ())
        elif n == 1:
            self.along_b(3)
            self.along_b(2)
        elif n == 2:
            self.along_b(5)
            self.along_b(4)
        elif n == 3:
            self.along_b(1)
            self.along_b(0)
        elif n == 4:
            self.along_a(2, (10,))
        elif n == 5:
            self.along_a(p.other, (12,))
        elif n == 6:
            self.along_a(0, (8,))
        elif n == 7:
            self.along_z(p.pair, (3 + p.pair,))
        elif n == 8:
            self.along_z(2, (9, 5))
        elif n == 9:
            self.along_z(p.other, (11, 3 + p.other))

    def result(self, store):
        self.sum_into(self.place.me, (7, 3, 0, 1, 2), store)


class Across:
    def __init__(self, place, send_sem, recv_sem):
        self.place, self.send_sem, self.recv_sem = place, send_sem, recv_sem
        self.count = 0

    def copy(self, k, source, target):
        p = self.place
        return pltpu.make_async_remote_copy(
            src_ref=source,
            dst_ref=target,
            send_sem=self.send_sem.at[k],
            recv_sem=self.recv_sem.at[k],
            device_id=(p.me, 1 - p.core),
            device_id_type=MESH,
        )

    def send(self, source, target, here=None):
        k = self.count
        self.count += 1
        copy = self.copy(k, source, target)
        copy.start()
        landing = target if here is None else here
        return copy.wait_send, self.copy(k, landing, landing).wait_recv


def dot(left, right):
    return jnp.dot(left, right, preferred_element_type=F32)


def dot_left_t(left, right):
    return lax.dot_general(left, right, (((0,), (0,)), ((), ())), preferred_element_type=F32)


def dot_right_t(left, right):
    return lax.dot_general(left, right, (((1,), (1,)), ((), ())), preferred_element_type=F32)


def fold(values):
    rows, columns = values.shape
    return jnp.sum(values.reshape(rows // 8, 8, columns), axis=0)


def rows_at(index, size):
    if isinstance(index, int):
        return pl.ds(index * size, size)
    return pl.ds(pl.multiple_of(index * size, size), size)


SHORT = 8
BQ, BV, BO, G1, S1, B2, G2, S2 = range(SHORT)
EPSILON = 1e-12


def layer_kernel(
    tokens,
    lengths,
    cotangent,
    query_weight,
    key_weight,
    value_weight,
    output_weight,
    inner_weight,
    outer_weight,
    vecs,
    layer_out,
    token_grad,
    query_grad,
    key_grad,
    value_grad,
    output_grad,
    inner_grad,
    outer_grad,
    vec_grad,
    x_all,
    qkv,
    mix,
    acc,
    out_part,
    in_part,
    xhat,
    scale1,
    first,
    act,
    slope,
    dout,
    gbuf,
    w_qkv,
    w_o,
    w_i,
    w_2,
    t_2,
    t_i,
    t_o,
    landed_2,
    landed_i,
    landed_o,
    stage_q,
    stage_i,
    f_s,
    f_i,
    f_2,
    mask,
    vec_all,
    params,
    inner_bias,
    g_part,
    i_part,
    g_sum,
    g_other,
    v_terms,
    v_landed,
    local_sem,
    core_send,
    core_recv,
    send_sem,
    recv_sem,
    ready_sem,
):
    p = Place()
    me, core = p.me, p.core
    peer = 1 - core
    across = Across(p, core_send, core_recv)
    pending = []

    own_rows = rows_at(core, 512)
    peer_rows = rows_at(peer, 512)

    def local(k, source, target):
        return pltpu.make_async_copy(source, target, local_sem.at[k])

    loads = [
        local(0, query_weight, f_s.at[0]),
        local(1, key_weight, f_s.at[1]),
        local(2, value_weight, f_s.at[2]),
        local(3, output_weight, f_s.at[3]),
        local(4, inner_weight, f_i),
        local(5, outer_weight, f_2),
        local(6, tokens, x_all.at[own_rows]),
        local(7, cotangent, gbuf),
    ]
    for copy in loads:
        copy.start()

    places = lax.broadcasted_iota(jnp.int32, (8, 256), 1)
    seq_of = lax.broadcasted_iota(jnp.int32, (8, 256), 0)
    limit = jnp.where(seq_of == 0, lengths[0], lengths[1])
    mask[core] = jnp.where(places < limit, 1.0, 0.0).astype(F32)
    vec_all[core, me] = vecs[...]
    g_part[...] = jnp.zeros_like(g_part)
    i_part[...] = jnp.zeros_like(i_part)

    for copy in loads[:4]:
        copy.wait()
    my_rows = rows_at(core, 32)
    for n in range(3):
        w_qkv[me, my_rows, 512 * n : 512 * n + 512] = f_s[n, :, rows_at(core, 512)].astype(LOW)
        stage_q[:, 512 * n : 512 * n + 512] = f_s[n, :, rows_at(peer, 512)].astype(LOW)
    w_o[me, core] = f_s[3].astype(LOW)
    p.meet()
    sent_q, got_q = across.send(stage_q, w_qkv.at[me, my_rows], w_qkv.at[me, rows_at(peer, 32)])
    sent_m, got_m = across.send(mask.at[core], mask.at[core], mask.at[peer])
    gather_o = Gather(p, w_o.at[:, core], send_sem, recv_sem, COPIES)
    gather_v = Gather(p, vec_all.at[core], send_sem, recv_sem, 4 * COPIES)
    gather_q = Gather(p, w_qkv, send_sem, recv_sem, 0)
    gather_i = Gather(p, w_i, send_sem, recv_sem, 2 * COPIES)
    gather_2 = Gather(p, w_2, send_sem, recv_sem, 3 * COPIES)
    gather_o.step(0)
    gather_v.step(0)
    loads[4].wait()
    for n in range(16):
        here, there = 2 * n + core, 2 * n + peer
        at = slice(128 * n, 128 * n + 128)
        w_i[me, my_rows, at] = f_i[:, rows_at(here, 128)].astype(LOW)
        stage_i[:, at] = f_i[:, rows_at(there, 128)].astype(LOW)
    sent_i, got_i = across.send(stage_i, w_i.at[me, my_rows], w_i.at[me, rows_at(peer, 32)])
    got_q()
    gather_q.step(0)
    loads[6].wait()
    sent_x, got_x = across.send(x_all.at[own_rows], x_all.at[own_rows], x_all.at[peer_rows])
    loads[5].wait()
    w_2[me] = f_2[...].astype(LOW)
    got_i()
    pending += [sent_q, sent_m, sent_i, sent_x]

    def qov(n):
        gather_q.step(n)
        gather_o.step(n)
        gather_v.step(n)

    for n in (1, 2, 3, 4, 5):
        qov(n)
    gather_i.step(0)
    for n in (6, 7, 8):
        qov(n)
    for n in (1, 2):
        gather_i.step(n)
    for n in (9, 10, 11):
        qov(n)
    sent_o, got_o = across.send(
        w_o.at[rows_at(peer, 8), core], w_o.at[rows_at(peer, 8), core], w_o.at[rows_at(core, 8), peer]
    )
    sent_v, got_v = across.send(vec_all.at[core], vec_all.at[core], vec_all.at[peer])
    pending += [sent_o, sent_v]
    for n in (3, 4, 5):
        gather_i.step(n)

    got_v()
    lane_group = lax.broadcasted_iota(jnp.int32, (16, 128), 1) // 32
    for t in range(8):
        pieces = [vec_all[i % 2, 2 * t + i // 2].astype(F32) for i in range(4)]
        tile = jnp.where(
            lane_group < 2,
            jnp.where(lane_group == 0, pieces[0], pieces[1]),
            jnp.where(lane_group == 2, pieces[2], pieces[3]),
        )
        params[:, 128 * t : 128 * t + 128] = tile
    for n in range(16):
        inner_bias[:, 128 * n : 128 * n + 128] = vec_all[core, n].astype(F32)[8:16]

    def param(n):
        return params[n : n + 1, :]

    got_x()
    got_m()

    @pl.loop(0, 4)
    def _(s):
        rows = rows_at(s, 256)
        block = x_all[rows, :]
        for n in range(3):
            part = dot(block, w_qkv[:, :, 512 * n : 512 * n + 512].reshape(1024, 512))
            if n != 1:
                part = part + params[BQ if n == 0 else BV, rows_at(core, 512)][None, :]
            qkv[rows, 512 * n : 512 * n + 512] = part.astype(LOW)

    left_half = lax.broadcasted_iota(jnp.int32, (256, 128), 1) < HD

    def heads_of(s, t):
        rows = rows_at(s, 256)
        return [qkv[rows, pl.ds(pl.multiple_of(512 * n + 128 * t, 128), 128)] for n in range(3)]

    def softmax(query_half, key, valid):
        raw = dot_right_t(query_half, key)
        raw = jnp.where(valid, raw, -1000000000.0)
        grown = jnp.exp(raw - jnp.max(raw, axis=-1, keepdims=True))
        return grown * (1.0 / jnp.sum(grown, axis=-1, keepdims=True))

    def halves(pair):
        none = jnp.zeros_like(pair)
        return jnp.where(left_half, pair, none), jnp.where(left_half, none, pair)

    scale = jnp.array(1.0 / math.sqrt(HD), LOW)

    def attention(owner, n):
        s = 2 * owner + n
        valid = mask[owner, n : n + 1, :] > 0.5

        @pl.loop(0, 4)
        def _(t):
            query, key, value = heads_of(s, t)
            outs = [
                dot(softmax(half, key, valid).astype(LOW), value) for half in halves(query * scale)
            ]
            both = jnp.where(left_half, outs[0], outs[1]).astype(LOW)
            mix[rows_at(s, 256), rows_at(t, 128)] = both

    def branch(s):
        out_use = w_o[rows_at(core, 8)].reshape(512, 1024)
        return dot(mix[rows_at(s, 256), :], out_use)

    got_o()
    sent_part, got_part = [], []
    for n in range(2):
        attention(peer, n)
        at = slice(256 * n, 256 * n + 256)
        out_part[at] = branch(2 * peer + n)
        sent, got = across.send(out_part.at[at], in_part.at[at])
        sent_part.append(sent)
        got_part.append(got)
        if n == 0:
            gather_i.step(6)
            gather_i.step(7)
            gather_2.step(0)
        else:
            gather_i.step(8)
            gather_2.step(1)
    for n in range(2):
        attention(core, n)
        acc[256 * n : 256 * n + 256] = branch(2 * core + n)
        if n == 0:
            gather_i.step(9)
            gather_2.step(2)
        else:
            gather_i.step(10)
            gather_2.step(3)

    def norm_of(hidden):
        center = hidden - jnp.mean(hidden, axis=-1, keepdims=True)
        spread = jnp.mean(center * center, axis=-1, keepdims=True)
        inverse = lax.rsqrt(spread + EPSILON)
        return center * inverse, inverse

    def norm_back(grown, normal, inverse):
        along = jnp.mean(grown * normal, axis=-1, keepdims=True)
        return inverse * (grown - jnp.mean(grown, axis=-1, keepdims=True) - normal * along)

    BLOCK = 64

    def own_first(n):
        return first.at[8 * core + n]

    sent_first, got_first = [], []
    for half in range(2):
        got_part[half]()

        @pl.loop(4 * half, 4 * half + 4)
        def _(n):
            at = rows_at(n, BLOCK)
            hidden = (
                x_all[pl.ds(pl.multiple_of(512 * core + BLOCK * n, BLOCK), BLOCK), :].astype(F32)
                + acc[at]
                + in_part[at]
                + param(BO)
            )
            normal, inverse = norm_of(hidden)
            xhat[rows_at(n, 2)] = normal.reshape(2, 32, 1024)
            scale1[at] = jnp.broadcast_to(inverse, (BLOCK, 128))
            first[8 * core + n] = (normal * param(G1) + param(S1)).astype(LOW).reshape(2, 32, 1024)

        mine = pl.ds(8 * core + 4 * half, 4)
        theirs = pl.ds(8 * peer + 4 * half, 4)
        sent, got = across.send(first.at[mine], first.at[mine], first.at[theirs])
        sent_first.append(sent)
        got_first.append(got)
    for sent in sent_part:
        sent()
    pending += sent_first
    gather_2.step(4)
    gather_2.step(5)
    gather_i.step(11)

    def inner_block(rows64, act_rows):
        block = first[pl.ds(rows64, 4)].reshape(256, 1024)

        @pl.loop(0, 4)
        def _(n):
            columns = rows_at(n, 512)
            inner = dot(block, w_i[:, :, columns].reshape(1024, 512)) + inner_bias[0:1, columns]
            error = lax.erf(inner * (1.0 / math.sqrt(2.0)))
            chance = 0.5 * (1.0 + error)
            bell = jnp.exp(-0.5 * inner * inner) * (1.0 / math.sqrt(2.0 * math.pi))
            act[act_rows, columns] = (inner * chance).astype(LOW)
            slope[pl.ds(rows64, 4), :, columns] = (chance + inner * bell).astype(LOW).reshape(4, 64, 512)

    for half in range(2):
        inner_block(8 * core + 4 * half, pl.ds(pl.multiple_of(512 * core + 256 * half, 256), 256))
        gather_2.step(6 + half)
    for half in range(2):
        got_first[half]()
        inner_block(8 * peer + 4 * half, pl.ds(pl.multiple_of(512 * peer + 256 * half, 256), 256))
        if half == 0:
            gather_2.step(8)
            gather_2.step(9)

    def outer_group(chips, fresh, after=None):
        for owner, target in ((peer, out_part), (core, acc)):
            for half in range(2):
                rows = pl.ds(pl.multiple_of(512 * owner + 256 * half, 256), 256)
                left = jnp.concatenate([act[rows, rows_at(chip, 128)] for chip in chips], axis=1)
                at = slice(256 * half, 256 * half + 256)
                for n in range(2):
                    columns = slice(512 * n, 512 * n + 512)
                    right = jnp.concatenate([w_2[chip, :, columns] for chip in chips], axis=0)
                    part = dot(left, right)
                    target[at, columns] = part if fresh else target[at, columns] + part
                if after is not None and target is out_part:
                    after(half)

    outer_group([p.chip(z, p.a, p.b) for z in range(4)], True)
    outer_group([p.chip(z, 1 - p.a, p.b) for z in range(4)], False)
    gather_2.step(10)
    far = 1 - p.b
    outer_group([p.chip(p.back(j), a, far) for j in (0, 2) for a in (p.a, 1 - p.a)], False)
    gather_2.step(11)
    sent_part, got_part = [], []

    def pass_part(half):
        at = slice(256 * half, 256 * half + 256)
        sent, got = across.send(out_part.at[at], in_part.at[at])
        sent_part.append(sent)
        got_part.append(got)

    outer_group(
        [p.chip(p.back(j), a, far) for j in (p.other, p.pair) for a in (p.a, 1 - p.a)], False, pass_part
    )

    loads[7].wait()
    sent_dout, got_dout = [], []
    for half in range(2):
        got_part[half]()

        @pl.loop(4 * half, 4 * half + 4)
        def _(n):
            at = rows_at(n, BLOCK)
            hidden = xhat[rows_at(n, 2)].reshape(BLOCK, 1024) * param(G1) + param(S1) + acc[at] + in_part[at] + param(B2)
            normal, inverse = norm_of(hidden)
            given = gbuf[at].astype(F32)
            gbuf[at] = (normal * param(G2) + param(S2)).astype(LOW)
            g_part[G2] += fold(given * normal)
            g_part[S2] += fold(given)
            down = norm_back(given * param(G2), normal, inverse)
            acc[at] = down
            low = down.astype(LOW)
            g_part[B2] += fold(low.astype(F32))
            dout[pl.ds(pl.multiple_of(512 * core + BLOCK * n, BLOCK), BLOCK), :] = low

        mine = pl.ds(pl.multiple_of(512 * core + 256 * half, 256), 256)
        theirs = pl.ds(pl.multiple_of(512 * peer + 256 * half, 256), 256)
        sent, got = across.send(dout.at[mine], dout.at[mine], dout.at[theirs])
        sent_dout.append(sent)
        got_dout.append(got)
    store_out = local(8, gbuf, layer_out)
    store_out.start()

    planes = (p.z_pair, p.back(2), p.back(p.other), p.z)
    reduce_2 = Reduce(p, lambda i: t_2.at[i], lambda k: landed_2.at[k], 32, send_sem, recv_sem, 5 * COPIES)
    reduce_i = Reduce(p, lambda i: t_i.at[i], lambda k: landed_i.at[k], 32, send_sem, recv_sem, 6 * COPIES)
    reduce_o = Reduce(p, lambda i: t_o.at[i], lambda k: landed_o.at[k], 32, send_sem, recv_sem, 7 * COPIES)
    reduce_q = Reduce(
        p,
        lambda i: slope.at[i, :, pl.ds(0, 1536)],
        lambda k: w_i.at[k, :, pl.ds(0, 1536)],
        32,
        send_sem,
        recv_sem,
        8 * COPIES,
    )
    reduce_v = Reduce(p, lambda i: v_terms.at[i], lambda k: v_landed.at[k], 16, send_sem, recv_sem, 9 * COPIES)

    got_dout[0]()
    got_dout[1]()
    for step, z in enumerate(planes):
        for half in range(2):
            left = act[:, pl.ds(pl.multiple_of(512 * z + 256 * half, 256), 256)]
            part = dot_left_t(left, dout[...])
            t_2[pl.ds(4 * z + 2 * half, 2)] = part.astype(LOW).reshape(2, 128, 1024)
        if step < 3:
            reduce_2.step(step)

    def d_inner_columns(n):
        columns = rows_at(n, 512)

        @pl.loop(0, 4)
        def _(s):
            rows = rows_at(s, 256)
            back = dot_right_t(dout[rows, :], w_2[pl.ds(4 * n, 4)].reshape(512, 1024))
            bent = slope[pl.ds(4 * s, 4), :, columns].reshape(256, 512).astype(F32)
            low = (back * bent).astype(LOW)
            act[rows, columns] = low
            i_part[:, columns] += fold(low.astype(F32))

    for n in range(4):
        d_inner_columns(n)
    reduce_2.step(3)

    for step, z in enumerate(planes):
        for n in range(4):
            columns = slice(512 * n, 512 * n + 512)
            left = first[:, :, :, pl.ds(pl.multiple_of(256 * z, 256), 256)].reshape(1024, 256)
            part = dot_left_t(left, act[:, columns])
            t_i[pl.ds(4 * z, 4), :, columns] = part.astype(LOW).reshape(4, 64, 512)
        if step < 3:
            reduce_i.step(step)
        if step == 1:
            reduce_2.step(4)
        if step == 2:
            reduce_2.step(5)

    for sent in sent_part:
        sent()
    sent_part, got_part = [], []

    def d_first(owner, half, n):
        rows = pl.ds(pl.multiple_of(512 * owner + 256 * half, 256), 256)
        return dot_right_t(act[rows, :], w_i[4 * n : 4 * n + 4].reshape(256, 2048))

    for half in range(2):
        at = slice(256 * half, 256 * half + 256)
        for n in range(4):
            out_part[at, 256 * n : 256 * n + 256] = d_first(peer, half, n)
        pass_part(half)
    reduce_2.step(6)
    for half in range(2):
        at = slice(256 * half, 256 * half + 256)
        for n in range(4):
            acc[at, 256 * n : 256 * n + 256] += d_first(core, half, n)
    gather_i.finish()
    p.signal_peers(ready_sem)
    reduce_2.step(7)

    for sent in sent_dout:
        sent()
    sent_dout, got_dout = [], []
    for half in range(2):
        got_part[half]()

        @pl.loop(4 * half, 4 * half + 4)
        def _(n):
            at = rows_at(n, BLOCK)
            normal = xhat[rows_at(n, 2)].reshape(BLOCK, 1024)
            given = acc[at] + in_part[at]
            g_part[G1] += fold(given * normal)
            g_part[S1] += fold(given)
            down = norm_back(given * param(G1), normal, scale1[at, 0:1])
            acc[at] = down
            low = down.astype(LOW)
            g_part[BO] += fold(low.astype(F32))
            dout[pl.ds(pl.multiple_of(512 * core + BLOCK * n, BLOCK), BLOCK), :] = low

        mine = pl.ds(pl.multiple_of(512 * core + 256 * half, 256), 256)
        theirs = pl.ds(pl.multiple_of(512 * peer + 256 * half, 256), 256)
        sent, got = across.send(dout.at[mine], dout.at[mine], dout.at[theirs])
        sent_dout.append(sent)
        got_dout.append(got)
    reduce_2.step(8)
    reduce_i.step(3)
    got_dout[0]()
    got_dout[1]()

    for sent in sent_first:
        sent()
    pending = [each for each in pending if each not in sent_first]
    for half in range(2):
        part = dot_left_t(mix[:, 256 * half : 256 * half + 256], dout[...])
        first[4 * half : 4 * half + 4] = part.astype(LOW).reshape(4, 2, 32, 1024)
    t_o[pl.ds(8 * core, 8)] = first[0:8, core]
    sent_t, got_t = across.send(
        first.at[pl.ds(0, 8), peer], t_o.at[pl.ds(8 * core, 8)], t_o.at[pl.ds(8 * peer, 8)]
    )
    pending.append(sent_t)

    @pl.loop(0, 4)
    def _(s):
        rows = rows_at(s, 256)
        mix[rows, :] = dot_right_t(dout[rows, :], w_o[rows_at(core, 8)].reshape(512, 1024)).astype(LOW)

    got_t()
    for n in range(3):
        reduce_o.step(n)
    reduce_2.step(9)
    reduce_i.step(4)

    def attention_back(owner, n):
        s = 2 * owner + n
        valid = mask[owner, n : n + 1, :] > 0.5
        rows = rows_at(s, 256)

        @pl.loop(0, 4)
        def _(t):
            query, key, value = heads_of(s, t)
            columns = rows_at(t, 128)
            d_mix = mix[rows, columns]
            scaled = query * scale
            d_query, d_key, d_value = [], [], []
            for q_half, m_half in zip(halves(scaled), halves(d_mix)):
                probs = softmax(q_half, key, valid)
                d_probs = dot_right_t(m_half, value)
                d_value.append(dot_left_t(probs.astype(LOW), d_mix))
                delta = jnp.sum(probs * d_probs, axis=-1, keepdims=True)
                d_scores = (probs * (d_probs - delta)).astype(LOW)
                d_query.append(dot(d_scores, key))
                d_key.append(dot_left_t(d_scores, scaled))
            low_q = (jnp.where(left_half, *d_query) * (1.0 / math.sqrt(HD))).astype(LOW)
            low_k = jnp.where(left_half, *d_key).astype(LOW)
            low_v = jnp.where(left_half, *d_value).astype(LOW)
            for n_part, low in enumerate((low_q, low_k, low_v)):
                qkv[rows, pl.ds(pl.multiple_of(512 * n_part + 128 * t, 128), 128)] = low
            here = pl.ds(pl.multiple_of(512 * core + 128 * t, 128), 128)
            g_part[BQ, :, here] += fold(low_q.astype(F32))
            g_part[BV, :, here] += fold(low_v.astype(F32))

    between = {
        0: ((reduce_i, 5), (reduce_o, 3)),
        1: ((reduce_i, 6), (reduce_o, 4), (reduce_o, 5)),
        2: ((reduce_i, 7), (reduce_o, 6)),
        3: ((reduce_i, 8), (reduce_o, 7)),
    }
    for turn, (owner, n) in enumerate(((peer, 0), (peer, 1), (core, 0), (core, 1))):
        attention_back(owner, n)
        for which, step in between[turn]:
            which.step(step)

    pl.semaphore_wait(ready_sem, 5)
    for step, z in enumerate(planes):
        for n in range(3):
            columns = slice(512 * n, 512 * n + 512)
            left = x_all[:, pl.ds(pl.multiple_of(256 * z, 256), 256)]
            part = dot_left_t(left, qkv[:, columns])
            slope[pl.ds(4 * z, 4), :, columns] = part.astype(LOW).reshape(4, 64, 512)
        if step < 3:
            reduce_q.step(step)
    reduce_i.step(9)
    reduce_o.step(8)
    reduce_o.step(9)

    for n in range(SHORT):
        g_sum[n : n + 1, :] = jnp.sum(g_part[n], axis=0, keepdims=True)
    sent_g, got_g = across.send(g_sum, g_other)
    pending.append(sent_g)

    for sent in sent_part:
        sent()
    sent_part, got_part = [], []

    def d_tokens(owner, half, n):
        rows = pl.ds(pl.multiple_of(512 * owner + 256 * half, 256), 256)
        return dot_right_t(qkv[rows, :], w_qkv[4 * n : 4 * n + 4].reshape(256, 1536))

    for half in range(2):
        at = slice(256 * half, 256 * half + 256)
        for n in range(4):
            out_part[at, 256 * n : 256 * n + 256] = d_tokens(peer, half, n)
        pass_part(half)
    got_g()
    v_terms[...] = jnp.zeros_like(v_terms)
    for n in range(16):
        t = n // 2
        at = slice(128 * t, 128 * t + 128)
        v_terms[n, 0:8] = g_sum[:, at] + g_other[:, at]
        v_terms[n, 8:9] = jnp.sum(i_part[:, 128 * n : 128 * n + 128], axis=0, keepdims=True)
    for n in range(3):
        reduce_v.step(n)
    reduce_q.step(3)
    for half in range(2):
        at = slice(256 * half, 256 * half + 256)
        for n in range(4):
            acc[at, 256 * n : 256 * n + 256] += d_tokens(core, half, n)
    reduce_v.step(3)
    store_out.wait()
    for half in range(2):
        got_part[half]()

        @pl.loop(4 * half, 4 * half + 4)
        def _(n):
            at = rows_at(n, BLOCK)
            gbuf[at] = (acc[at] + in_part[at]).astype(LOW)

    store_tokens = local(9, gbuf, token_grad)
    store_tokens.start()

    def to_2(n, total):
        f_2[rows_at(n, 32)] = total

    for n in (4, 5, 6):
        reduce_q.step(n)
        reduce_v.step(n)
    reduce_2.result(to_2)
    store_2 = local(5, f_2, outer_grad)
    store_2.start()

    def halves_to(first_block):
        def store(n, total):
            xhat[first_block + 2 * n] = total[:, :1024]
            xhat[first_block + 2 * n + 1, :, : total.shape[1] - 1024] = total[:, 1024:]

        return store

    def column(block, n):
        return xhat[block + n // 8, :, 128 * (n % 8) : 128 * (n % 8) + 128]

    reduce_i.result(halves_to(0))
    sent_i, got_i = across.send(xhat.at[pl.ds(2 * peer, 2)], xhat.at[4:6])
    for n in (7, 8, 9):
        reduce_q.step(n)
        reduce_v.step(n)

    def to_o(n, total):
        f_s[3] = total

    reduce_o.result(to_o)
    store_o = local(3, f_s.at[3], output_grad)
    store_o.start()
    got_i()
    for n in range(16):
        f_i[:, rows_at(2 * n + core, 128)] = column(2 * core, n)
        f_i[:, rows_at(2 * n + peer, 128)] = column(4, n)
    store_i = local(4, f_i, inner_grad)
    store_i.start()

    def to_v(n, total):
        vec_grad[...] = total

    reduce_v.result(to_v)

    reduce_q.result(halves_to(8))
    sent_q, got_q = across.send(xhat.at[pl.ds(8 + 2 * peer, 2)], xhat.at[12:14])
    got_q()
    stores = []
    for n, target in enumerate((query_grad, key_grad, value_grad)):
        for owner, block in ((core, 8 + 2 * core), (peer, 12)):
            f_s[n, :, rows_at(owner, 512)] = xhat[block + n // 2, :, 512 * (n % 2) : 512 * (n % 2) + 512]
        stores.append(local(n, f_s.at[n], target))
        stores[-1].start()

    for each in (gather_q, gather_o, gather_i, gather_2, gather_v):
        each.finish()
    for each in (reduce_q, reduce_o, reduce_i, reduce_2, reduce_v):
        each.finish()
    for sent in pending + sent_part + sent_dout + [sent_i, sent_q]:
        sent()
    for copy in stores + [store_2, store_o, store_i, store_tokens]:
        copy.wait()


def layer(*arrays):
    def low(*shape):
        return pltpu.VMEM(shape, LOW)

    def full(*shape):
        return pltpu.VMEM(shape, F32)

    hbm = pl.BlockSpec(memory_space=pl.ANY)
    vmem = pl.BlockSpec(memory_space=pltpu.VMEM)
    smem = pl.BlockSpec(memory_space=pltpu.SMEM)
    scratch = [
        low(1024, 1024),
        low(1024, 1536),
        low(1024, 512),
        full(512, 1024),
        full(512, 1024),
        full(512, 1024),
        full(16, 32, 1024),
        full(512, 128),
        low(16, 2, 32, 1024),
        low(1024, 2048),
        low(16, 64, 2048),
        low(1024, 1024),
        low(512, 1024),
        low(16, 64, 1536),
        low(16, 2, 32, 1024),
        low(16, 64, 2048),
        low(16, 128, 1024),
        low(16, 128, 1024),
        low(16, 64, 2048),
        low(16, 32, 1024),
        low(COPIES, 128, 1024),
        low(COPIES, 64, 2048),
        low(COPIES, 32, 1024),
        low(32, 1536),
        low(32, 2048),
        full(4, 32, 1024),
        full(32, 4096),
        full(128, 1024),
        full(2, 8, 256),
        low(2, 16, 16, 128),
        full(16, 1024),
        full(8, 2048),
        full(SHORT, 8, 1024),
        full(8, 2048),
        full(8, 1024),
        full(8, 1024),
        full(16, 16, 128),
        full(COPIES, 16, 128),
        pltpu.SemaphoreType.DMA((10,)),
        pltpu.SemaphoreType.DMA((24,)),
        pltpu.SemaphoreType.DMA((24,)),
        pltpu.SemaphoreType.DMA((10 * COPIES,)),
        pltpu.SemaphoreType.DMA((10 * COPIES,)),
        pltpu.SemaphoreType.REGULAR,
    ]
    shape = jax.ShapeDtypeStruct
    return pl.pallas_call(
        layer_kernel,
        out_shape=(
            shape((512, 1024), LOW),
            shape((512, 1024), LOW),
            shape((32, 1024), F32),
            shape((32, 1024), F32),
            shape((32, 1024), F32),
            shape((32, 1024), F32),
            shape((32, 4096), F32),
            shape((128, 1024), F32),
            shape((16, 128), F32),
        ),
        in_specs=[hbm, smem] + [hbm] * 7 + [vmem],
        out_specs=(hbm,) * 8 + (vmem,),
        scratch_shapes=scratch,
        compiler_params=pltpu.CompilerParams(
            collective_id=0, has_side_effects=True, vmem_limit_bytes=VMEM_BYTES
        ),
        cost_estimate=pl.CostEstimate(flops=40_000_000_000, bytes_accessed=8 << 20, transcendentals=0),
    )(*arrays)


VMEM_BYTES = 65_400 << 10


def one_kernel_device(
    tokens,
    lengths,
    cotangent,
    query_weight,
    key_weight,
    value_weight,
    output_weight,
    query_bias,
    value_bias,
    output_bias,
    first_gain,
    first_shift,
    inner_weight,
    inner_bias,
    outer_weight,
    outer_bias,
    second_gain,
    second_shift,
):
    count, seq, width = tokens.shape
    rows = count * seq
    short = (query_bias, value_bias, output_bias, first_gain, first_shift, outer_bias, second_gain, second_shift)
    tiled = jnp.tile(jnp.stack(short).astype(LOW), (1, 4))
    vecs = jnp.concatenate([tiled, inner_bias.astype(LOW)[None], jnp.zeros((7, 128), LOW)])
    outs = layer(
        tokens.reshape(rows, width),
        lengths,
        cotangent.reshape(rows, width),
        query_weight,
        key_weight,
        value_weight,
        output_weight,
        inner_weight,
        outer_weight,
        vecs,
    )
    layer_rows, token_grad, query_g, key_g, value_g, output_g, inner_g, outer_g, vec = outs
    group = 2 * lax.rem(lax.axis_index("dp"), 2) + lax.axis_index("fsdp")
    part = lax.dynamic_slice(vec, (0, 32 * group), (SHORT, 32))
    return (
        layer_rows.reshape(count, seq, width),
        token_grad.reshape(count, seq, width),
        query_g,
        key_g,
        value_g,
        output_g,
        part[BQ],
        part[BV],
        part[BO],
        part[G1],
        part[S1],
        inner_g,
        vec[8],
        outer_g,
        part[B2],
        part[G2],
        part[S2],
    )


epsilon = 1e-12


def normalize(hidden, gain, shift):
    center = hidden - jnp.mean(hidden, axis=-1, keepdims=True)
    spread = jnp.mean(center * center, axis=-1, keepdims=True)
    return center * lax.rsqrt(spread + epsilon) * gain + shift


def gelu_exact(inner):
    return jax.nn.gelu(inner, approximate=False)


def matmul(left, right):
    return jnp.dot(left, right, preferred_element_type=jnp.float32)


def matmul_left_t(left, right):
    return lax.dot_general(
        left, right, (((0,), (0,)), ((), ())), preferred_element_type=jnp.float32
    )


def matmul_right_t(left, right):
    return lax.dot_general(
        left, right, (((1,), (1,)), ((), ())), preferred_element_type=jnp.float32
    )


def row_sum(values):
    return jnp.sum(values.astype(jnp.float32), axis=0)


def per_device(
    tokens,
    lengths,
    cotangent,
    query_weight,
    key_weight,
    value_weight,
    output_weight,
    query_bias,
    value_bias,
    output_bias,
    first_gain,
    first_shift,
    inner_weight,
    inner_bias,
    outer_weight,
    outer_bias,
    second_gain,
    second_shift,
):
    attn_master = (
        query_weight,
        key_weight,
        value_weight,
        output_weight,
        query_bias,
        value_bias,
        output_bias,
        first_gain,
        first_shift,
    )
    ffn_master = (inner_weight, inner_bias, outer_weight, outer_bias, second_gain, second_shift)
    attn_half = [param.astype(jnp.bfloat16) for param in attn_master]
    ffn_half = [param.astype(jnp.bfloat16) for param in ffn_master]
    micro_count, rows, width = tokens.shape
    heads = width // HD
    owners = lax.axis_size(("dp", "fsdp"))
    scale = 1.0 / math.sqrt(HD)
    positions = jnp.arange(rows, dtype=jnp.int32)
    attn_totals = [
        jnp.zeros((param.shape[0] * owners,) + param.shape[1:], jnp.float32)
        for param in attn_master
    ]
    ffn_totals = [
        jnp.zeros((param.shape[0] * owners,) + param.shape[1:], jnp.float32) for param in ffn_master
    ]
    outputs_list = []
    token_grads_list = []
    for micro in range(micro_count):
        token_rows = tokens[micro]
        cot_rows = cotangent[micro].astype(jnp.float32)
        valid_keys = positions < lengths[micro]
        attn_full = (
            lax.all_gather(attn_half[0], ("dp", "fsdp"), axis=0, tiled=True),
            lax.all_gather(attn_half[1], ("dp", "fsdp"), axis=0, tiled=True),
            lax.all_gather(attn_half[2], ("dp", "fsdp"), axis=0, tiled=True),
            lax.all_gather(attn_half[3], ("dp", "fsdp"), axis=0, tiled=True),
            lax.all_gather(attn_half[4], ("dp", "fsdp"), axis=0, tiled=True),
            lax.all_gather(attn_half[5], ("dp", "fsdp"), axis=0, tiled=True),
            lax.all_gather(attn_half[6], ("dp", "fsdp"), axis=0, tiled=True),
            lax.all_gather(attn_half[7], ("dp", "fsdp"), axis=0, tiled=True),
            lax.all_gather(attn_half[8], ("dp", "fsdp"), axis=0, tiled=True),
        )
        query_use, key_use, value_use, output_use = (
            attn_full[0],
            attn_full[1],
            attn_full[2],
            attn_full[3],
        )
        bias_query = attn_full[4].astype(jnp.float32)
        bias_value = attn_full[5].astype(jnp.float32)
        bias_output = attn_full[6].astype(jnp.float32)
        gain_first = attn_full[7].astype(jnp.float32)
        shift_first = attn_full[8].astype(jnp.float32)
        query_rows = (matmul(token_rows, query_use) + bias_query).astype(jnp.bfloat16)
        key_rows = matmul(token_rows, key_use).astype(jnp.bfloat16)
        value_rows = (matmul(token_rows, value_use) + bias_value).astype(jnp.bfloat16)
        query_heads = query_rows.reshape(rows, heads, HD)
        key_heads = key_rows.reshape(rows, heads, HD)
        value_heads = value_rows.reshape(rows, heads, HD)

        def attention_scores():
            raw_scores = (
                jnp.einsum(
                    "qhd,khd->hqk", query_heads, key_heads, preferred_element_type=jnp.float32
                )
                * scale
            )
            return jnp.where(valid_keys[None, None, :], raw_scores, -1000000000.0)

        scores = attention_scores()
        peak = jnp.max(scores, axis=-1, keepdims=True)
        log_total = peak + jnp.log(jnp.sum(jnp.exp(scores - peak), axis=-1, keepdims=True))
        probs_low = jnp.exp(scores - log_total).astype(jnp.bfloat16)
        mixed = (
            jnp.einsum("hqk,khd->qhd", probs_low, value_heads, preferred_element_type=jnp.float32)
            .reshape(rows, width)
            .astype(jnp.bfloat16)
        )
        residual = token_rows.astype(jnp.float32) + matmul(mixed, output_use) + bias_output
        first = normalize(residual, gain_first, shift_first)
        first_low = first.astype(jnp.bfloat16)
        ffn_full = (
            lax.all_gather(ffn_half[0], ("dp", "fsdp"), axis=0, tiled=True),
            lax.all_gather(ffn_half[1], ("dp", "fsdp"), axis=0, tiled=True),
            lax.all_gather(ffn_half[2], ("dp", "fsdp"), axis=0, tiled=True),
            lax.all_gather(ffn_half[3], ("dp", "fsdp"), axis=0, tiled=True),
            lax.all_gather(ffn_half[4], ("dp", "fsdp"), axis=0, tiled=True),
            lax.all_gather(ffn_half[5], ("dp", "fsdp"), axis=0, tiled=True),
        )
        inner = matmul(first_low, ffn_full[0]) + ffn_full[1].astype(jnp.float32)
        active = gelu_exact(inner).astype(jnp.bfloat16)
        second_in = first + matmul(active, ffn_full[2]) + ffn_full[3].astype(jnp.float32)
        gain_second = ffn_full[4].astype(jnp.float32)
        shift_second = ffn_full[5].astype(jnp.float32)
        layer_rows, pull_second = jax.vjp(normalize, second_in, gain_second, shift_second)
        outputs_list.append(layer_rows.astype(jnp.bfloat16))
        ffn_full = (
            lax.all_gather(ffn_half[0], ("dp", "fsdp"), axis=0, tiled=True),
            lax.all_gather(ffn_half[1], ("dp", "fsdp"), axis=0, tiled=True),
            lax.all_gather(ffn_half[2], ("dp", "fsdp"), axis=0, tiled=True),
            lax.all_gather(ffn_half[3], ("dp", "fsdp"), axis=0, tiled=True),
            lax.all_gather(ffn_half[4], ("dp", "fsdp"), axis=0, tiled=True),
            lax.all_gather(ffn_half[5], ("dp", "fsdp"), axis=0, tiled=True),
        )
        d_second, d_gain_second, d_shift_second = pull_second(cot_rows)
        d_outer = d_second.astype(jnp.bfloat16)
        ffn_totals[2] = ffn_totals[2] + matmul_left_t(active, d_outer)
        ffn_totals[3] = ffn_totals[3] + row_sum(d_outer)
        ffn_totals[4] = ffn_totals[4] + d_gain_second
        ffn_totals[5] = ffn_totals[5] + d_shift_second
        d_active = matmul_right_t(d_outer, ffn_full[2])
        gelu_value, pull_gelu = jax.vjp(gelu_exact, inner)
        (d_inner,) = pull_gelu(d_active)
        d_inner_low = d_inner.astype(jnp.bfloat16)
        ffn_totals[0] = ffn_totals[0] + matmul_left_t(first_low, d_inner_low)
        ffn_totals[1] = ffn_totals[1] + row_sum(d_inner_low)
        d_first = matmul_right_t(d_inner_low, ffn_full[0]) + d_second
        attn_full = (
            lax.all_gather(attn_half[0], ("dp", "fsdp"), axis=0, tiled=True),
            lax.all_gather(attn_half[1], ("dp", "fsdp"), axis=0, tiled=True),
            lax.all_gather(attn_half[2], ("dp", "fsdp"), axis=0, tiled=True),
            lax.all_gather(attn_half[3], ("dp", "fsdp"), axis=0, tiled=True),
            lax.all_gather(attn_half[4], ("dp", "fsdp"), axis=0, tiled=True),
            lax.all_gather(attn_half[5], ("dp", "fsdp"), axis=0, tiled=True),
            lax.all_gather(attn_half[6], ("dp", "fsdp"), axis=0, tiled=True),
            lax.all_gather(attn_half[7], ("dp", "fsdp"), axis=0, tiled=True),
            lax.all_gather(attn_half[8], ("dp", "fsdp"), axis=0, tiled=True),
        )
        query_use, key_use, value_use, output_use = (
            attn_full[0],
            attn_full[1],
            attn_full[2],
            attn_full[3],
        )
        norm_value, pull_first = jax.vjp(
            normalize, residual, attn_full[7].astype(jnp.float32), attn_full[8].astype(jnp.float32)
        )
        d_residual, d_gain_first, d_shift_first = pull_first(d_first)
        attn_totals[7] = attn_totals[7] + d_gain_first
        attn_totals[8] = attn_totals[8] + d_shift_first
        d_branch = d_residual.astype(jnp.bfloat16)
        attn_totals[3] = attn_totals[3] + matmul_left_t(mixed, d_branch)
        attn_totals[6] = attn_totals[6] + row_sum(d_branch)
        d_mixed = matmul_right_t(d_branch, output_use).astype(jnp.bfloat16).reshape(rows, heads, HD)
        scores = attention_scores()
        probs = jnp.exp(scores - log_total)
        probs_low = probs.astype(jnp.bfloat16)
        d_probs = jnp.einsum(
            "qhd,khd->hqk", d_mixed, value_heads, preferred_element_type=jnp.float32
        )
        d_values = jnp.einsum(
            "hqk,qhd->khd", probs_low, d_mixed, preferred_element_type=jnp.float32
        ).reshape(rows, width)
        delta_rows = jnp.sum(probs * d_probs, axis=-1, keepdims=True)
        d_scores = (probs * (d_probs - delta_rows)).astype(jnp.bfloat16)
        d_queries = (
            (
                jnp.einsum("hqk,khd->qhd", d_scores, key_heads, preferred_element_type=jnp.float32)
                * scale
            )
            .reshape(rows, width)
            .astype(jnp.bfloat16)
        )
        d_keys = (
            jnp.einsum(
                "hqk,qhd->khd", d_scores, query_heads, preferred_element_type=jnp.float32
            ).reshape(rows, width)
            * scale
        )
        key_low = d_keys.astype(jnp.bfloat16)
        value_low = d_values.astype(jnp.bfloat16)
        attn_totals[0] = attn_totals[0] + matmul_left_t(token_rows, d_queries)
        attn_totals[1] = attn_totals[1] + matmul_left_t(token_rows, key_low)
        attn_totals[2] = attn_totals[2] + matmul_left_t(token_rows, value_low)
        attn_totals[4] = attn_totals[4] + row_sum(d_queries)
        attn_totals[5] = attn_totals[5] + row_sum(value_low)
        token_grad = (
            d_residual
            + matmul_right_t(d_queries, query_use)
            + matmul_right_t(key_low, key_use)
            + matmul_right_t(value_low, value_use)
        )
        token_grads_list.append(token_grad.astype(jnp.bfloat16))
    attn_shards = (
        lax.psum_scatter(attn_totals[0], ("dp", "fsdp"), scatter_dimension=0, tiled=True),
        lax.psum_scatter(attn_totals[1], ("dp", "fsdp"), scatter_dimension=0, tiled=True),
        lax.psum_scatter(attn_totals[2], ("dp", "fsdp"), scatter_dimension=0, tiled=True),
        lax.psum_scatter(attn_totals[3], ("dp", "fsdp"), scatter_dimension=0, tiled=True),
        lax.psum_scatter(attn_totals[4], ("dp", "fsdp"), scatter_dimension=0, tiled=True),
        lax.psum_scatter(attn_totals[5], ("dp", "fsdp"), scatter_dimension=0, tiled=True),
        lax.psum_scatter(attn_totals[6], ("dp", "fsdp"), scatter_dimension=0, tiled=True),
        lax.psum_scatter(attn_totals[7], ("dp", "fsdp"), scatter_dimension=0, tiled=True),
        lax.psum_scatter(attn_totals[8], ("dp", "fsdp"), scatter_dimension=0, tiled=True),
    )
    ffn_shards = (
        lax.psum_scatter(ffn_totals[0], ("dp", "fsdp"), scatter_dimension=0, tiled=True),
        lax.psum_scatter(ffn_totals[1], ("dp", "fsdp"), scatter_dimension=0, tiled=True),
        lax.psum_scatter(ffn_totals[2], ("dp", "fsdp"), scatter_dimension=0, tiled=True),
        lax.psum_scatter(ffn_totals[3], ("dp", "fsdp"), scatter_dimension=0, tiled=True),
        lax.psum_scatter(ffn_totals[4], ("dp", "fsdp"), scatter_dimension=0, tiled=True),
        lax.psum_scatter(ffn_totals[5], ("dp", "fsdp"), scatter_dimension=0, tiled=True),
    )
    return (
        jnp.stack(outputs_list),
        jnp.stack(token_grads_list),
        attn_shards[0],
        attn_shards[1],
        attn_shards[2],
        attn_shards[3],
        attn_shards[4],
        attn_shards[5],
        attn_shards[6],
        attn_shards[7],
        attn_shards[8],
        ffn_shards[0],
        ffn_shards[1],
        ffn_shards[2],
        ffn_shards[3],
        ffn_shards[4],
        ffn_shards[5],
    )


def solution(mesh):
    in_specs = (
        P(("dp", "fsdp"), None, None),
        P(("dp", "fsdp")),
        P(("dp", "fsdp"), None, None),
        P(("dp", "fsdp"), None),
        P(("dp", "fsdp"), None),
        P(("dp", "fsdp"), None),
        P(("dp", "fsdp"), None),
        P(("dp", "fsdp")),
        P(("dp", "fsdp")),
        P(("dp", "fsdp")),
        P(("dp", "fsdp")),
        P(("dp", "fsdp")),
        P(("dp", "fsdp"), None),
        P(("dp", "fsdp")),
        P(("dp", "fsdp"), None),
        P(("dp", "fsdp")),
        P(("dp", "fsdp")),
        P(("dp", "fsdp")),
    )
    out_specs = (
        P(("dp", "fsdp"), None, None),
        P(("dp", "fsdp"), None, None),
        P(("dp", "fsdp"), None),
        P(("dp", "fsdp"), None),
        P(("dp", "fsdp"), None),
        P(("dp", "fsdp"), None),
        P(("dp", "fsdp")),
        P(("dp", "fsdp")),
        P(("dp", "fsdp")),
        P(("dp", "fsdp")),
        P(("dp", "fsdp")),
        P(("dp", "fsdp"), None),
        P(("dp", "fsdp")),
        P(("dp", "fsdp"), None),
        P(("dp", "fsdp")),
        P(("dp", "fsdp")),
        P(("dp", "fsdp")),
    )
    one_kernel = dict(mesh.shape) == {"dp": 16, "fsdp": 2}
    device = one_kernel_device if one_kernel else per_device
    return jax.shard_map(
        device, mesh=mesh, in_specs=in_specs, out_specs=out_specs, check_vma=False
    )
```

```python
import functools
import math

import jax
import jax.numpy as jnp
from jax import lax
from jax.experimental import pallas as pl
from jax.experimental.pallas import tpu as pltpu
from jax.sharding import PartitionSpec as P

MESH = pl.DeviceIdType.MESH
COPIES = 15
HD = 64
LOW = jnp.bfloat16
F32 = jnp.float32


class Place:
    def __init__(self):
        self.me = lax.axis_index("dp")
        self.core = lax.axis_index("fsdp")
        x, y, self.z = lax.rem(self.me, 2), lax.rem(self.me // 2, 2), self.me // 4
        self.a = x + self.core * (y - x)
        self.b = y + self.core * (x - y)
        odd = lax.rem(self.z, 2)
        self.pair, self.other = 3 - 2 * odd, 1 + 2 * odd
        self.z_pair = self.z + 1 - 2 * odd

    def chip(self, z, a, b):
        return z * 4 + (b + self.core * (a - b)) * 2 + (a + self.core * (b - a))

    def back(self, j):
        return lax.rem(self.z - j + 4, 4)

    def peers(self):
        along_z = [self.chip(lax.rem(self.z + k, 4), self.a, self.b) for k in (1, 2, 3)]
        return along_z + [self.chip(self.z, 1 - self.a, self.b), self.chip(self.z, self.a, 1 - self.b)]

    def signal_peers(self, sem):
        for chip in self.peers():
            pl.semaphore_signal(sem, inc=1, device_id=(chip, self.core), device_id_type=MESH)

    def announce(self):
        sem = pltpu.get_barrier_semaphore()
        self.signal_peers(sem)
        pl.semaphore_signal(sem, inc=1, device_id=(self.me, 1 - self.core), device_id_type=MESH)

    def meet(self):
        pl.semaphore_wait(pltpu.get_barrier_semaphore(), 6)


class Hops:
    def __init__(self, place, send_sem, recv_sem, base):
        self.place, self.send_sem, self.recv_sem, self.base = place, send_sem, recv_sem, base
        self.started = []

    def send(self, k, source, target, chip):
        copy = pltpu.make_async_remote_copy(
            src_ref=source,
            dst_ref=target,
            send_sem=self.send_sem.at[self.base + k],
            recv_sem=self.recv_sem.at[self.base + k],
            device_id=(chip, self.place.core),
            device_id_type=MESH,
        )
        copy.start()
        self.started.append(copy)

    def arrived(self, k, block):
        pltpu.make_async_remote_copy(
            src_ref=block,
            dst_ref=block,
            send_sem=self.send_sem.at[self.base + k],
            recv_sem=self.recv_sem.at[self.base + k],
            device_id=(self.place.me, self.place.core),
            device_id_type=MESH,
        ).wait_recv()

    def finish(self):
        for copy in self.started:
            copy.wait_send()
        self.started = []


class Gather(Hops):
    def __init__(self, place, held, *rest):
        super().__init__(place, *rest)
        self.held = held

    def pass_on(self, k, block, chip):
        self.send(k, self.held.at[block], self.held.at[block], chip)

    def wait(self, *copies):
        for k in copies:
            self.arrived(k, self.held.at[self.place.me])

    def run(self, *hops):
        for hop in hops:
            self.take(hop)

    def take(self, name):
        p = self.place
        kind, which = name
        which = {PAIR: p.pair, OTHER: p.other}.get(which, which)
        if kind == Z:
            self.pass_on(which - 1, p.me, p.chip(lax.rem(p.z + which, 4), p.a, p.b))
        elif kind == A:
            if name != A0:
                self.wait(which - 1)
            self.pass_on(3 + which, p.chip(p.back(which), p.a, p.b), p.chip(p.z, 1 - p.a, p.b))
        elif kind == B:
            j = (0, 0, 2, 2, p.other, p.other)[which]
            if which % 2:
                self.wait(3 + j)
            block = p.chip(p.back(j), (p.a, 1 - p.a)[which % 2], p.b)
            self.pass_on(7 + which, block, p.chip(p.z, p.a, 1 - p.b))
        elif kind == P_:
            self.wait(7 + which)
            block = p.chip(p.z, (p.a, 1 - p.a)[which], 1 - p.b)
            self.pass_on(13 + which, block, p.chip(p.z_pair, p.a, p.b))
        else:
            self.wait(*((), (3 + p.pair,), (9, 10), (11, 12, 13, 14))[which])


class Reduce(Hops):
    def __init__(self, place, terms, landed, chunk, *rest):
        super().__init__(place, *rest)
        self.terms, self.landed, self.chunk = terms, landed, chunk

    def sum_into(self, block, ks, store):
        for k in ks:
            self.arrived(k, self.landed(k))
        term = self.terms(block)
        landed = [self.landed(k) for k in ks]
        rows = term.shape[0]

        def some(n):
            at = rows_at(n, self.chunk)
            total = term[at].astype(F32)
            for each in landed:
                total += each[at].astype(F32)
            store(n, total)

        if rows == self.chunk:
            some(0)
        else:
            pl.loop(0, rows // self.chunk)(some)

    def add_and_send(self, k, block, ks, chip):
        term = self.terms(block)
        if ks:

            def store(n, total):
                term[rows_at(n, self.chunk)] = total.astype(term.dtype)

            self.sum_into(block, ks, store)
        self.send(k, term, self.landed(k), chip)

    def run(self, *hops):
        for hop in hops:
            self.take(hop)

    def take(self, name):
        p = self.place
        kind, which = name
        which = {PAIR: p.pair, OTHER: p.other}.get(which, which)
        if kind == P_:
            block = p.chip(p.z_pair, (p.a, 1 - p.a)[which], 1 - p.b)
            self.add_and_send(13 + which, block, (), p.chip(p.z_pair, p.a, p.b))
        elif kind == B:
            j = (0, 0, 2, 2, p.other, p.other)[which]
            block = p.chip(p.back(j), (p.a, 1 - p.a)[which % 2], 1 - p.b)
            landed = (13 + which,) if which < 2 else ()
            self.add_and_send(7 + which, block, landed, p.chip(p.z, p.a, 1 - p.b))
        elif kind == A:
            landed = {A0: (8,), A2: (10,), Ao: (12,), Ap: ()}[name]
            block = p.chip(p.back(which), 1 - p.a, p.b)
            self.add_and_send(3 + which, block, landed, p.chip(p.z, 1 - p.a, p.b))
        else:
            landed = {Z2: (9, 5), Zo: (11, 3 + p.other), Zp: (3 + p.pair,)}[name]
            owner = p.chip(p.back(which), p.a, p.b)
            self.add_and_send(3 - which, owner, landed, owner)

    def result(self, store):
        self.sum_into(self.place.me, (7, 3, 0, 1, 2), store)


class Across:
    def __init__(self, place, send_sem, recv_sem):
        self.place, self.send_sem, self.recv_sem = place, send_sem, recv_sem
        self.count = 0

    def copy(self, k, source, target):
        p = self.place
        return pltpu.make_async_remote_copy(
            src_ref=source,
            dst_ref=target,
            send_sem=self.send_sem.at[k],
            recv_sem=self.recv_sem.at[k],
            device_id=(p.me, 1 - p.core),
            device_id_type=MESH,
        )

    def send(self, source, target, here=None):
        k = self.count
        self.count += 1
        copy = self.copy(k, source, target)
        copy.start()
        landing = target if here is None else here
        return copy.wait_send, self.copy(k, landing, landing).wait_recv


def dot(left, right):
    return jnp.dot(left, right, preferred_element_type=F32)


def dot_left_t(left, right):
    return lax.dot_general(left, right, (((0,), (0,)), ((), ())), preferred_element_type=F32)


def dot_right_t(left, right):
    return lax.dot_general(left, right, (((1,), (1,)), ((), ())), preferred_element_type=F32)


def fold(values):
    rows, columns = values.shape
    return jnp.sum(values.reshape(rows // 8, 8, columns), axis=0)


def rows_at(index, size):
    if isinstance(index, int):
        return pl.ds(index * size, size)
    return pl.ds(pl.multiple_of(index * size, size), size)


Z, A, B, P_, E = range(5)
PAIR, OTHER = -1, -2
Z1, Z2, Z3, Zp, Zo = (Z, 1), (Z, 2), (Z, 3), (Z, PAIR), (Z, OTHER)
A0, A2, Ap, Ao = (A, 0), (A, 2), (A, PAIR), (A, OTHER)
B0, B1, B2, B3, B4, B5 = [(B, n) for n in range(6)]
P0, P1 = (P_, 0), (P_, 1)
E1, E2, E3 = (E, 1), (E, 2), (E, 3)
EARLY = (Z2, A0, B0, Z1, Z3)

SHORT = 8
BQ, BV, BO, G1, S1, BF, G2, S2 = range(SHORT)
EPSILON = 1e-12


def layer_kernel(
    tokens,
    lengths,
    cotangent,
    query_weight,
    key_weight,
    value_weight,
    output_weight,
    inner_weight,
    outer_weight,
    *rest,
):
    short_shards, rest = rest[: SHORT + 1], rest[SHORT + 1 :]
    layer_body(
        tokens,
        lengths,
        cotangent,
        query_weight,
        key_weight,
        value_weight,
        output_weight,
        inner_weight,
        outer_weight,
        short_shards,
        rest[-SHORT - 1 :],
        *rest[: -SHORT - 1],
    )


def layer_body(
    tokens,
    lengths,
    cotangent,
    query_weight,
    key_weight,
    value_weight,
    output_weight,
    inner_weight,
    outer_weight,
    short_shards,
    short_here,
    layer_out,
    token_grad,
    query_grad,
    key_grad,
    value_grad,
    output_grad,
    inner_grad,
    outer_grad,
    vec_grad,
    x_all,
    qkv,
    mix,
    acc,
    out_part,
    in_part,
    xhat,
    scale1,
    first,
    act,
    slope,
    dout,
    gbuf,
    w_qkv,
    w_o,
    w_i,
    w_2,
    t_2,
    t_i,
    t_o,
    landed_2,
    landed_i,
    landed_o,
    stage_q,
    stage_i,
    f_s,
    f_i,
    f_2,
    mask,
    vec_all,
    params,
    inner_bias,
    g_part,
    i_part,
    g_sum,
    g_other,
    v_terms,
    v_landed,
    v_stage,
    local_sem,
    core_send,
    core_recv,
    send_sem,
    recv_sem,
    ready_sem,
):
    p = Place()
    me, core = p.me, p.core
    peer = 1 - core
    across = Across(p, core_send, core_recv)
    pending = []

    own_rows = rows_at(core, 512)
    peer_rows = rows_at(peer, 512)

    def local(k, source, target):
        return pltpu.make_async_copy(source, target, local_sem.at[k])

    loads = [
        local(0, query_weight, f_s.at[0]),
        local(1, key_weight, f_s.at[1]),
        local(2, value_weight, f_s.at[2]),
        local(3, output_weight, f_s.at[3]),
        local(4, inner_weight, f_i),
        local(5, outer_weight, f_2),
        local(6, tokens, x_all.at[own_rows]),
        local(7, cotangent, gbuf),
    ]
    loads += [local(10 + n, short_shards[n], short_here[n]) for n in range(SHORT + 1)]
    for copy in loads:
        copy.start()

    places = lax.broadcasted_iota(jnp.int32, (8, 256), 1)
    seq_of = lax.broadcasted_iota(jnp.int32, (8, 256), 0)
    limit = jnp.where(seq_of == 0, lengths[0], lengths[1])
    mask[core] = jnp.where(places < limit, 1.0, 0.0).astype(F32)
    p.announce()
    v_stage[...] = jnp.zeros_like(v_stage)
    for copy in loads[8:]:
        copy.wait()
    for n in range(SHORT):
        v_stage[n : n + 1, 0:32] = short_here[n][...]
    v_stage[SHORT : SHORT + 1, :] = short_here[SHORT][...]
    piece = v_stage[...]
    four = piece + pltpu.roll(piece, 32, 1) + pltpu.roll(piece, 64, 1) + pltpu.roll(piece, 96, 1)
    is_short = lax.broadcasted_iota(jnp.int32, (16, 128), 0) < SHORT
    vec_all[core, me] = jnp.where(is_short, four, piece).astype(LOW)
    g_part[...] = jnp.zeros_like(g_part)
    i_part[...] = jnp.zeros_like(i_part)

    for copy in loads[:4]:
        copy.wait()
    my_rows = rows_at(core, 32)
    for n in range(3):
        w_qkv[me, my_rows, 512 * n : 512 * n + 512] = f_s[n, :, rows_at(core, 512)].astype(LOW)
        stage_q[:, 512 * n : 512 * n + 512] = f_s[n, :, rows_at(peer, 512)].astype(LOW)
    w_o[me, core] = f_s[3].astype(LOW)
    p.meet()
    sent_q, got_q = across.send(stage_q, w_qkv.at[me, my_rows], w_qkv.at[me, rows_at(peer, 32)])
    sent_m, got_m = across.send(mask.at[core], mask.at[core], mask.at[peer])
    gather_o = Gather(p, w_o.at[:, core], send_sem, recv_sem, COPIES)
    gather_v = Gather(p, vec_all.at[core], send_sem, recv_sem, 4 * COPIES)
    gather_q = Gather(p, w_qkv, send_sem, recv_sem, 0)
    gather_i = Gather(p, w_i, send_sem, recv_sem, 2 * COPIES)
    gather_2 = Gather(p, w_2, send_sem, recv_sem, 3 * COPIES)
    gather_o.run(*EARLY)
    gather_v.run(*EARLY)
    loads[4].wait()
    for n in range(16):
        here, there = 2 * n + core, 2 * n + peer
        at = slice(128 * n, 128 * n + 128)
        w_i[me, my_rows, at] = f_i[:, rows_at(here, 128)].astype(LOW)
        stage_i[:, at] = f_i[:, rows_at(there, 128)].astype(LOW)
    sent_i, got_i = across.send(stage_i, w_i.at[me, my_rows], w_i.at[me, rows_at(peer, 32)])
    got_q()
    gather_q.run(*EARLY)
    loads[6].wait()
    sent_x, got_x = across.send(x_all.at[own_rows], x_all.at[own_rows], x_all.at[peer_rows])
    loads[5].wait()
    w_2[me] = f_2[...].astype(LOW)
    got_i()
    pending += [sent_q, sent_m, sent_i, sent_x]
    sent, got = {}, {}

    def exchange(name, source, target, here=None):
        sent[name], got[name] = across.send(source, target, here)

    def done(*names):
        for name in names:
            sent.pop(name)()

    def relay_output():
        mine = rows_at(core, 8)
        theirs = rows_at(peer, 8)
        exchange("o", w_o.at[theirs, core], w_o.at[theirs, core], w_o.at[mine, peer])
        exchange("v", vec_all.at[core], vec_all.at[core], vec_all.at[peer])

    def short_params():
        got["v"]()
        lane_group = lax.broadcasted_iota(jnp.int32, (16, 128), 1) // 32
        for t in range(8):
            pieces = [vec_all[i % 2, 2 * t + i // 2].astype(F32) for i in range(4)]
            tile = jnp.where(
                lane_group < 2,
                jnp.where(lane_group == 0, pieces[0], pieces[1]),
                jnp.where(lane_group == 2, pieces[2], pieces[3]),
            )
            params[:, 128 * t : 128 * t + 128] = tile
        for n in range(16):
            inner_bias[:, 128 * n : 128 * n + 128] = vec_all[core, n].astype(F32)[8:16]
        got_x()
        got_m()

    def param(n):
        return params[n : n + 1, :]

    def project(turn):
        owner = (core, peer)[turn]

        @pl.loop(0, 2)
        def _(half):
            rows = rows_at(2 * owner + half, 256)
            block = x_all[rows, :]
            for n in range(3):
                part = dot(block, w_qkv[:, :, 512 * n : 512 * n + 512].reshape(1024, 512))
                if n != 1:
                    part = part + params[BQ if n == 0 else BV, rows_at(core, 512)][None, :]
                qkv[rows, 512 * n : 512 * n + 512] = part.astype(LOW)

    left_half = lax.broadcasted_iota(jnp.int32, (256, 128), 1) < HD

    def heads_of(s, t):
        rows = rows_at(s, 256)
        return [qkv[rows, pl.ds(pl.multiple_of(512 * n + 128 * t, 128), 128)] for n in range(3)]

    def softmax(query_half, key, valid):
        raw = dot_right_t(query_half, key)
        raw = jnp.where(valid, raw, -1000000000.0)
        grown = jnp.exp(raw - jnp.max(raw, axis=-1, keepdims=True))
        return grown * (1.0 / jnp.sum(grown, axis=-1, keepdims=True))

    def halves(pair):
        none = jnp.zeros_like(pair)
        return jnp.where(left_half, pair, none), jnp.where(left_half, none, pair)

    scale = jnp.array(1.0 / math.sqrt(HD), LOW)

    def turn_of(turn):
        return (peer, peer, core, core)[turn], turn % 2

    def attention(turn, part):
        owner, n = turn_of(turn)
        s = 2 * owner + n
        valid = mask[owner, n : n + 1, :] > 0.5

        @pl.loop(2 * part, 2 * part + 2)
        def _(t):
            query, key, value = heads_of(s, t)
            outs = [
                dot(softmax(half, key, valid).astype(LOW), value) for half in halves(query * scale)
            ]
            both = jnp.where(left_half, outs[0], outs[1]).astype(LOW)
            mix[rows_at(s, 256), rows_at(t, 128)] = both

    def part_name(half):
        return "part0" if half == 0 else "part1"

    def pass_part(half):
        at = slice(256 * half, 256 * half + 256)
        exchange(part_name(half), out_part.at[at], in_part.at[at])

    def branch(turn):
        owner, n = turn_of(turn)
        if turn == 0:
            got["o"]()
        out_use = w_o[rows_at(core, 8)].reshape(512, 1024)
        part = dot(mix[rows_at(2 * owner + n, 256), :], out_use)
        at = slice(256 * n, 256 * n + 256)
        if turn < 2:
            out_part[at] = part
            pass_part(n)
        else:
            acc[at] = part

    def norm_of(hidden):
        center = hidden - jnp.mean(hidden, axis=-1, keepdims=True)
        spread = jnp.mean(center * center, axis=-1, keepdims=True)
        inverse = lax.rsqrt(spread + EPSILON)
        return center * inverse, inverse

    def norm_back(grown, normal, inverse):
        along = jnp.mean(grown * normal, axis=-1, keepdims=True)
        return inverse * (grown - jnp.mean(grown, axis=-1, keepdims=True) - normal * along)

    BLOCK = 64

    def tokens_of(owner, n):
        return pl.ds(pl.multiple_of(512 * owner + BLOCK * n, BLOCK), BLOCK)

    def half_of(owner, half):
        return pl.ds(pl.multiple_of(512 * owner + 256 * half, 256), 256)

    def share(name, whole, half):
        exchange(name + str(half), whole.at[half_of(core, half)], whole.at[half_of(core, half)], whole.at[half_of(peer, half)])

    def norm_first(half):
        got[part_name(half)]()

        @pl.loop(4 * half, 4 * half + 4)
        def _(n):
            at = rows_at(n, BLOCK)
            hidden = x_all[tokens_of(core, n), :].astype(F32) + acc[at] + in_part[at] + param(BO)
            normal, inverse = norm_of(hidden)
            xhat[rows_at(n, 2)] = normal.reshape(2, 32, 1024)
            scale1[at] = jnp.broadcast_to(inverse, (BLOCK, 128))
            first[8 * core + n] = (normal * param(G1) + param(S1)).astype(LOW).reshape(2, 32, 1024)

        mine = pl.ds(8 * core + 4 * half, 4)
        theirs = pl.ds(8 * peer + 4 * half, 4)
        exchange("first" + str(half), first.at[mine], first.at[mine], first.at[theirs])
        if half == 1:
            done("part0", "part1")

    def inner(turn):
        owner, half = ((core, 0), (core, 1), (peer, 0), (peer, 1))[turn]
        if turn > 1:
            got["first" + str(half)]()
        rows64 = 8 * owner + 4 * half
        act_rows = half_of(owner, half)
        block = first[pl.ds(rows64, 4)].reshape(256, 1024)

        @pl.loop(0, 4)
        def _(n):
            columns = rows_at(n, 512)
            before = dot(block, w_i[:, :, columns].reshape(1024, 512)) + inner_bias[0:1, columns]
            error = lax.erf(before * (1.0 / math.sqrt(2.0)))
            chance = 0.5 * (1.0 + error)
            bell = jnp.exp(-0.5 * before * before) * (1.0 / math.sqrt(2.0 * math.pi))
            act[act_rows, columns] = (before * chance).astype(LOW)
            slope[pl.ds(rows64, 4), :, columns] = (chance + before * bell).astype(LOW).reshape(4, 64, 512)

    far = 1 - p.b

    def chips_of(group):
        if group < 2:
            a = (p.a, 1 - p.a)[group]
            return [p.chip(z, a, p.b) for z in range(4)]
        return [p.chip(p.back(j), a, far) for j in ((0, 2), (p.other, p.pair))[group - 2] for a in (p.a, 1 - p.a)]

    def outer_half(group, turn):
        owner, half = ((peer, 0), (peer, 1), (core, 0), (core, 1))[turn]
        target = out_part if turn < 2 else acc
        chips = chips_of(group)
        left = jnp.concatenate([act[half_of(owner, half), rows_at(chip, 128)] for chip in chips], axis=1)
        at = slice(256 * half, 256 * half + 256)
        for n in range(2):
            columns = slice(512 * n, 512 * n + 512)
            right = jnp.concatenate([w_2[chip, :, columns] for chip in chips], axis=0)
            part = dot(left, right)
            target[at, columns] = part if group == 0 else target[at, columns] + part
        if group == 3 and turn < 2:
            pass_part(half)

    def outer(group):
        for turn in range(4):
            outer_half(group, turn)

    def norm_second(half):
        got[part_name(half)]()
        if half == 0:
            loads[7].wait()

        @pl.loop(4 * half, 4 * half + 4)
        def _(n):
            at = rows_at(n, BLOCK)
            hidden = xhat[rows_at(n, 2)].reshape(BLOCK, 1024) * param(G1) + param(S1)
            hidden = hidden + acc[at] + in_part[at] + param(BF)
            normal, inverse = norm_of(hidden)
            given = gbuf[at].astype(F32)
            gbuf[at] = (normal * param(G2) + param(S2)).astype(LOW)
            g_part[G2] += fold(given * normal)
            g_part[S2] += fold(given)
            down = norm_back(given * param(G2), normal, inverse)
            acc[at] = down
            low = down.astype(LOW)
            g_part[BF] += fold(low.astype(F32))
            dout[tokens_of(core, n), :] = low

        share("dout", dout, half)
        if half == 1:
            store_out.start()

    store_out = local(8, gbuf, layer_out)
    planes = (p.z_pair, p.back(2), p.back(p.other), p.z)

    def outer_terms(step):
        if step == 0:
            got["dout0"]()
            got["dout1"]()
        z = planes[step]
        for half in range(2):
            left = act[:, pl.ds(pl.multiple_of(512 * z + 256 * half, 256), 256)]
            part = dot_left_t(left, dout[...])
            t_2[pl.ds(4 * z + 2 * half, 2)] = part.astype(LOW).reshape(2, 128, 1024)

    def d_inner(n):
        columns = rows_at(n, 512)

        @pl.loop(0, 4)
        def _(s):
            rows = rows_at(s, 256)
            back = dot_right_t(dout[rows, :], w_2[pl.ds(4 * n, 4)].reshape(512, 1024))
            bent = slope[pl.ds(4 * s, 4), :, columns].reshape(256, 512).astype(F32)
            low = (back * bent).astype(LOW)
            act[rows, columns] = low
            i_part[:, columns] += fold(low.astype(F32))

    def inner_terms(step):
        z = planes[step]
        for n in range(4):
            columns = slice(512 * n, 512 * n + 512)
            left = first[:, :, :, pl.ds(pl.multiple_of(256 * z, 256), 256)].reshape(1024, 256)
            part = dot_left_t(left, act[:, columns])
            t_i[pl.ds(4 * z, 4), :, columns] = part.astype(LOW).reshape(4, 64, 512)

    def d_first(turn):
        owner, half = ((peer, 0), (peer, 1), (core, 0), (core, 1))[turn]
        if turn == 0:
            done("part0", "part1")
        at = slice(256 * half, 256 * half + 256)
        for n in range(4):
            part = dot_right_t(act[half_of(owner, half), :], w_i[4 * n : 4 * n + 4].reshape(256, 2048))
            columns = slice(256 * n, 256 * n + 256)
            if turn < 2:
                out_part[at, columns] = part
            else:
                acc[at, columns] += part
        if turn < 2:
            pass_part(half)
        if turn == 3:
            gather_i.finish()
            p.signal_peers(ready_sem)

    def norm_first_back(half):
        if half == 0:
            done("dout0", "dout1")
        got[part_name(half)]()

        @pl.loop(4 * half, 4 * half + 4)
        def _(n):
            at = rows_at(n, BLOCK)
            normal = xhat[rows_at(n, 2)].reshape(BLOCK, 1024)
            given = acc[at] + in_part[at]
            g_part[G1] += fold(given * normal)
            g_part[S1] += fold(given)
            down = norm_back(given * param(G1), normal, scale1[at, 0:1])
            acc[at] = down
            low = down.astype(LOW)
            g_part[BO] += fold(low.astype(F32))
            dout[tokens_of(core, n), :] = low

        share("dout", dout, half)

    def output_terms():
        got["dout0"]()
        got["dout1"]()
        done("first0", "first1")
        for half in range(2):
            part = dot_left_t(mix[:, 256 * half : 256 * half + 256], dout[...])
            first[4 * half : 4 * half + 4] = part.astype(LOW).reshape(4, 2, 32, 1024)
        t_o[pl.ds(8 * core, 8)] = first[0:8, core]
        exchange("t", first.at[pl.ds(0, 8), peer], t_o.at[pl.ds(8 * core, 8)], t_o.at[pl.ds(8 * peer, 8)])

    def d_mixed():
        @pl.loop(0, 4)
        def _(s):
            rows = rows_at(s, 256)
            mix[rows, :] = dot_right_t(dout[rows, :], w_o[rows_at(core, 8)].reshape(512, 1024)).astype(LOW)

        got["t"]()

    def attention_back(turn, part):
        owner, n = turn_of(turn)
        s = 2 * owner + n
        valid = mask[owner, n : n + 1, :] > 0.5
        rows = rows_at(s, 256)

        @pl.loop(2 * part, 2 * part + 2)
        def _(t):
            query, key, value = heads_of(s, t)
            columns = rows_at(t, 128)
            d_mix = mix[rows, columns]
            scaled = query * scale
            d_query, d_key, d_value = [], [], []
            for q_half, m_half in zip(halves(scaled), halves(d_mix)):
                probs = softmax(q_half, key, valid)
                d_probs = dot_right_t(m_half, value)
                d_value.append(dot_left_t(probs.astype(LOW), d_mix))
                delta = jnp.sum(probs * d_probs, axis=-1, keepdims=True)
                d_scores = (probs * (d_probs - delta)).astype(LOW)
                d_query.append(dot(d_scores, key))
                d_key.append(dot_left_t(d_scores, scaled))
            low_q = (jnp.where(left_half, *d_query) * (1.0 / math.sqrt(HD))).astype(LOW)
            low_k = jnp.where(left_half, *d_key).astype(LOW)
            low_v = jnp.where(left_half, *d_value).astype(LOW)
            for n_part, low in enumerate((low_q, low_k, low_v)):
                qkv[rows, pl.ds(pl.multiple_of(512 * n_part + 128 * t, 128), 128)] = low
            here = pl.ds(pl.multiple_of(512 * core + 128 * t, 128), 128)
            g_part[BQ, :, here] += fold(low_q.astype(F32))
            g_part[BV, :, here] += fold(low_v.astype(F32))

    def query_terms(step):
        if step == 0:
            pl.semaphore_wait(ready_sem, 5)
        z = planes[step]
        for n in range(3):
            columns = slice(512 * n, 512 * n + 512)
            left = x_all[:, pl.ds(pl.multiple_of(256 * z, 256), 256)]
            part = dot_left_t(left, qkv[:, columns])
            slope[pl.ds(4 * z, 4), :, columns] = part.astype(LOW).reshape(4, 64, 512)

    def short_sums():
        for n in range(SHORT):
            g_sum[n : n + 1, :] = jnp.sum(g_part[n], axis=0, keepdims=True)
        exchange("g", g_sum, g_other)

    def short_terms():
        got["g"]()
        v_terms[...] = jnp.zeros_like(v_terms)
        for n in range(16):
            t = n // 2
            at = slice(128 * t, 128 * t + 128)
            v_terms[n, 0:8] = g_sum[:, at] + g_other[:, at]
            v_terms[n, 8:9] = jnp.sum(i_part[:, 128 * n : 128 * n + 128], axis=0, keepdims=True)

    def d_tokens(turn):
        owner, half = ((peer, 0), (peer, 1), (core, 0), (core, 1))[turn]
        if turn == 0:
            done("part0", "part1")
        at = slice(256 * half, 256 * half + 256)
        for n in range(4):
            part = dot_right_t(qkv[half_of(owner, half), :], w_qkv[4 * n : 4 * n + 4].reshape(256, 1536))
            columns = slice(256 * n, 256 * n + 256)
            if turn < 2:
                out_part[at, columns] = part
            else:
                acc[at, columns] += part
        if turn < 2:
            pass_part(half)

    store_tokens = local(9, gbuf, token_grad)

    def tokens_out():
        store_out.wait()
        for half in range(2):
            got[part_name(half)]()

            @pl.loop(4 * half, 4 * half + 4)
            def _(n):
                at = rows_at(n, BLOCK)
                gbuf[at] = (acc[at] + in_part[at]).astype(LOW)

        store_tokens.start()

    reduce_2 = Reduce(p, lambda i: t_2.at[i], lambda k: landed_2.at[k], 32, send_sem, recv_sem, 5 * COPIES)
    reduce_i = Reduce(p, lambda i: t_i.at[i], lambda k: landed_i.at[k], 32, send_sem, recv_sem, 6 * COPIES)
    reduce_o = Reduce(p, lambda i: t_o.at[i], lambda k: landed_o.at[k], 32, send_sem, recv_sem, 7 * COPIES)
    reduce_q = Reduce(
        p,
        lambda i: slope.at[i, :, pl.ds(0, 1536)],
        lambda k: w_i.at[k, :, pl.ds(0, 1536)],
        32,
        send_sem,
        recv_sem,
        8 * COPIES,
    )
    reduce_v = Reduce(p, lambda i: v_terms.at[i], lambda k: v_landed.at[k], 16, send_sem, recv_sem, 9 * COPIES)

    stores = []

    def store(k, source, target):
        stores.append(local(k, source, target))
        stores[-1].start()

    def result_2():
        def put(n, total):
            f_2[rows_at(n, 32)] = total

        reduce_2.result(put)
        store(5, f_2, outer_grad)

    def halves_to(first_block):
        def put(n, total):
            xhat[first_block + 2 * n] = total[:, :1024]
            xhat[first_block + 2 * n + 1, :, : total.shape[1] - 1024] = total[:, 1024:]

        return put

    def column(block, n):
        return xhat[block + n // 8, :, 128 * (n % 8) : 128 * (n % 8) + 128]

    def result_i():
        reduce_i.result(halves_to(0))
        exchange("i", xhat.at[pl.ds(2 * peer, 2)], xhat.at[4:6])

    def result_i_out():
        got["i"]()
        for n in range(16):
            f_i[:, rows_at(2 * n + core, 128)] = column(2 * core, n)
            f_i[:, rows_at(2 * n + peer, 128)] = column(4, n)
        store(4, f_i, inner_grad)

    def result_o():
        def put(n, total):
            f_s[3] = total

        reduce_o.result(put)
        store(3, f_s.at[3], output_grad)

    def result_v():
        def put(n, total):
            group = 2 * lax.rem(me, 2) + core
            turned = total
            for n_group in (1, 2, 3):
                turned = jnp.where(group == n_group, pltpu.roll(total, 128 - 32 * n_group, 1), turned)
            is_short = lax.broadcasted_iota(jnp.int32, (16, 128), 0) < SHORT
            vec_grad[...] = jnp.where(is_short, turned, total)

        reduce_v.result(put)

    def result_q():
        reduce_q.result(halves_to(8))
        exchange("q", xhat.at[pl.ds(8 + 2 * peer, 2)], xhat.at[12:14])

    def result_q_out():
        got["q"]()
        for n, target in enumerate((query_grad, key_grad, value_grad)):
            for owner, block in ((core, 8 + 2 * core), (peer, 12)):
                f_s[n, :, rows_at(owner, 512)] = xhat[block + n // 2, :, 512 * (n % 2) : 512 * (n % 2) + 512]
            store(n, f_s.at[n], target)

    gather_v.run(A2, P0, Ap)
    gather_q.run(B1)
    gather_o.run(P0)
    gather_i.run(A0)
    gather_v.run(B1)
    gather_o.run(Ap)
    gather_v.run(Ao)
    gather_o.run(B1)
    gather_v.run(P1, B2)
    gather_o.run(A2)
    gather_v.run(B3)
    gather_q.run(Ap)
    gather_v.run(B5)
    gather_q.run(P0)
    gather_o.run(Ao)
    gather_i.run(B0)
    gather_o.run(P1, B4)
    gather_q.run(A2)
    gather_v.run(E2, B4)
    gather_i.run(Z2)
    gather_o.run(B3)
    gather_q.run(P1, Ao)
    gather_o.run(B2)
    gather_q.run(B3, B2)
    gather_i.run(B1, Z3)
    gather_q.run(B5)
    gather_i.run(Z1)
    gather_v.run(E1)
    gather_o.run(B5)
    gather_2.run(A0)
    gather_o.run(E2)
    gather_q.run(B4)
    gather_o.run(E3)
    gather_i.run(A2)
    gather_v.run(E3)
    gather_o.run(E1)
    gather_i.run(B2)
    relay_output()
    gather_q.run(E3)
    gather_i.run(P0, Ao, B4)
    gather_2.run(Z2)
    gather_q.run(E2)
    gather_2.run(B1)
    gather_q.run(E1)
    short_params()
    project(1)
    project(0)
    attention(0, 0)
    attention(0, 1)
    gather_2.run(Z3)
    branch(0)
    gather_2.run(Z1)
    gather_i.run(B3)
    gather_2.run(B0)
    gather_i.run(B5)
    attention(1, 0)
    gather_i.run(Ap)
    attention(1, 1)
    branch(1)
    attention(2, 0)
    gather_i.run(P1)
    attention(2, 1)
    gather_2.run(Ap)
    branch(2)
    attention(3, 0)
    gather_i.run(E1)
    gather_2.run(A2)
    attention(3, 1)
    gather_2.run(P1)
    branch(3)
    norm_first(0)
    gather_2.run(B2, P0)
    norm_first(1)
    gather_2.run(Ao)
    gather_i.run(E2, E3)
    inner(0)
    gather_2.run(B3)
    inner(1)
    gather_2.run(E1)
    inner(2)
    gather_2.run(B5, B4)
    inner(3)
    outer(0)
    gather_2.run(E2)
    outer(1)
    outer(2)
    gather_2.run(E3)
    outer(3)
    norm_second(0)
    norm_second(1)
    outer_terms(0)
    reduce_2.run(Ap)
    outer_terms(1)
    reduce_2.run(P1, B2)
    outer_terms(2)
    outer_terms(3)
    reduce_2.run(B3)
    d_inner(0)
    d_inner(1)
    reduce_2.run(Zp, P0, B5)
    d_inner(2)
    reduce_2.run(B4)
    d_inner(3)
    reduce_2.run(A2)
    inner_terms(0)
    reduce_i.run(P0)
    inner_terms(1)
    inner_terms(2)
    reduce_i.run(B5)
    inner_terms(3)
    reduce_i.run(B3)
    reduce_2.run(B1)
    d_first(0)
    d_first(1)
    d_first(2)
    reduce_2.run(Ao)
    d_first(3)
    norm_first_back(0)
    norm_first_back(1)
    reduce_2.run(Z2)
    reduce_i.run(Ap, P1)
    output_terms()
    reduce_i.run(B4, B2)
    reduce_2.run(B0, A0)
    d_mixed()
    reduce_o.run(Ap)
    attention_back(0, 0)
    attention_back(0, 1)
    reduce_2.run(Zo)
    attention_back(1, 0)
    reduce_o.run(P0, B2)
    reduce_i.run(Ao)
    attention_back(1, 1)
    reduce_o.run(P1)
    attention_back(2, 0)
    reduce_i.run(A2)
    attention_back(2, 1)
    reduce_i.run(Zo, Zp)
    reduce_o.run(B3)
    reduce_i.run(B1, B0)
    attention_back(3, 0)
    attention_back(3, 1)
    reduce_o.run(B5, A2)
    short_sums()
    reduce_i.run(A0)
    query_terms(0)
    reduce_o.run(Z2, Zp)
    query_terms(1)
    reduce_o.run(B1)
    reduce_i.run(Z2)
    reduce_o.run(B4)
    short_terms()
    query_terms(2)
    reduce_o.run(Ao)
    reduce_q.run(B4, B5)
    query_terms(3)
    d_tokens(0)
    reduce_q.run(P1)
    d_tokens(1)
    reduce_v.run(B5)
    reduce_q.run(B3, Ao)
    reduce_o.run(Zo)
    reduce_q.run(Ap)
    reduce_v.run(B3, Ao)
    reduce_q.run(B2)
    reduce_v.run(A2)
    d_tokens(2)
    d_tokens(3)
    reduce_q.run(P0, Zo, A2)
    reduce_v.run(P0, P1)
    tokens_out()
    reduce_v.run(Ap)
    reduce_q.run(Z2)
    reduce_v.run(B1)
    reduce_q.run(B1)
    reduce_v.run(B4)
    reduce_o.run(A0)
    reduce_v.run(B2)
    reduce_q.run(Zp)
    reduce_v.run(A0, Zo, Z2, Zp)
    reduce_o.run(B0)
    result_2()
    reduce_q.run(B0, A0)
    result_o()
    result_i()
    reduce_v.run(B0)
    result_q()
    result_i_out()
    result_v()
    result_q_out()

    for each in (gather_q, gather_o, gather_i, gather_2, gather_v):
        each.finish()
    for each in (reduce_q, reduce_o, reduce_i, reduce_2, reduce_v):
        each.finish()
    for each in pending + list(sent.values()):
        each()
    for copy in stores + [store_tokens]:
        copy.wait()


def layer(*arrays):
    def low(*shape):
        return pltpu.VMEM(shape, LOW)

    def full(*shape):
        return pltpu.VMEM(shape, F32)

    hbm = pl.BlockSpec(memory_space=pl.ANY)
    vmem = pl.BlockSpec(memory_space=pltpu.VMEM)
    smem = pl.BlockSpec(memory_space=pltpu.SMEM)
    scratch = [
        low(1024, 1024),
        low(1024, 1536),
        low(1024, 512),
        full(512, 1024),
        full(512, 1024),
        full(512, 1024),
        full(16, 32, 1024),
        full(512, 128),
        low(16, 2, 32, 1024),
        low(1024, 2048),
        low(16, 64, 2048),
        low(1024, 1024),
        low(512, 1024),
        low(16, 64, 1536),
        low(16, 2, 32, 1024),
        low(16, 64, 2048),
        low(16, 128, 1024),
        low(16, 128, 1024),
        low(16, 64, 2048),
        low(16, 32, 1024),
        low(COPIES, 128, 1024),
        low(COPIES, 64, 2048),
        low(COPIES, 32, 1024),
        low(32, 1536),
        low(32, 2048),
        full(4, 32, 1024),
        full(32, 4096),
        full(128, 1024),
        full(2, 8, 256),
        low(2, 16, 16, 128),
        full(16, 1024),
        full(8, 2048),
        full(SHORT, 8, 1024),
        full(8, 2048),
        full(8, 1024),
        full(8, 1024),
        full(16, 16, 128),
        full(COPIES, 16, 128),
        full(16, 128),
        pltpu.SemaphoreType.DMA((19,)),
        pltpu.SemaphoreType.DMA((24,)),
        pltpu.SemaphoreType.DMA((24,)),
        pltpu.SemaphoreType.DMA((10 * COPIES,)),
        pltpu.SemaphoreType.DMA((10 * COPIES,)),
        pltpu.SemaphoreType.REGULAR,
    ] + [full(1, 32)] * SHORT + [full(1, 128)]
    shape = jax.ShapeDtypeStruct
    return pl.pallas_call(
        layer_kernel,
        out_shape=(
            shape((512, 1024), LOW),
            shape((512, 1024), LOW),
            shape((32, 1024), F32),
            shape((32, 1024), F32),
            shape((32, 1024), F32),
            shape((32, 1024), F32),
            shape((32, 4096), F32),
            shape((128, 1024), F32),
            shape((16, 128), F32),
        ),
        in_specs=[hbm, smem] + [hbm] * (7 + SHORT + 1),
        out_specs=(hbm,) * 8 + (vmem,),
        scratch_shapes=scratch,
        compiler_params=pltpu.CompilerParams(
            collective_id=0, has_side_effects=True, vmem_limit_bytes=VMEM_BYTES
        ),
        cost_estimate=pl.CostEstimate(flops=40_000_000_000, bytes_accessed=8 << 20, transcendentals=0),
    )(*arrays)


VMEM_BYTES = 65_400 << 10


def hand_over_kernel(*refs):
    sources, vec, targets, parts = refs[:8], refs[8], refs[9:17], refs[17 : 17 + SHORT + 1]
    held, (in_sem, out_sem) = refs[17 + SHORT + 1 : -2], refs[-2:]
    loads = [pltpu.make_async_copy(sources[n], held[n], in_sem.at[n]) for n in range(8)]
    stores = [pltpu.make_async_copy(held[n], targets[n], out_sem.at[n]) for n in range(8)]
    for load in loads:
        load.start()
    for n in range(SHORT):
        parts[n][...] = vec[n : n + 1, 0:32]
    parts[SHORT][...] = vec[SHORT : SHORT + 1, :]
    for load, store in zip(loads, stores):
        load.wait()
        store.start()
    for store in stores:
        store.wait()


def hand_over(*results):
    hbm = pl.BlockSpec(memory_space=pl.ANY)
    vmem = pl.BlockSpec(memory_space=pltpu.VMEM)
    shape = jax.ShapeDtypeStruct
    return pl.pallas_call(
        hand_over_kernel,
        out_shape=tuple(shape(each.shape, each.dtype) for each in results[:8])
        + (shape((1, 32), F32),) * SHORT
        + (shape((1, 128), F32),),
        in_specs=[hbm] * 8 + [vmem],
        out_specs=(hbm,) * 8 + (vmem,) * (SHORT + 1),
        scratch_shapes=[pltpu.VMEM(each.shape, each.dtype) for each in results[:8]]
        + [pltpu.SemaphoreType.DMA((8,))] * 2,
        compiler_params=pltpu.CompilerParams(vmem_limit_bytes=VMEM_BYTES),
    )(*results)


def one_kernel_device(
    tokens,
    lengths,
    cotangent,
    query_weight,
    key_weight,
    value_weight,
    output_weight,
    query_bias,
    value_bias,
    output_bias,
    first_gain,
    first_shift,
    inner_weight,
    inner_bias,
    outer_weight,
    outer_bias,
    second_gain,
    second_shift,
):
    count, seq, width = tokens.shape
    rows = count * seq
    short = (query_bias, value_bias, output_bias, first_gain, first_shift, outer_bias, second_gain, second_shift)
    outs = layer(
        tokens.reshape(rows, width),
        lengths,
        cotangent.reshape(rows, width),
        query_weight,
        key_weight,
        value_weight,
        output_weight,
        inner_weight,
        outer_weight,
        *[each.reshape(1, -1) for each in short + (inner_bias,)],
    )
    outs = hand_over(*outs)
    layer_rows, token_grad, query_g, key_g, value_g, output_g, inner_g, outer_g, *part = outs
    part = [each.reshape(-1) for each in part]
    return (
        layer_rows.reshape(count, seq, width),
        token_grad.reshape(count, seq, width),
        query_g,
        key_g,
        value_g,
        output_g,
        part[BQ],
        part[BV],
        part[BO],
        part[G1],
        part[S1],
        inner_g,
        part[SHORT],
        outer_g,
        part[BF],
        part[G2],
        part[S2],
    )


epsilon = 1e-12


def normalize(hidden, gain, shift):
    center = hidden - jnp.mean(hidden, axis=-1, keepdims=True)
    spread = jnp.mean(center * center, axis=-1, keepdims=True)
    return center * lax.rsqrt(spread + epsilon) * gain + shift


def gelu_exact(inner):
    return jax.nn.gelu(inner, approximate=False)


def matmul(left, right):
    return jnp.dot(left, right, preferred_element_type=jnp.float32)


def matmul_left_t(left, right):
    return lax.dot_general(
        left, right, (((0,), (0,)), ((), ())), preferred_element_type=jnp.float32
    )


def matmul_right_t(left, right):
    return lax.dot_general(
        left, right, (((1,), (1,)), ((), ())), preferred_element_type=jnp.float32
    )


def row_sum(values):
    return jnp.sum(values.astype(jnp.float32), axis=0)


def per_device(
    tokens,
    lengths,
    cotangent,
    query_weight,
    key_weight,
    value_weight,
    output_weight,
    query_bias,
    value_bias,
    output_bias,
    first_gain,
    first_shift,
    inner_weight,
    inner_bias,
    outer_weight,
    outer_bias,
    second_gain,
    second_shift,
):
    attn_master = (
        query_weight,
        key_weight,
        value_weight,
        output_weight,
        query_bias,
        value_bias,
        output_bias,
        first_gain,
        first_shift,
    )
    ffn_master = (inner_weight, inner_bias, outer_weight, outer_bias, second_gain, second_shift)
    attn_half = [param.astype(jnp.bfloat16) for param in attn_master]
    ffn_half = [param.astype(jnp.bfloat16) for param in ffn_master]
    micro_count, rows, width = tokens.shape
    heads = width // HD
    owners = lax.axis_size(("dp", "fsdp"))
    scale = 1.0 / math.sqrt(HD)
    positions = jnp.arange(rows, dtype=jnp.int32)
    attn_totals = [
        jnp.zeros((param.shape[0] * owners,) + param.shape[1:], jnp.float32)
        for param in attn_master
    ]
    ffn_totals = [
        jnp.zeros((param.shape[0] * owners,) + param.shape[1:], jnp.float32) for param in ffn_master
    ]
    outputs_list = []
    token_grads_list = []
    for micro in range(micro_count):
        token_rows = tokens[micro]
        cot_rows = cotangent[micro].astype(jnp.float32)
        valid_keys = positions < lengths[micro]
        attn_full = (
            lax.all_gather(attn_half[0], ("dp", "fsdp"), axis=0, tiled=True),
            lax.all_gather(attn_half[1], ("dp", "fsdp"), axis=0, tiled=True),
            lax.all_gather(attn_half[2], ("dp", "fsdp"), axis=0, tiled=True),
            lax.all_gather(attn_half[3], ("dp", "fsdp"), axis=0, tiled=True),
            lax.all_gather(attn_half[4], ("dp", "fsdp"), axis=0, tiled=True),
            lax.all_gather(attn_half[5], ("dp", "fsdp"), axis=0, tiled=True),
            lax.all_gather(attn_half[6], ("dp", "fsdp"), axis=0, tiled=True),
            lax.all_gather(attn_half[7], ("dp", "fsdp"), axis=0, tiled=True),
            lax.all_gather(attn_half[8], ("dp", "fsdp"), axis=0, tiled=True),
        )
        query_use, key_use, value_use, output_use = (
            attn_full[0],
            attn_full[1],
            attn_full[2],
            attn_full[3],
        )
        bias_query = attn_full[4].astype(jnp.float32)
        bias_value = attn_full[5].astype(jnp.float32)
        bias_output = attn_full[6].astype(jnp.float32)
        gain_first = attn_full[7].astype(jnp.float32)
        shift_first = attn_full[8].astype(jnp.float32)
        query_rows = (matmul(token_rows, query_use) + bias_query).astype(jnp.bfloat16)
        key_rows = matmul(token_rows, key_use).astype(jnp.bfloat16)
        value_rows = (matmul(token_rows, value_use) + bias_value).astype(jnp.bfloat16)
        query_heads = query_rows.reshape(rows, heads, HD)
        key_heads = key_rows.reshape(rows, heads, HD)
        value_heads = value_rows.reshape(rows, heads, HD)

        def attention_scores():
            raw_scores = (
                jnp.einsum(
                    "qhd,khd->hqk", query_heads, key_heads, preferred_element_type=jnp.float32
                )
                * scale
            )
            return jnp.where(valid_keys[None, None, :], raw_scores, -1000000000.0)

        scores = attention_scores()
        peak = jnp.max(scores, axis=-1, keepdims=True)
        log_total = peak + jnp.log(jnp.sum(jnp.exp(scores - peak), axis=-1, keepdims=True))
        probs_low = jnp.exp(scores - log_total).astype(jnp.bfloat16)
        mixed = (
            jnp.einsum("hqk,khd->qhd", probs_low, value_heads, preferred_element_type=jnp.float32)
            .reshape(rows, width)
            .astype(jnp.bfloat16)
        )
        residual = token_rows.astype(jnp.float32) + matmul(mixed, output_use) + bias_output
        first = normalize(residual, gain_first, shift_first)
        first_low = first.astype(jnp.bfloat16)
        ffn_full = (
            lax.all_gather(ffn_half[0], ("dp", "fsdp"), axis=0, tiled=True),
            lax.all_gather(ffn_half[1], ("dp", "fsdp"), axis=0, tiled=True),
            lax.all_gather(ffn_half[2], ("dp", "fsdp"), axis=0, tiled=True),
            lax.all_gather(ffn_half[3], ("dp", "fsdp"), axis=0, tiled=True),
            lax.all_gather(ffn_half[4], ("dp", "fsdp"), axis=0, tiled=True),
            lax.all_gather(ffn_half[5], ("dp", "fsdp"), axis=0, tiled=True),
        )
        inner = matmul(first_low, ffn_full[0]) + ffn_full[1].astype(jnp.float32)
        active = gelu_exact(inner).astype(jnp.bfloat16)
        second_in = first + matmul(active, ffn_full[2]) + ffn_full[3].astype(jnp.float32)
        gain_second = ffn_full[4].astype(jnp.float32)
        shift_second = ffn_full[5].astype(jnp.float32)
        layer_rows, pull_second = jax.vjp(normalize, second_in, gain_second, shift_second)
        outputs_list.append(layer_rows.astype(jnp.bfloat16))
        ffn_full = (
            lax.all_gather(ffn_half[0], ("dp", "fsdp"), axis=0, tiled=True),
            lax.all_gather(ffn_half[1], ("dp", "fsdp"), axis=0, tiled=True),
            lax.all_gather(ffn_half[2], ("dp", "fsdp"), axis=0, tiled=True),
            lax.all_gather(ffn_half[3], ("dp", "fsdp"), axis=0, tiled=True),
            lax.all_gather(ffn_half[4], ("dp", "fsdp"), axis=0, tiled=True),
            lax.all_gather(ffn_half[5], ("dp", "fsdp"), axis=0, tiled=True),
        )
        d_second, d_gain_second, d_shift_second = pull_second(cot_rows)
        d_outer = d_second.astype(jnp.bfloat16)
        ffn_totals[2] = ffn_totals[2] + matmul_left_t(active, d_outer)
        ffn_totals[3] = ffn_totals[3] + row_sum(d_outer)
        ffn_totals[4] = ffn_totals[4] + d_gain_second
        ffn_totals[5] = ffn_totals[5] + d_shift_second
        d_active = matmul_right_t(d_outer, ffn_full[2])
        gelu_value, pull_gelu = jax.vjp(gelu_exact, inner)
        (d_inner,) = pull_gelu(d_active)
        d_inner_low = d_inner.astype(jnp.bfloat16)
        ffn_totals[0] = ffn_totals[0] + matmul_left_t(first_low, d_inner_low)
        ffn_totals[1] = ffn_totals[1] + row_sum(d_inner_low)
        d_first = matmul_right_t(d_inner_low, ffn_full[0]) + d_second
        attn_full = (
            lax.all_gather(attn_half[0], ("dp", "fsdp"), axis=0, tiled=True),
            lax.all_gather(attn_half[1], ("dp", "fsdp"), axis=0, tiled=True),
            lax.all_gather(attn_half[2], ("dp", "fsdp"), axis=0, tiled=True),
            lax.all_gather(attn_half[3], ("dp", "fsdp"), axis=0, tiled=True),
            lax.all_gather(attn_half[4], ("dp", "fsdp"), axis=0, tiled=True),
            lax.all_gather(attn_half[5], ("dp", "fsdp"), axis=0, tiled=True),
            lax.all_gather(attn_half[6], ("dp", "fsdp"), axis=0, tiled=True),
            lax.all_gather(attn_half[7], ("dp", "fsdp"), axis=0, tiled=True),
            lax.all_gather(attn_half[8], ("dp", "fsdp"), axis=0, tiled=True),
        )
        query_use, key_use, value_use, output_use = (
            attn_full[0],
            attn_full[1],
            attn_full[2],
            attn_full[3],
        )
        norm_value, pull_first = jax.vjp(
            normalize, residual, attn_full[7].astype(jnp.float32), attn_full[8].astype(jnp.float32)
        )
        d_residual, d_gain_first, d_shift_first = pull_first(d_first)
        attn_totals[7] = attn_totals[7] + d_gain_first
        attn_totals[8] = attn_totals[8] + d_shift_first
        d_branch = d_residual.astype(jnp.bfloat16)
        attn_totals[3] = attn_totals[3] + matmul_left_t(mixed, d_branch)
        attn_totals[6] = attn_totals[6] + row_sum(d_branch)
        d_mixed = matmul_right_t(d_branch, output_use).astype(jnp.bfloat16).reshape(rows, heads, HD)
        scores = attention_scores()
        probs = jnp.exp(scores - log_total)
        probs_low = probs.astype(jnp.bfloat16)
        d_probs = jnp.einsum(
            "qhd,khd->hqk", d_mixed, value_heads, preferred_element_type=jnp.float32
        )
        d_values = jnp.einsum(
            "hqk,qhd->khd", probs_low, d_mixed, preferred_element_type=jnp.float32
        ).reshape(rows, width)
        delta_rows = jnp.sum(probs * d_probs, axis=-1, keepdims=True)
        d_scores = (probs * (d_probs - delta_rows)).astype(jnp.bfloat16)
        d_queries = (
            (
                jnp.einsum("hqk,khd->qhd", d_scores, key_heads, preferred_element_type=jnp.float32)
                * scale
            )
            .reshape(rows, width)
            .astype(jnp.bfloat16)
        )
        d_keys = (
            jnp.einsum(
                "hqk,qhd->khd", d_scores, query_heads, preferred_element_type=jnp.float32
            ).reshape(rows, width)
            * scale
        )
        key_low = d_keys.astype(jnp.bfloat16)
        value_low = d_values.astype(jnp.bfloat16)
        attn_totals[0] = attn_totals[0] + matmul_left_t(token_rows, d_queries)
        attn_totals[1] = attn_totals[1] + matmul_left_t(token_rows, key_low)
        attn_totals[2] = attn_totals[2] + matmul_left_t(token_rows, value_low)
        attn_totals[4] = attn_totals[4] + row_sum(d_queries)
        attn_totals[5] = attn_totals[5] + row_sum(value_low)
        token_grad = (
            d_residual
            + matmul_right_t(d_queries, query_use)
            + matmul_right_t(key_low, key_use)
            + matmul_right_t(value_low, value_use)
        )
        token_grads_list.append(token_grad.astype(jnp.bfloat16))
    attn_shards = (
        lax.psum_scatter(attn_totals[0], ("dp", "fsdp"), scatter_dimension=0, tiled=True),
        lax.psum_scatter(attn_totals[1], ("dp", "fsdp"), scatter_dimension=0, tiled=True),
        lax.psum_scatter(attn_totals[2], ("dp", "fsdp"), scatter_dimension=0, tiled=True),
        lax.psum_scatter(attn_totals[3], ("dp", "fsdp"), scatter_dimension=0, tiled=True),
        lax.psum_scatter(attn_totals[4], ("dp", "fsdp"), scatter_dimension=0, tiled=True),
        lax.psum_scatter(attn_totals[5], ("dp", "fsdp"), scatter_dimension=0, tiled=True),
        lax.psum_scatter(attn_totals[6], ("dp", "fsdp"), scatter_dimension=0, tiled=True),
        lax.psum_scatter(attn_totals[7], ("dp", "fsdp"), scatter_dimension=0, tiled=True),
        lax.psum_scatter(attn_totals[8], ("dp", "fsdp"), scatter_dimension=0, tiled=True),
    )
    ffn_shards = (
        lax.psum_scatter(ffn_totals[0], ("dp", "fsdp"), scatter_dimension=0, tiled=True),
        lax.psum_scatter(ffn_totals[1], ("dp", "fsdp"), scatter_dimension=0, tiled=True),
        lax.psum_scatter(ffn_totals[2], ("dp", "fsdp"), scatter_dimension=0, tiled=True),
        lax.psum_scatter(ffn_totals[3], ("dp", "fsdp"), scatter_dimension=0, tiled=True),
        lax.psum_scatter(ffn_totals[4], ("dp", "fsdp"), scatter_dimension=0, tiled=True),
        lax.psum_scatter(ffn_totals[5], ("dp", "fsdp"), scatter_dimension=0, tiled=True),
    )
    return (
        jnp.stack(outputs_list),
        jnp.stack(token_grads_list),
        attn_shards[0],
        attn_shards[1],
        attn_shards[2],
        attn_shards[3],
        attn_shards[4],
        attn_shards[5],
        attn_shards[6],
        attn_shards[7],
        attn_shards[8],
        ffn_shards[0],
        ffn_shards[1],
        ffn_shards[2],
        ffn_shards[3],
        ffn_shards[4],
        ffn_shards[5],
    )


def solution(mesh):
    in_specs = (
        P(("dp", "fsdp"), None, None),
        P(("dp", "fsdp")),
        P(("dp", "fsdp"), None, None),
        P(("dp", "fsdp"), None),
        P(("dp", "fsdp"), None),
        P(("dp", "fsdp"), None),
        P(("dp", "fsdp"), None),
        P(("dp", "fsdp")),
        P(("dp", "fsdp")),
        P(("dp", "fsdp")),
        P(("dp", "fsdp")),
        P(("dp", "fsdp")),
        P(("dp", "fsdp"), None),
        P(("dp", "fsdp")),
        P(("dp", "fsdp"), None),
        P(("dp", "fsdp")),
        P(("dp", "fsdp")),
        P(("dp", "fsdp")),
    )
    out_specs = (
        P(("dp", "fsdp"), None, None),
        P(("dp", "fsdp"), None, None),
        P(("dp", "fsdp"), None),
        P(("dp", "fsdp"), None),
        P(("dp", "fsdp"), None),
        P(("dp", "fsdp"), None),
        P(("dp", "fsdp")),
        P(("dp", "fsdp")),
        P(("dp", "fsdp")),
        P(("dp", "fsdp")),
        P(("dp", "fsdp")),
        P(("dp", "fsdp"), None),
        P(("dp", "fsdp")),
        P(("dp", "fsdp"), None),
        P(("dp", "fsdp")),
        P(("dp", "fsdp")),
        P(("dp", "fsdp")),
    )
    one_kernel = dict(mesh.shape) == {"dp": 16, "fsdp": 2}
    device = one_kernel_device if one_kernel else per_device
    return jax.shard_map(
        device, mesh=mesh, in_specs=in_specs, out_specs=out_specs, check_vma=False
    )
```

```python
import functools
import math

import jax
import jax.numpy as jnp
from jax import lax
from jax.experimental import pallas as pl
from jax.experimental.pallas import tpu as pltpu
from jax.sharding import PartitionSpec as P

MESH = pl.DeviceIdType.MESH
COPIES = 15
HD = 64
LOW = jnp.bfloat16
F32 = jnp.float32


class Place:
    def __init__(self):
        self.me = lax.axis_index("dp")
        self.core = lax.axis_index("fsdp")
        x, y, self.z = lax.rem(self.me, 2), lax.rem(self.me // 2, 2), self.me // 4
        self.a = x + self.core * (y - x)
        self.b = y + self.core * (x - y)
        odd = lax.rem(self.z, 2)
        self.pair, self.other = 3 - 2 * odd, 1 + 2 * odd
        self.z_pair = self.z + 1 - 2 * odd

    def chip(self, z, a, b):
        return z * 4 + (b + self.core * (a - b)) * 2 + (a + self.core * (b - a))

    def back(self, j):
        return lax.rem(self.z - j + 4, 4)

    def peers(self):
        along_z = [self.chip(lax.rem(self.z + k, 4), self.a, self.b) for k in (1, 2, 3)]
        return along_z + [self.chip(self.z, 1 - self.a, self.b), self.chip(self.z, self.a, 1 - self.b)]

    def signal_peers(self, sem):
        for chip in self.peers():
            pl.semaphore_signal(sem, inc=1, device_id=(chip, self.core), device_id_type=MESH)

    def announce(self):
        sem = pltpu.get_barrier_semaphore()
        self.signal_peers(sem)
        pl.semaphore_signal(sem, inc=1, device_id=(self.me, 1 - self.core), device_id_type=MESH)

    def meet(self):
        pl.semaphore_wait(pltpu.get_barrier_semaphore(), 6)


class Hops:
    def __init__(self, place, send_sem, recv_sem, base):
        self.place, self.send_sem, self.recv_sem, self.base = place, send_sem, recv_sem, base
        self.started = []

    def send(self, k, source, target, chip):
        copy = pltpu.make_async_remote_copy(
            src_ref=source,
            dst_ref=target,
            send_sem=self.send_sem.at[self.base + k],
            recv_sem=self.recv_sem.at[self.base + k],
            device_id=(chip, self.place.core),
            device_id_type=MESH,
        )
        copy.start()
        self.started.append(copy)

    def arrived(self, k, block):
        pltpu.make_async_remote_copy(
            src_ref=block,
            dst_ref=block,
            send_sem=self.send_sem.at[self.base + k],
            recv_sem=self.recv_sem.at[self.base + k],
            device_id=(self.place.me, self.place.core),
            device_id_type=MESH,
        ).wait_recv()

    def finish(self):
        for copy in self.started:
            copy.wait_send()
        self.started = []


class Gather(Hops):
    def __init__(self, place, held, *rest):
        super().__init__(place, *rest)
        self.held = held

    def pass_on(self, k, block, chip):
        self.send(k, self.held.at[block], self.held.at[block], chip)

    def wait(self, *copies):
        for k in copies:
            self.arrived(k, self.held.at[self.place.me])

    def run(self, *hops):
        for hop in hops:
            self.take(hop)

    def take(self, name):
        p = self.place
        kind, which = name
        which = {PAIR: p.pair, OTHER: p.other}.get(which, which)
        if kind == Z:
            self.pass_on(which - 1, p.me, p.chip(lax.rem(p.z + which, 4), p.a, p.b))
        elif kind == A:
            if name != A0:
                self.wait(which - 1)
            self.pass_on(3 + which, p.chip(p.back(which), p.a, p.b), p.chip(p.z, 1 - p.a, p.b))
        elif kind == B:
            j = (0, 0, 2, 2, p.other, p.other)[which]
            if which % 2:
                self.wait(3 + j)
            block = p.chip(p.back(j), (p.a, 1 - p.a)[which % 2], p.b)
            self.pass_on(7 + which, block, p.chip(p.z, p.a, 1 - p.b))
        elif kind == P_:
            self.wait(7 + which)
            block = p.chip(p.z, (p.a, 1 - p.a)[which], 1 - p.b)
            self.pass_on(13 + which, block, p.chip(p.z_pair, p.a, p.b))
        else:
            self.wait(*((), (3 + p.pair,), (9, 10), (11, 12, 13, 14))[which])


class Reduce(Hops):
    def __init__(self, place, terms, landed, chunk, *rest):
        super().__init__(place, *rest)
        self.terms, self.landed, self.chunk = terms, landed, chunk

    def sum_into(self, block, ks, store):
        for k in ks:
            self.arrived(k, self.landed(k))
        term = self.terms(block)
        landed = [self.landed(k) for k in ks]
        rows = term.shape[0]

        def some(n):
            at = rows_at(n, self.chunk)
            total = term[at].astype(F32)
            for each in landed:
                total += each[at].astype(F32)
            store(n, total)

        if rows == self.chunk:
            some(0)
        else:
            pl.loop(0, rows // self.chunk)(some)

    def add_and_send(self, k, block, ks, chip):
        term = self.terms(block)
        if ks:

            def store(n, total):
                term[rows_at(n, self.chunk)] = total.astype(term.dtype)

            self.sum_into(block, ks, store)
        self.send(k, term, self.landed(k), chip)

    def run(self, *hops):
        for hop in hops:
            self.take(hop)

    def take(self, name):
        p = self.place
        kind, which = name
        which = {PAIR: p.pair, OTHER: p.other}.get(which, which)
        if kind == P_:
            block = p.chip(p.z_pair, (p.a, 1 - p.a)[which], 1 - p.b)
            self.add_and_send(13 + which, block, (), p.chip(p.z_pair, p.a, p.b))
        elif kind == B:
            j = (0, 0, 2, 2, p.other, p.other)[which]
            block = p.chip(p.back(j), (p.a, 1 - p.a)[which % 2], 1 - p.b)
            landed = (13 + which,) if which < 2 else ()
            self.add_and_send(7 + which, block, landed, p.chip(p.z, p.a, 1 - p.b))
        elif kind == A:
            landed = {A0: (8,), A2: (10,), Ao: (12,), Ap: ()}[name]
            block = p.chip(p.back(which), 1 - p.a, p.b)
            self.add_and_send(3 + which, block, landed, p.chip(p.z, 1 - p.a, p.b))
        else:
            landed = {Z2: (9, 5), Zo: (11, 3 + p.other), Zp: (3 + p.pair,)}[name]
            owner = p.chip(p.back(which), p.a, p.b)
            self.add_and_send(3 - which, owner, landed, owner)

    def result(self, store):
        self.sum_into(self.place.me, (7, 3, 0, 1, 2), store)


class Across:
    def __init__(self, place, send_sem, recv_sem):
        self.place, self.send_sem, self.recv_sem = place, send_sem, recv_sem
        self.count = 0

    def copy(self, k, source, target):
        p = self.place
        return pltpu.make_async_remote_copy(
            src_ref=source,
            dst_ref=target,
            send_sem=self.send_sem.at[k],
            recv_sem=self.recv_sem.at[k],
            device_id=(p.me, 1 - p.core),
            device_id_type=MESH,
        )

    def send(self, source, target, here=None):
        k = self.count
        self.count += 1
        copy = self.copy(k, source, target)
        copy.start()
        landing = target if here is None else here
        return copy.wait_send, self.copy(k, landing, landing).wait_recv


def dot(left, right):
    return jnp.dot(left, right, preferred_element_type=F32)


def dot_left_t(left, right):
    return lax.dot_general(left, right, (((0,), (0,)), ((), ())), preferred_element_type=F32)


def dot_right_t(left, right):
    return lax.dot_general(left, right, (((1,), (1,)), ((), ())), preferred_element_type=F32)


def fold(values):
    rows, columns = values.shape
    return jnp.sum(values.reshape(rows // 8, 8, columns), axis=0)


def rows_at(index, size):
    if isinstance(index, int):
        return pl.ds(index * size, size)
    return pl.ds(pl.multiple_of(index * size, size), size)


Z, A, B, P_, E = range(5)
PAIR, OTHER = -1, -2
Z1, Z2, Z3, Zp, Zo = (Z, 1), (Z, 2), (Z, 3), (Z, PAIR), (Z, OTHER)
A0, A2, Ap, Ao = (A, 0), (A, 2), (A, PAIR), (A, OTHER)
B0, B1, B2, B3, B4, B5 = [(B, n) for n in range(6)]
P0, P1 = (P_, 0), (P_, 1)
E1, E2, E3 = (E, 1), (E, 2), (E, 3)
EARLY = (Z2, A0, B0, Z1, Z3)

SHORT = 8
BQ, BV, BO, G1, S1, BF, G2, S2 = range(SHORT)
EPSILON = 1e-12


def layer_kernel(
    tokens,
    lengths,
    cotangent,
    query_weight,
    key_weight,
    value_weight,
    output_weight,
    inner_weight,
    outer_weight,
    *rest,
):
    short_shards, rest = rest[: SHORT + 1], rest[SHORT + 1 :]
    layer_body(
        tokens,
        lengths,
        cotangent,
        query_weight,
        key_weight,
        value_weight,
        output_weight,
        inner_weight,
        outer_weight,
        short_shards,
        rest[-SHORT - 1 :],
        *rest[: -SHORT - 1],
    )


def layer_body(
    tokens,
    lengths,
    cotangent,
    query_weight,
    key_weight,
    value_weight,
    output_weight,
    inner_weight,
    outer_weight,
    short_shards,
    short_here,
    layer_out,
    token_grad,
    query_grad,
    key_grad,
    value_grad,
    output_grad,
    inner_grad,
    outer_grad,
    vec_grad,
    x_all,
    qkv,
    mix,
    acc,
    out_part,
    in_part,
    xhat,
    scale1,
    first,
    act,
    slope,
    dout,
    gbuf,
    w_qkv,
    w_o,
    w_i,
    w_2,
    t_2,
    t_i,
    t_o,
    landed_2,
    landed_i,
    landed_o,
    stage_q,
    stage_i,
    f_s,
    f_i,
    f_2,
    mask,
    vec_all,
    params,
    inner_bias,
    g_part,
    i_part,
    g_sum,
    g_other,
    v_terms,
    v_landed,
    v_stage,
    local_sem,
    core_send,
    core_recv,
    send_sem,
    recv_sem,
    ready_sem,
):
    p = Place()
    me, core = p.me, p.core
    peer = 1 - core
    across = Across(p, core_send, core_recv)
    pending = []

    own_rows = rows_at(core, 512)
    peer_rows = rows_at(peer, 512)

    def local(k, source, target):
        return pltpu.make_async_copy(source, target, local_sem.at[k])

    loads = [
        local(0, query_weight, f_s.at[0]),
        local(1, key_weight, f_s.at[1]),
        local(2, value_weight, f_s.at[2]),
        local(3, output_weight, f_s.at[3]),
        local(4, inner_weight, f_i),
        local(5, outer_weight, f_2),
        local(6, tokens, x_all.at[own_rows]),
        local(7, cotangent, gbuf),
    ]
    loads += [local(10 + n, short_shards[n], short_here[n]) for n in range(SHORT + 1)]
    for copy in loads:
        copy.start()

    places = lax.broadcasted_iota(jnp.int32, (8, 256), 1)
    seq_of = lax.broadcasted_iota(jnp.int32, (8, 256), 0)
    limit = jnp.where(seq_of == 0, lengths[0], lengths[1])
    mask[core] = jnp.where(places < limit, 1.0, 0.0).astype(F32)
    p.announce()
    v_stage[...] = jnp.zeros_like(v_stage)
    for copy in loads[8:]:
        copy.wait()
    for n in range(SHORT):
        v_stage[n : n + 1, 0:32] = short_here[n][...]
    v_stage[SHORT : SHORT + 1, :] = short_here[SHORT][...]
    piece = v_stage[...]
    four = piece + pltpu.roll(piece, 32, 1) + pltpu.roll(piece, 64, 1) + pltpu.roll(piece, 96, 1)
    is_short = lax.broadcasted_iota(jnp.int32, (16, 128), 0) < SHORT
    vec_all[core, me] = jnp.where(is_short, four, piece).astype(LOW)
    g_part[...] = jnp.zeros_like(g_part)
    i_part[...] = jnp.zeros_like(i_part)

    for copy in loads[:4]:
        copy.wait()
    my_rows = rows_at(core, 32)
    for n in range(3):
        w_qkv[me, my_rows, 512 * n : 512 * n + 512] = f_s[n, :, rows_at(core, 512)].astype(LOW)
        stage_q[:, 512 * n : 512 * n + 512] = f_s[n, :, rows_at(peer, 512)].astype(LOW)
    w_o[me, core] = f_s[3].astype(LOW)
    loads[5].wait()
    w_2[me] = f_2[...].astype(LOW)
    p.meet()
    sent_q, got_q = across.send(stage_q, w_qkv.at[me, my_rows], w_qkv.at[me, rows_at(peer, 32)])
    sent_m, got_m = across.send(mask.at[core], mask.at[core], mask.at[peer])
    gather_o = Gather(p, w_o.at[:, core], send_sem, recv_sem, COPIES)
    gather_v = Gather(p, vec_all.at[core], send_sem, recv_sem, 4 * COPIES)
    gather_q = Gather(p, w_qkv, send_sem, recv_sem, 0)
    gather_i = Gather(p, w_i, send_sem, recv_sem, 2 * COPIES)
    gather_2 = Gather(p, w_2, send_sem, recv_sem, 3 * COPIES)
    gather_o.run(*EARLY)
    gather_v.run(*EARLY)
    gather_2.run(A0, B0)
    loads[4].wait()
    for n in range(16):
        here, there = 2 * n + core, 2 * n + peer
        at = slice(128 * n, 128 * n + 128)
        w_i[me, my_rows, at] = f_i[:, rows_at(here, 128)].astype(LOW)
        stage_i[:, at] = f_i[:, rows_at(there, 128)].astype(LOW)
    sent_i, got_i = across.send(stage_i, w_i.at[me, my_rows], w_i.at[me, rows_at(peer, 32)])
    got_q()
    gather_q.run(*EARLY)
    loads[6].wait()
    sent_x, got_x = across.send(x_all.at[own_rows], x_all.at[own_rows], x_all.at[peer_rows])
    got_i()
    pending += [sent_q, sent_m, sent_i, sent_x]
    sent, got = {}, {}

    def exchange(name, source, target, here=None):
        sent[name], got[name] = across.send(source, target, here)

    def done(*names):
        for name in names:
            sent.pop(name)()

    def relay_output():
        mine = rows_at(core, 8)
        theirs = rows_at(peer, 8)
        exchange("o", w_o.at[theirs, core], w_o.at[theirs, core], w_o.at[mine, peer])
        exchange("v", vec_all.at[core], vec_all.at[core], vec_all.at[peer])

    def short_params():
        got["v"]()
        lane_group = lax.broadcasted_iota(jnp.int32, (16, 128), 1) // 32
        for t in range(8):
            pieces = [vec_all[i % 2, 2 * t + i // 2].astype(F32) for i in range(4)]
            tile = jnp.where(
                lane_group < 2,
                jnp.where(lane_group == 0, pieces[0], pieces[1]),
                jnp.where(lane_group == 2, pieces[2], pieces[3]),
            )
            params[:, 128 * t : 128 * t + 128] = tile
        for n in range(16):
            inner_bias[:, 128 * n : 128 * n + 128] = vec_all[core, n].astype(F32)[8:16]
        got_x()
        got_m()

    def param(n):
        return params[n : n + 1, :]

    def project(turn):
        owner = (core, peer)[turn]

        @pl.loop(0, 2)
        def _(half):
            rows = rows_at(2 * owner + half, 256)
            block = x_all[rows, :]
            for n in range(3):
                part = dot(block, w_qkv[:, :, 512 * n : 512 * n + 512].reshape(1024, 512))
                if n != 1:
                    part = part + params[BQ if n == 0 else BV, rows_at(core, 512)][None, :]
                qkv[rows, 512 * n : 512 * n + 512] = part.astype(LOW)

    left_half = lax.broadcasted_iota(jnp.int32, (256, 128), 1) < HD

    def heads_of(s, t):
        rows = rows_at(s, 256)
        return [qkv[rows, pl.ds(pl.multiple_of(512 * n + 128 * t, 128), 128)] for n in range(3)]

    def softmax(query_half, key, valid):
        raw = dot_right_t(query_half, key)
        raw = jnp.where(valid, raw, -1000000000.0)
        grown = jnp.exp(raw - jnp.max(raw, axis=-1, keepdims=True))
        return grown * (1.0 / jnp.sum(grown, axis=-1, keepdims=True))

    def halves(pair):
        none = jnp.zeros_like(pair)
        return jnp.where(left_half, pair, none), jnp.where(left_half, none, pair)

    scale = jnp.array(1.0 / math.sqrt(HD), LOW)

    def turn_of(turn):
        return (peer, peer, core, core)[turn], turn % 2

    def attention(turn, part):
        owner, n = turn_of(turn)
        s = 2 * owner + n
        valid = mask[owner, n : n + 1, :] > 0.5

        @pl.loop(2 * part, 2 * part + 2)
        def _(t):
            query, key, value = heads_of(s, t)
            outs = [
                dot(softmax(half, key, valid).astype(LOW), value) for half in halves(query * scale)
            ]
            both = jnp.where(left_half, outs[0], outs[1]).astype(LOW)
            mix[rows_at(s, 256), rows_at(t, 128)] = both

    def part_name(half):
        return "part0" if half == 0 else "part1"

    def pass_part(half):
        at = slice(256 * half, 256 * half + 256)
        exchange(part_name(half), out_part.at[at], in_part.at[at])

    def branch(turn):
        owner, n = turn_of(turn)
        if turn == 0:
            got["o"]()
        out_use = w_o[rows_at(core, 8)].reshape(512, 1024)
        part = dot(mix[rows_at(2 * owner + n, 256), :], out_use)
        at = slice(256 * n, 256 * n + 256)
        if turn < 2:
            out_part[at] = part
            pass_part(n)
        else:
            acc[at] = part

    def norm_of(hidden):
        center = hidden - jnp.mean(hidden, axis=-1, keepdims=True)
        spread = jnp.mean(center * center, axis=-1, keepdims=True)
        inverse = lax.rsqrt(spread + EPSILON)
        return center * inverse, inverse

    def norm_back(grown, normal, inverse):
        along = jnp.mean(grown * normal, axis=-1, keepdims=True)
        return inverse * (grown - jnp.mean(grown, axis=-1, keepdims=True) - normal * along)

    BLOCK = 128

    def tokens_of(owner, n):
        return pl.ds(pl.multiple_of(512 * owner + BLOCK * n, BLOCK), BLOCK)

    def half_of(owner, half):
        return pl.ds(pl.multiple_of(512 * owner + 256 * half, 256), 256)

    def share(name, whole, half):
        exchange(name + str(half), whole.at[half_of(core, half)], whole.at[half_of(core, half)], whole.at[half_of(peer, half)])

    def norm_first(half):
        got[part_name(half)]()

        @pl.loop(2 * half, 2 * half + 2)
        def _(n):
            at = rows_at(n, BLOCK)
            hidden = x_all[tokens_of(core, n), :].astype(F32) + acc[at] + in_part[at] + param(BO)
            normal, inverse = norm_of(hidden)
            xhat[rows_at(n, 4)] = normal.reshape(4, 32, 1024)
            scale1[at] = jnp.broadcast_to(inverse, (BLOCK, 128))
            first[pl.ds(8 * core + 2 * n, 2)] = (normal * param(G1) + param(S1)).astype(LOW).reshape(2, 2, 32, 1024)

        mine = pl.ds(8 * core + 4 * half, 4)
        theirs = pl.ds(8 * peer + 4 * half, 4)
        exchange("first" + str(half), first.at[mine], first.at[mine], first.at[theirs])
        if half == 1:
            done("part0", "part1")

    def inner(turn):
        owner, half = ((core, 0), (core, 1), (peer, 0), (peer, 1))[turn]
        if turn > 1:
            got["first" + str(half)]()
        rows64 = 8 * owner + 4 * half
        act_rows = half_of(owner, half)
        block = first[pl.ds(rows64, 4)].reshape(256, 1024)

        @pl.loop(0, 4)
        def _(n):
            columns = rows_at(n, 512)
            before = dot(block, w_i[:, :, columns].reshape(1024, 512)) + inner_bias[0:1, columns]
            error = lax.erf(before * (1.0 / math.sqrt(2.0)))
            chance = 0.5 * (1.0 + error)
            bell = jnp.exp(-0.5 * before * before) * (1.0 / math.sqrt(2.0 * math.pi))
            act[act_rows, columns] = (before * chance).astype(LOW)
            slope[pl.ds(rows64, 4), :, columns] = (chance + before * bell).astype(LOW).reshape(4, 64, 512)

    far = 1 - p.b

    def chips_of(group):
        if group < 2:
            a = (p.a, 1 - p.a)[group]
            return [p.chip(z, a, p.b) for z in range(4)]
        return [p.chip(p.back(j), a, far) for j in ((0, 2), (p.other, p.pair))[group - 2] for a in (p.a, 1 - p.a)]

    def outer_half(group, turn):
        owner, half = ((peer, 0), (peer, 1), (core, 0), (core, 1))[turn]
        target = out_part if turn < 2 else acc
        chips = chips_of(group)
        left = jnp.concatenate([act[half_of(owner, half), rows_at(chip, 128)] for chip in chips], axis=1)
        at = slice(256 * half, 256 * half + 256)
        for n in range(2):
            columns = slice(512 * n, 512 * n + 512)
            right = jnp.concatenate([w_2[chip, :, columns] for chip in chips], axis=0)
            part = dot(left, right)
            target[at, columns] = part if group == 0 else target[at, columns] + part
        if group == 3 and turn < 2:
            pass_part(half)

    def outer(group):
        for turn in range(4):
            outer_half(group, turn)

    def norm_second(half):
        got[part_name(half)]()
        if half == 0:
            loads[7].wait()

        @pl.loop(2 * half, 2 * half + 2)
        def _(n):
            at = rows_at(n, BLOCK)
            hidden = xhat[rows_at(n, 4)].reshape(BLOCK, 1024) * param(G1) + param(S1)
            hidden = hidden + acc[at] + in_part[at] + param(BF)
            normal, inverse = norm_of(hidden)
            given = gbuf[at].astype(F32)
            gbuf[at] = (normal * param(G2) + param(S2)).astype(LOW)
            g_part[G2] += fold(given * normal)
            g_part[S2] += fold(given)
            down = norm_back(given * param(G2), normal, inverse)
            acc[at] = down
            low = down.astype(LOW)
            g_part[BF] += fold(low.astype(F32))
            dout[tokens_of(core, n), :] = low

        share("dout", dout, half)
        if half == 1:
            store_out.start()

    store_out = local(8, gbuf, layer_out)
    planes = (p.z_pair, p.back(2), p.back(p.other), p.z)

    def outer_terms(step):
        if step == 0:
            got["dout0"]()
            got["dout1"]()
        z = planes[step]
        for half in range(2):
            left = act[:, pl.ds(pl.multiple_of(512 * z + 256 * half, 256), 256)]
            part = dot_left_t(left, dout[...])
            t_2[pl.ds(4 * z + 2 * half, 2)] = part.astype(LOW).reshape(2, 128, 1024)

    def d_inner(n):
        columns = rows_at(n, 512)

        @pl.loop(0, 4)
        def _(s):
            rows = rows_at(s, 256)
            back = dot_right_t(dout[rows, :], w_2[pl.ds(4 * n, 4)].reshape(512, 1024))
            bent = slope[pl.ds(4 * s, 4), :, columns].reshape(256, 512).astype(F32)
            low = (back * bent).astype(LOW)
            act[rows, columns] = low
            i_part[:, columns] += fold(low.astype(F32))

    def inner_terms(step):
        z = planes[step]
        for n in range(4):
            columns = slice(512 * n, 512 * n + 512)
            left = first[:, :, :, pl.ds(pl.multiple_of(256 * z, 256), 256)].reshape(1024, 256)
            part = dot_left_t(left, act[:, columns])
            t_i[pl.ds(4 * z, 4), :, columns] = part.astype(LOW).reshape(4, 64, 512)

    def d_first(turn):
        owner, half = ((peer, 0), (peer, 1), (core, 0), (core, 1))[turn]
        if turn == 0:
            done("part0", "part1")
        at = slice(256 * half, 256 * half + 256)
        for n in range(4):
            part = dot_right_t(act[half_of(owner, half), :], w_i[4 * n : 4 * n + 4].reshape(256, 2048))
            columns = slice(256 * n, 256 * n + 256)
            if turn < 2:
                out_part[at, columns] = part
            else:
                acc[at, columns] += part
        if turn < 2:
            pass_part(half)
        if turn == 3:
            gather_i.finish()
            p.signal_peers(ready_sem)

    def norm_first_back(half):
        if half == 0:
            done("dout0", "dout1")
        got[part_name(half)]()

        @pl.loop(2 * half, 2 * half + 2)
        def _(n):
            at = rows_at(n, BLOCK)
            normal = xhat[rows_at(n, 4)].reshape(BLOCK, 1024)
            given = acc[at] + in_part[at]
            g_part[G1] += fold(given * normal)
            g_part[S1] += fold(given)
            down = norm_back(given * param(G1), normal, scale1[at, 0:1])
            acc[at] = down
            low = down.astype(LOW)
            g_part[BO] += fold(low.astype(F32))
            dout[tokens_of(core, n), :] = low

        share("dout", dout, half)

    def output_terms():
        got["dout0"]()
        got["dout1"]()
        done("first0", "first1")
        for half in range(2):
            part = dot_left_t(mix[:, 256 * half : 256 * half + 256], dout[...])
            first[4 * half : 4 * half + 4] = part.astype(LOW).reshape(4, 2, 32, 1024)
        t_o[pl.ds(8 * core, 8)] = first[0:8, core]
        exchange("t", first.at[pl.ds(0, 8), peer], t_o.at[pl.ds(8 * core, 8)], t_o.at[pl.ds(8 * peer, 8)])

    def d_mixed():
        @pl.loop(0, 4)
        def _(s):
            rows = rows_at(s, 256)
            mix[rows, :] = dot_right_t(dout[rows, :], w_o[rows_at(core, 8)].reshape(512, 1024)).astype(LOW)

        got["t"]()

    def attention_back(turn, part):
        owner, n = turn_of(turn)
        s = 2 * owner + n
        valid = mask[owner, n : n + 1, :] > 0.5
        rows = rows_at(s, 256)

        @pl.loop(2 * part, 2 * part + 2)
        def _(t):
            query, key, value = heads_of(s, t)
            columns = rows_at(t, 128)
            d_mix = mix[rows, columns]
            scaled = query * scale
            d_query, d_key, d_value = [], [], []
            for q_half, m_half in zip(halves(scaled), halves(d_mix)):
                probs = softmax(q_half, key, valid)
                d_probs = dot_right_t(m_half, value)
                d_value.append(dot_left_t(probs.astype(LOW), d_mix))
                delta = jnp.sum(probs * d_probs, axis=-1, keepdims=True)
                d_scores = (probs * (d_probs - delta)).astype(LOW)
                d_query.append(dot(d_scores, key))
                d_key.append(dot_left_t(d_scores, scaled))
            low_q = (jnp.where(left_half, *d_query) * (1.0 / math.sqrt(HD))).astype(LOW)
            low_k = jnp.where(left_half, *d_key).astype(LOW)
            low_v = jnp.where(left_half, *d_value).astype(LOW)
            for n_part, low in enumerate((low_q, low_k, low_v)):
                qkv[rows, pl.ds(pl.multiple_of(512 * n_part + 128 * t, 128), 128)] = low
            here = pl.ds(pl.multiple_of(512 * core + 128 * t, 128), 128)
            g_part[BQ, :, here] += fold(low_q.astype(F32))
            g_part[BV, :, here] += fold(low_v.astype(F32))

    def query_terms(step):
        if step == 0:
            pl.semaphore_wait(ready_sem, 5)
        z = planes[step]
        for n in range(3):
            columns = slice(512 * n, 512 * n + 512)
            left = x_all[:, pl.ds(pl.multiple_of(256 * z, 256), 256)]
            part = dot_left_t(left, qkv[:, columns])
            slope[pl.ds(4 * z, 4), :, columns] = part.astype(LOW).reshape(4, 64, 512)

    def short_sums():
        for n in range(SHORT):
            g_sum[n : n + 1, :] = jnp.sum(g_part[n], axis=0, keepdims=True)
        exchange("g", g_sum, g_other)

    def short_terms():
        got["g"]()
        v_terms[...] = jnp.zeros_like(v_terms)
        for n in range(16):
            t = n // 2
            at = slice(128 * t, 128 * t + 128)
            v_terms[n, 0:8] = g_sum[:, at] + g_other[:, at]
            v_terms[n, 8:9] = jnp.sum(i_part[:, 128 * n : 128 * n + 128], axis=0, keepdims=True)

    def d_tokens(turn):
        owner, half = ((peer, 0), (peer, 1), (core, 0), (core, 1))[turn]
        if turn == 0:
            done("part0", "part1")
        at = slice(256 * half, 256 * half + 256)
        for n in range(4):
            part = dot_right_t(qkv[half_of(owner, half), :], w_qkv[4 * n : 4 * n + 4].reshape(256, 1536))
            columns = slice(256 * n, 256 * n + 256)
            if turn < 2:
                out_part[at, columns] = part
            else:
                acc[at, columns] += part
        if turn < 2:
            pass_part(half)

    store_tokens = local(9, gbuf, token_grad)

    def tokens_out():
        store_out.wait()
        for half in range(2):
            got[part_name(half)]()

            @pl.loop(2 * half, 2 * half + 2)
            def _(n):
                at = rows_at(n, BLOCK)
                gbuf[at] = (acc[at] + in_part[at]).astype(LOW)

        store_tokens.start()

    reduce_2 = Reduce(p, lambda i: t_2.at[i], lambda k: landed_2.at[k], 32, send_sem, recv_sem, 5 * COPIES)
    reduce_i = Reduce(p, lambda i: t_i.at[i], lambda k: landed_i.at[k], 32, send_sem, recv_sem, 6 * COPIES)
    reduce_o = Reduce(p, lambda i: t_o.at[i], lambda k: landed_o.at[k], 32, send_sem, recv_sem, 7 * COPIES)
    reduce_q = Reduce(
        p,
        lambda i: slope.at[i, :, pl.ds(0, 1536)],
        lambda k: w_i.at[k, :, pl.ds(0, 1536)],
        32,
        send_sem,
        recv_sem,
        8 * COPIES,
    )
    reduce_v = Reduce(p, lambda i: v_terms.at[i], lambda k: v_landed.at[k], 16, send_sem, recv_sem, 9 * COPIES)

    stores = []

    def store(k, source, target):
        stores.append(local(k, source, target))
        stores[-1].start()

    def result_2():
        def put(n, total):
            f_2[rows_at(n, 32)] = total

        reduce_2.result(put)
        store(5, f_2, outer_grad)

    def halves_to(first_block):
        def put(n, total):
            xhat[first_block + 2 * n] = total[:, :1024]
            xhat[first_block + 2 * n + 1, :, : total.shape[1] - 1024] = total[:, 1024:]

        return put

    def column(block, n):
        return xhat[block + n // 8, :, 128 * (n % 8) : 128 * (n % 8) + 128]

    def result_i():
        reduce_i.result(halves_to(0))
        exchange("i", xhat.at[pl.ds(2 * peer, 2)], xhat.at[4:6])

    def result_i_out():
        got["i"]()
        for n in range(16):
            f_i[:, rows_at(2 * n + core, 128)] = column(2 * core, n)
            f_i[:, rows_at(2 * n + peer, 128)] = column(4, n)
        store(4, f_i, inner_grad)

    def result_o():
        def put(n, total):
            f_s[3] = total

        reduce_o.result(put)
        store(3, f_s.at[3], output_grad)

    def result_v():
        def put(n, total):
            group = 2 * lax.rem(me, 2) + core
            turned = total
            for n_group in (1, 2, 3):
                turned = jnp.where(group == n_group, pltpu.roll(total, 128 - 32 * n_group, 1), turned)
            is_short = lax.broadcasted_iota(jnp.int32, (16, 128), 0) < SHORT
            vec_grad[...] = jnp.where(is_short, turned, total)

        reduce_v.result(put)

    def result_q():
        reduce_q.result(halves_to(8))
        exchange("q", xhat.at[pl.ds(8 + 2 * peer, 2)], xhat.at[12:14])

    def result_q_out():
        got["q"]()
        for n, target in enumerate((query_grad, key_grad, value_grad)):
            for owner, block in ((core, 8 + 2 * core), (peer, 12)):
                f_s[n, :, rows_at(owner, 512)] = xhat[block + n // 2, :, 512 * (n % 2) : 512 * (n % 2) + 512]
            store(n, f_s.at[n], target)

    gather_o.run(A2)
    gather_v.run(Ap)
    gather_i.run(Z3)
    gather_v.run(B1)
    gather_i.run(B0)
    gather_o.run(Ap)
    gather_v.run(P0)
    gather_o.run(B2, B1, B3)
    gather_v.run(A2)
    gather_q.run(P0)
    gather_v.run(E1)
    gather_o.run(Ao)
    gather_v.run(Ao)
    gather_q.run(B1)
    gather_o.run(B4)
    gather_i.run(A0)
    gather_o.run(P1)
    gather_v.run(B4)
    gather_i.run(Z2)
    gather_v.run(P1)
    gather_q.run(A2)
    gather_i.run(B1)
    gather_o.run(P0)
    gather_q.run(B2, P1)
    gather_o.run(E1)
    gather_i.run(Z1)
    gather_v.run(B3, B2)
    gather_q.run(Ao, Ap, B3, B4)
    gather_v.run(B5)
    gather_2.run(Z2)
    gather_o.run(B5)
    gather_i.run(P0)
    gather_q.run(B5)
    gather_v.run(E3)
    gather_q.run(E2, E1)
    gather_o.run(E2)
    gather_i.run(A2, B2)
    gather_v.run(E2)
    gather_q.run(E3)
    gather_i.run(P1)
    gather_o.run(E3)
    relay_output()
    short_params()
    gather_2.run(Z1, Z3, B1)
    project(1)
    gather_i.run(B3, Ao)
    project(0)
    attention(0, 0)
    attention(0, 1)
    branch(0)
    gather_i.run(B4)
    attention(1, 0)
    gather_2.run(A2)
    attention(1, 1)
    gather_i.run(E2, Ap)
    gather_2.run(P0)
    branch(1)
    attention(2, 0)
    gather_i.run(B5)
    attention(2, 1)
    gather_2.run(B2, P1)
    branch(2)
    attention(3, 0)
    gather_2.run(B3)
    attention(3, 1)
    branch(3)
    norm_first(0)
    gather_i.run(E3)
    norm_first(1)
    gather_i.run(E1)
    gather_2.run(Ao, B4)
    inner(0)
    inner(1)
    gather_2.run(Ap)
    inner(2)
    inner(3)
    gather_2.run(B5, E2)
    outer(0)
    gather_2.run(E1)
    outer(1)
    outer(2)
    gather_2.run(E3)
    outer(3)
    norm_second(0)
    norm_second(1)
    outer_terms(0)
    reduce_2.run(Ap)
    outer_terms(1)
    reduce_2.run(P0)
    outer_terms(2)
    reduce_2.run(B5, P1, B2, B3)
    outer_terms(3)
    reduce_2.run(B4)
    d_inner(0)
    d_inner(1)
    d_inner(2)
    d_inner(3)
    inner_terms(0)
    reduce_i.run(P0, P1)
    reduce_2.run(A2)
    inner_terms(1)
    inner_terms(2)
    reduce_2.run(B1)
    reduce_i.run(B5, B3)
    reduce_2.run(Ao)
    reduce_i.run(B4, B2)
    inner_terms(3)
    reduce_2.run(Z2)
    d_first(0)
    d_first(1)
    d_first(2)
    d_first(3)
    reduce_2.run(Zo)
    norm_first_back(0)
    norm_first_back(1)
    reduce_i.run(Ao)
    reduce_2.run(A0)
    reduce_i.run(Ap)
    reduce_2.run(Zp)
    reduce_i.run(B0)
    output_terms()
    reduce_2.run(B0)
    d_mixed()
    reduce_i.run(B1)
    reduce_o.run(B3, P1)
    attention_back(0, 0)
    reduce_i.run(A2)
    attention_back(0, 1)
    reduce_o.run(Ap)
    reduce_i.run(Zo)
    attention_back(1, 0)
    attention_back(1, 1)
    attention_back(2, 0)
    reduce_o.run(B5, P0)
    reduce_i.run(Zp)
    reduce_o.run(B4)
    attention_back(2, 1)
    reduce_o.run(B1)
    reduce_i.run(Z2)
    attention_back(3, 0)
    reduce_o.run(B2)
    attention_back(3, 1)
    reduce_o.run(Ao, A2)
    query_terms(0)
    reduce_o.run(A0)
    reduce_i.run(A0)
    reduce_q.run(P0)
    query_terms(1)
    query_terms(2)
    reduce_q.run(B5)
    short_sums()
    reduce_q.run(B4)
    query_terms(3)
    reduce_o.run(Zo)
    d_tokens(0)
    reduce_o.run(Z2)
    d_tokens(1)
    reduce_q.run(Ao, Ap, P1)
    short_terms()
    reduce_v.run(P0)
    d_tokens(2)
    d_tokens(3)
    reduce_v.run(P1)
    reduce_q.run(B3)
    reduce_v.run(B3)
    reduce_q.run(B2)
    reduce_v.run(B5)
    reduce_q.run(Zo)
    tokens_out()
    result_2()
    reduce_q.run(A2, Zp)
    reduce_v.run(Ap, Ao)
    reduce_q.run(B1)
    reduce_o.run(B0)
    result_i()
    reduce_v.run(A2)
    reduce_q.run(Z2)
    reduce_v.run(B2)
    reduce_o.run(Zp)
    reduce_q.run(B0)
    reduce_v.run(Zp)
    reduce_q.run(A0)
    result_i_out()
    reduce_v.run(Z2, B0, B1, B4, A0, Zo)
    result_q()
    result_o()
    result_v()
    result_q_out()

    for each in (gather_q, gather_o, gather_i, gather_2, gather_v):
        each.finish()
    for each in (reduce_q, reduce_o, reduce_i, reduce_2, reduce_v):
        each.finish()
    for each in pending + list(sent.values()):
        each()
    for copy in stores + [store_tokens]:
        copy.wait()


def layer(*arrays):
    def low(*shape):
        return pltpu.VMEM(shape, LOW)

    def full(*shape):
        return pltpu.VMEM(shape, F32)

    hbm = pl.BlockSpec(memory_space=pl.ANY)
    vmem = pl.BlockSpec(memory_space=pltpu.VMEM)
    smem = pl.BlockSpec(memory_space=pltpu.SMEM)
    scratch = [
        low(1024, 1024),
        low(1024, 1536),
        low(1024, 512),
        full(512, 1024),
        full(512, 1024),
        full(512, 1024),
        full(16, 32, 1024),
        full(512, 128),
        low(16, 2, 32, 1024),
        low(1024, 2048),
        low(16, 64, 2048),
        low(1024, 1024),
        low(512, 1024),
        low(16, 64, 1536),
        low(16, 2, 32, 1024),
        low(16, 64, 2048),
        low(16, 128, 1024),
        low(16, 128, 1024),
        low(16, 64, 2048),
        low(16, 32, 1024),
        low(COPIES, 128, 1024),
        low(COPIES, 64, 2048),
        low(COPIES, 32, 1024),
        low(32, 1536),
        low(32, 2048),
        full(4, 32, 1024),
        full(32, 4096),
        full(128, 1024),
        full(2, 8, 256),
        low(2, 16, 16, 128),
        full(16, 1024),
        full(8, 2048),
        full(SHORT, 8, 1024),
        full(8, 2048),
        full(8, 1024),
        full(8, 1024),
        full(16, 16, 128),
        full(COPIES, 16, 128),
        full(16, 128),
        pltpu.SemaphoreType.DMA((19,)),
        pltpu.SemaphoreType.DMA((24,)),
        pltpu.SemaphoreType.DMA((24,)),
        pltpu.SemaphoreType.DMA((10 * COPIES,)),
        pltpu.SemaphoreType.DMA((10 * COPIES,)),
        pltpu.SemaphoreType.REGULAR,
    ] + [full(1, 32)] * SHORT + [full(1, 128)]
    shape = jax.ShapeDtypeStruct
    return pl.pallas_call(
        layer_kernel,
        out_shape=(
            shape((512, 1024), LOW),
            shape((512, 1024), LOW),
            shape((32, 1024), F32),
            shape((32, 1024), F32),
            shape((32, 1024), F32),
            shape((32, 1024), F32),
            shape((32, 4096), F32),
            shape((128, 1024), F32),
            shape((16, 128), F32),
        ),
        in_specs=[hbm, smem] + [hbm] * (7 + SHORT + 1),
        out_specs=(hbm,) * 8 + (vmem,),
        scratch_shapes=scratch,
        compiler_params=pltpu.CompilerParams(
            collective_id=0, has_side_effects=True, vmem_limit_bytes=VMEM_BYTES
        ),
        cost_estimate=pl.CostEstimate(flops=40_000_000_000, bytes_accessed=8 << 20, transcendentals=0),
    )(*arrays)


VMEM_BYTES = 65_400 << 10


def hand_over_kernel(*refs):
    sources, vec, targets, parts = refs[:8], refs[8], refs[9:17], refs[17 : 17 + SHORT + 1]
    held, (in_sem, out_sem) = refs[17 + SHORT + 1 : -2], refs[-2:]
    loads = [pltpu.make_async_copy(sources[n], held[n], in_sem.at[n]) for n in range(8)]
    stores = [pltpu.make_async_copy(held[n], targets[n], out_sem.at[n]) for n in range(8)]
    for load in loads:
        load.start()
    for n in range(SHORT):
        parts[n][...] = vec[n : n + 1, 0:32]
    parts[SHORT][...] = vec[SHORT : SHORT + 1, :]
    for load, store in zip(loads, stores):
        load.wait()
        store.start()
    for store in stores:
        store.wait()


def hand_over(*results):
    hbm = pl.BlockSpec(memory_space=pl.ANY)
    vmem = pl.BlockSpec(memory_space=pltpu.VMEM)
    shape = jax.ShapeDtypeStruct
    return pl.pallas_call(
        hand_over_kernel,
        out_shape=tuple(shape(each.shape, each.dtype) for each in results[:8])
        + (shape((1, 32), F32),) * SHORT
        + (shape((1, 128), F32),),
        in_specs=[hbm] * 8 + [vmem],
        out_specs=(hbm,) * 8 + (vmem,) * (SHORT + 1),
        scratch_shapes=[pltpu.VMEM(each.shape, each.dtype) for each in results[:8]]
        + [pltpu.SemaphoreType.DMA((8,))] * 2,
        compiler_params=pltpu.CompilerParams(vmem_limit_bytes=VMEM_BYTES),
    )(*results)


def one_kernel_device(
    tokens,
    lengths,
    cotangent,
    query_weight,
    key_weight,
    value_weight,
    output_weight,
    query_bias,
    value_bias,
    output_bias,
    first_gain,
    first_shift,
    inner_weight,
    inner_bias,
    outer_weight,
    outer_bias,
    second_gain,
    second_shift,
):
    count, seq, width = tokens.shape
    rows = count * seq
    short = (query_bias, value_bias, output_bias, first_gain, first_shift, outer_bias, second_gain, second_shift)
    outs = layer(
        tokens.reshape(rows, width),
        lengths,
        cotangent.reshape(rows, width),
        query_weight,
        key_weight,
        value_weight,
        output_weight,
        inner_weight,
        outer_weight,
        *[each.reshape(1, -1) for each in short + (inner_bias,)],
    )
    outs = hand_over(*outs)
    layer_rows, token_grad, query_g, key_g, value_g, output_g, inner_g, outer_g, *part = outs
    part = [each.reshape(-1) for each in part]
    return (
        layer_rows.reshape(count, seq, width),
        token_grad.reshape(count, seq, width),
        query_g,
        key_g,
        value_g,
        output_g,
        part[BQ],
        part[BV],
        part[BO],
        part[G1],
        part[S1],
        inner_g,
        part[SHORT],
        outer_g,
        part[BF],
        part[G2],
        part[S2],
    )


epsilon = 1e-12


def normalize(hidden, gain, shift):
    center = hidden - jnp.mean(hidden, axis=-1, keepdims=True)
    spread = jnp.mean(center * center, axis=-1, keepdims=True)
    return center * lax.rsqrt(spread + epsilon) * gain + shift


def gelu_exact(inner):
    return jax.nn.gelu(inner, approximate=False)


def matmul(left, right):
    return jnp.dot(left, right, preferred_element_type=jnp.float32)


def matmul_left_t(left, right):
    return lax.dot_general(
        left, right, (((0,), (0,)), ((), ())), preferred_element_type=jnp.float32
    )


def matmul_right_t(left, right):
    return lax.dot_general(
        left, right, (((1,), (1,)), ((), ())), preferred_element_type=jnp.float32
    )


def row_sum(values):
    return jnp.sum(values.astype(jnp.float32), axis=0)


def per_device(
    tokens,
    lengths,
    cotangent,
    query_weight,
    key_weight,
    value_weight,
    output_weight,
    query_bias,
    value_bias,
    output_bias,
    first_gain,
    first_shift,
    inner_weight,
    inner_bias,
    outer_weight,
    outer_bias,
    second_gain,
    second_shift,
):
    attn_master = (
        query_weight,
        key_weight,
        value_weight,
        output_weight,
        query_bias,
        value_bias,
        output_bias,
        first_gain,
        first_shift,
    )
    ffn_master = (inner_weight, inner_bias, outer_weight, outer_bias, second_gain, second_shift)
    attn_half = [param.astype(jnp.bfloat16) for param in attn_master]
    ffn_half = [param.astype(jnp.bfloat16) for param in ffn_master]
    micro_count, rows, width = tokens.shape
    heads = width // HD
    owners = lax.axis_size(("dp", "fsdp"))
    scale = 1.0 / math.sqrt(HD)
    positions = jnp.arange(rows, dtype=jnp.int32)
    attn_totals = [
        jnp.zeros((param.shape[0] * owners,) + param.shape[1:], jnp.float32)
        for param in attn_master
    ]
    ffn_totals = [
        jnp.zeros((param.shape[0] * owners,) + param.shape[1:], jnp.float32) for param in ffn_master
    ]
    outputs_list = []
    token_grads_list = []
    for micro in range(micro_count):
        token_rows = tokens[micro]
        cot_rows = cotangent[micro].astype(jnp.float32)
        valid_keys = positions < lengths[micro]
        attn_full = (
            lax.all_gather(attn_half[0], ("dp", "fsdp"), axis=0, tiled=True),
            lax.all_gather(attn_half[1], ("dp", "fsdp"), axis=0, tiled=True),
            lax.all_gather(attn_half[2], ("dp", "fsdp"), axis=0, tiled=True),
            lax.all_gather(attn_half[3], ("dp", "fsdp"), axis=0, tiled=True),
            lax.all_gather(attn_half[4], ("dp", "fsdp"), axis=0, tiled=True),
            lax.all_gather(attn_half[5], ("dp", "fsdp"), axis=0, tiled=True),
            lax.all_gather(attn_half[6], ("dp", "fsdp"), axis=0, tiled=True),
            lax.all_gather(attn_half[7], ("dp", "fsdp"), axis=0, tiled=True),
            lax.all_gather(attn_half[8], ("dp", "fsdp"), axis=0, tiled=True),
        )
        query_use, key_use, value_use, output_use = (
            attn_full[0],
            attn_full[1],
            attn_full[2],
            attn_full[3],
        )
        bias_query = attn_full[4].astype(jnp.float32)
        bias_value = attn_full[5].astype(jnp.float32)
        bias_output = attn_full[6].astype(jnp.float32)
        gain_first = attn_full[7].astype(jnp.float32)
        shift_first = attn_full[8].astype(jnp.float32)
        query_rows = (matmul(token_rows, query_use) + bias_query).astype(jnp.bfloat16)
        key_rows = matmul(token_rows, key_use).astype(jnp.bfloat16)
        value_rows = (matmul(token_rows, value_use) + bias_value).astype(jnp.bfloat16)
        query_heads = query_rows.reshape(rows, heads, HD)
        key_heads = key_rows.reshape(rows, heads, HD)
        value_heads = value_rows.reshape(rows, heads, HD)

        def attention_scores():
            raw_scores = (
                jnp.einsum(
                    "qhd,khd->hqk", query_heads, key_heads, preferred_element_type=jnp.float32
                )
                * scale
            )
            return jnp.where(valid_keys[None, None, :], raw_scores, -1000000000.0)

        scores = attention_scores()
        peak = jnp.max(scores, axis=-1, keepdims=True)
        log_total = peak + jnp.log(jnp.sum(jnp.exp(scores - peak), axis=-1, keepdims=True))
        probs_low = jnp.exp(scores - log_total).astype(jnp.bfloat16)
        mixed = (
            jnp.einsum("hqk,khd->qhd", probs_low, value_heads, preferred_element_type=jnp.float32)
            .reshape(rows, width)
            .astype(jnp.bfloat16)
        )
        residual = token_rows.astype(jnp.float32) + matmul(mixed, output_use) + bias_output
        first = normalize(residual, gain_first, shift_first)
        first_low = first.astype(jnp.bfloat16)
        ffn_full = (
            lax.all_gather(ffn_half[0], ("dp", "fsdp"), axis=0, tiled=True),
            lax.all_gather(ffn_half[1], ("dp", "fsdp"), axis=0, tiled=True),
            lax.all_gather(ffn_half[2], ("dp", "fsdp"), axis=0, tiled=True),
            lax.all_gather(ffn_half[3], ("dp", "fsdp"), axis=0, tiled=True),
            lax.all_gather(ffn_half[4], ("dp", "fsdp"), axis=0, tiled=True),
            lax.all_gather(ffn_half[5], ("dp", "fsdp"), axis=0, tiled=True),
        )
        inner = matmul(first_low, ffn_full[0]) + ffn_full[1].astype(jnp.float32)
        active = gelu_exact(inner).astype(jnp.bfloat16)
        second_in = first + matmul(active, ffn_full[2]) + ffn_full[3].astype(jnp.float32)
        gain_second = ffn_full[4].astype(jnp.float32)
        shift_second = ffn_full[5].astype(jnp.float32)
        layer_rows, pull_second = jax.vjp(normalize, second_in, gain_second, shift_second)
        outputs_list.append(layer_rows.astype(jnp.bfloat16))
        ffn_full = (
            lax.all_gather(ffn_half[0], ("dp", "fsdp"), axis=0, tiled=True),
            lax.all_gather(ffn_half[1], ("dp", "fsdp"), axis=0, tiled=True),
            lax.all_gather(ffn_half[2], ("dp", "fsdp"), axis=0, tiled=True),
            lax.all_gather(ffn_half[3], ("dp", "fsdp"), axis=0, tiled=True),
            lax.all_gather(ffn_half[4], ("dp", "fsdp"), axis=0, tiled=True),
            lax.all_gather(ffn_half[5], ("dp", "fsdp"), axis=0, tiled=True),
        )
        d_second, d_gain_second, d_shift_second = pull_second(cot_rows)
        d_outer = d_second.astype(jnp.bfloat16)
        ffn_totals[2] = ffn_totals[2] + matmul_left_t(active, d_outer)
        ffn_totals[3] = ffn_totals[3] + row_sum(d_outer)
        ffn_totals[4] = ffn_totals[4] + d_gain_second
        ffn_totals[5] = ffn_totals[5] + d_shift_second
        d_active = matmul_right_t(d_outer, ffn_full[2])
        gelu_value, pull_gelu = jax.vjp(gelu_exact, inner)
        (d_inner,) = pull_gelu(d_active)
        d_inner_low = d_inner.astype(jnp.bfloat16)
        ffn_totals[0] = ffn_totals[0] + matmul_left_t(first_low, d_inner_low)
        ffn_totals[1] = ffn_totals[1] + row_sum(d_inner_low)
        d_first = matmul_right_t(d_inner_low, ffn_full[0]) + d_second
        attn_full = (
            lax.all_gather(attn_half[0], ("dp", "fsdp"), axis=0, tiled=True),
            lax.all_gather(attn_half[1], ("dp", "fsdp"), axis=0, tiled=True),
            lax.all_gather(attn_half[2], ("dp", "fsdp"), axis=0, tiled=True),
            lax.all_gather(attn_half[3], ("dp", "fsdp"), axis=0, tiled=True),
            lax.all_gather(attn_half[4], ("dp", "fsdp"), axis=0, tiled=True),
            lax.all_gather(attn_half[5], ("dp", "fsdp"), axis=0, tiled=True),
            lax.all_gather(attn_half[6], ("dp", "fsdp"), axis=0, tiled=True),
            lax.all_gather(attn_half[7], ("dp", "fsdp"), axis=0, tiled=True),
            lax.all_gather(attn_half[8], ("dp", "fsdp"), axis=0, tiled=True),
        )
        query_use, key_use, value_use, output_use = (
            attn_full[0],
            attn_full[1],
            attn_full[2],
            attn_full[3],
        )
        norm_value, pull_first = jax.vjp(
            normalize, residual, attn_full[7].astype(jnp.float32), attn_full[8].astype(jnp.float32)
        )
        d_residual, d_gain_first, d_shift_first = pull_first(d_first)
        attn_totals[7] = attn_totals[7] + d_gain_first
        attn_totals[8] = attn_totals[8] + d_shift_first
        d_branch = d_residual.astype(jnp.bfloat16)
        attn_totals[3] = attn_totals[3] + matmul_left_t(mixed, d_branch)
        attn_totals[6] = attn_totals[6] + row_sum(d_branch)
        d_mixed = matmul_right_t(d_branch, output_use).astype(jnp.bfloat16).reshape(rows, heads, HD)
        scores = attention_scores()
        probs = jnp.exp(scores - log_total)
        probs_low = probs.astype(jnp.bfloat16)
        d_probs = jnp.einsum(
            "qhd,khd->hqk", d_mixed, value_heads, preferred_element_type=jnp.float32
        )
        d_values = jnp.einsum(
            "hqk,qhd->khd", probs_low, d_mixed, preferred_element_type=jnp.float32
        ).reshape(rows, width)
        delta_rows = jnp.sum(probs * d_probs, axis=-1, keepdims=True)
        d_scores = (probs * (d_probs - delta_rows)).astype(jnp.bfloat16)
        d_queries = (
            (
                jnp.einsum("hqk,khd->qhd", d_scores, key_heads, preferred_element_type=jnp.float32)
                * scale
            )
            .reshape(rows, width)
            .astype(jnp.bfloat16)
        )
        d_keys = (
            jnp.einsum(
                "hqk,qhd->khd", d_scores, query_heads, preferred_element_type=jnp.float32
            ).reshape(rows, width)
            * scale
        )
        key_low = d_keys.astype(jnp.bfloat16)
        value_low = d_values.astype(jnp.bfloat16)
        attn_totals[0] = attn_totals[0] + matmul_left_t(token_rows, d_queries)
        attn_totals[1] = attn_totals[1] + matmul_left_t(token_rows, key_low)
        attn_totals[2] = attn_totals[2] + matmul_left_t(token_rows, value_low)
        attn_totals[4] = attn_totals[4] + row_sum(d_queries)
        attn_totals[5] = attn_totals[5] + row_sum(value_low)
        token_grad = (
            d_residual
            + matmul_right_t(d_queries, query_use)
            + matmul_right_t(key_low, key_use)
            + matmul_right_t(value_low, value_use)
        )
        token_grads_list.append(token_grad.astype(jnp.bfloat16))
    attn_shards = (
        lax.psum_scatter(attn_totals[0], ("dp", "fsdp"), scatter_dimension=0, tiled=True),
        lax.psum_scatter(attn_totals[1], ("dp", "fsdp"), scatter_dimension=0, tiled=True),
        lax.psum_scatter(attn_totals[2], ("dp", "fsdp"), scatter_dimension=0, tiled=True),
        lax.psum_scatter(attn_totals[3], ("dp", "fsdp"), scatter_dimension=0, tiled=True),
        lax.psum_scatter(attn_totals[4], ("dp", "fsdp"), scatter_dimension=0, tiled=True),
        lax.psum_scatter(attn_totals[5], ("dp", "fsdp"), scatter_dimension=0, tiled=True),
        lax.psum_scatter(attn_totals[6], ("dp", "fsdp"), scatter_dimension=0, tiled=True),
        lax.psum_scatter(attn_totals[7], ("dp", "fsdp"), scatter_dimension=0, tiled=True),
        lax.psum_scatter(attn_totals[8], ("dp", "fsdp"), scatter_dimension=0, tiled=True),
    )
    ffn_shards = (
        lax.psum_scatter(ffn_totals[0], ("dp", "fsdp"), scatter_dimension=0, tiled=True),
        lax.psum_scatter(ffn_totals[1], ("dp", "fsdp"), scatter_dimension=0, tiled=True),
        lax.psum_scatter(ffn_totals[2], ("dp", "fsdp"), scatter_dimension=0, tiled=True),
        lax.psum_scatter(ffn_totals[3], ("dp", "fsdp"), scatter_dimension=0, tiled=True),
        lax.psum_scatter(ffn_totals[4], ("dp", "fsdp"), scatter_dimension=0, tiled=True),
        lax.psum_scatter(ffn_totals[5], ("dp", "fsdp"), scatter_dimension=0, tiled=True),
    )
    return (
        jnp.stack(outputs_list),
        jnp.stack(token_grads_list),
        attn_shards[0],
        attn_shards[1],
        attn_shards[2],
        attn_shards[3],
        attn_shards[4],
        attn_shards[5],
        attn_shards[6],
        attn_shards[7],
        attn_shards[8],
        ffn_shards[0],
        ffn_shards[1],
        ffn_shards[2],
        ffn_shards[3],
        ffn_shards[4],
        ffn_shards[5],
    )


def solution(mesh):
    in_specs = (
        P(("dp", "fsdp"), None, None),
        P(("dp", "fsdp")),
        P(("dp", "fsdp"), None, None),
        P(("dp", "fsdp"), None),
        P(("dp", "fsdp"), None),
        P(("dp", "fsdp"), None),
        P(("dp", "fsdp"), None),
        P(("dp", "fsdp")),
        P(("dp", "fsdp")),
        P(("dp", "fsdp")),
        P(("dp", "fsdp")),
        P(("dp", "fsdp")),
        P(("dp", "fsdp"), None),
        P(("dp", "fsdp")),
        P(("dp", "fsdp"), None),
        P(("dp", "fsdp")),
        P(("dp", "fsdp")),
        P(("dp", "fsdp")),
    )
    out_specs = (
        P(("dp", "fsdp"), None, None),
        P(("dp", "fsdp"), None, None),
        P(("dp", "fsdp"), None),
        P(("dp", "fsdp"), None),
        P(("dp", "fsdp"), None),
        P(("dp", "fsdp"), None),
        P(("dp", "fsdp")),
        P(("dp", "fsdp")),
        P(("dp", "fsdp")),
        P(("dp", "fsdp")),
        P(("dp", "fsdp")),
        P(("dp", "fsdp"), None),
        P(("dp", "fsdp")),
        P(("dp", "fsdp"), None),
        P(("dp", "fsdp")),
        P(("dp", "fsdp")),
        P(("dp", "fsdp")),
    )
    one_kernel = dict(mesh.shape) == {"dp": 16, "fsdp": 2}
    device = one_kernel_device if one_kernel else per_device
    return jax.shard_map(
        device, mesh=mesh, in_specs=in_specs, out_specs=out_specs, check_vma=False
    )
```

```python
import functools
import math

import jax
import jax.numpy as jnp
from jax import lax
from jax.experimental import pallas as pl
from jax.experimental.pallas import tpu as pltpu
from jax.sharding import PartitionSpec as P

MESH = pl.DeviceIdType.MESH
COPIES = 15
HD = 64
LOW = jnp.bfloat16
F32 = jnp.float32


class Place:
    def __init__(self):
        self.me = lax.axis_index("dp")
        self.core = lax.axis_index("fsdp")
        x, y, self.z = lax.rem(self.me, 2), lax.rem(self.me // 2, 2), self.me // 4
        self.a = x + self.core * (y - x)
        self.b = y + self.core * (x - y)
        odd = lax.rem(self.z, 2)
        self.pair, self.other = 3 - 2 * odd, 1 + 2 * odd
        self.z_pair = self.z + 1 - 2 * odd

    def chip(self, z, a, b):
        return z * 4 + (b + self.core * (a - b)) * 2 + (a + self.core * (b - a))

    def back(self, j):
        return lax.rem(self.z - j + 4, 4)

    def peers(self):
        along_z = [self.chip(lax.rem(self.z + k, 4), self.a, self.b) for k in (1, 2, 3)]
        return along_z + [self.chip(self.z, 1 - self.a, self.b), self.chip(self.z, self.a, 1 - self.b)]

    def signal_peers(self, sem):
        for chip in self.peers():
            pl.semaphore_signal(sem, inc=1, device_id=(chip, self.core), device_id_type=MESH)

    def announce(self):
        sem = pltpu.get_barrier_semaphore()
        self.signal_peers(sem)
        pl.semaphore_signal(sem, inc=1, device_id=(self.me, 1 - self.core), device_id_type=MESH)

    def meet(self):
        pl.semaphore_wait(pltpu.get_barrier_semaphore(), 6)


class Hops:
    def __init__(self, place, send_sem, recv_sem, base):
        self.place, self.send_sem, self.recv_sem, self.base = place, send_sem, recv_sem, base
        self.started = []

    def send(self, k, source, target, chip):
        copy = pltpu.make_async_remote_copy(
            src_ref=source,
            dst_ref=target,
            send_sem=self.send_sem.at[self.base + k],
            recv_sem=self.recv_sem.at[self.base + k],
            device_id=(chip, self.place.core),
            device_id_type=MESH,
        )
        copy.start()
        self.started.append(copy)

    def arrived(self, k, block):
        pltpu.make_async_remote_copy(
            src_ref=block,
            dst_ref=block,
            send_sem=self.send_sem.at[self.base + k],
            recv_sem=self.recv_sem.at[self.base + k],
            device_id=(self.place.me, self.place.core),
            device_id_type=MESH,
        ).wait_recv()

    def finish(self):
        for copy in self.started:
            copy.wait_send()
        self.started = []


class Gather(Hops):
    def __init__(self, place, held, *rest):
        super().__init__(place, *rest)
        self.held = held

    def pass_on(self, k, block, chip):
        self.send(k, self.held.at[block], self.held.at[block], chip)

    def wait(self, *copies):
        for k in copies:
            self.arrived(k, self.held.at[self.place.me])

    def run(self, *hops):
        for hop in hops:
            self.take(hop)

    def take(self, name):
        p = self.place
        kind, which = name
        which = {PAIR: p.pair, OTHER: p.other}.get(which, which)
        if kind == Z:
            self.pass_on(which - 1, p.me, p.chip(lax.rem(p.z + which, 4), p.a, p.b))
        elif kind == A:
            if name != A0:
                self.wait(which - 1)
            self.pass_on(3 + which, p.chip(p.back(which), p.a, p.b), p.chip(p.z, 1 - p.a, p.b))
        elif kind == B:
            j = (0, 0, 2, 2, p.other, p.other)[which]
            if which % 2:
                self.wait(3 + j)
            block = p.chip(p.back(j), (p.a, 1 - p.a)[which % 2], p.b)
            self.pass_on(7 + which, block, p.chip(p.z, p.a, 1 - p.b))
        elif kind == P_:
            self.wait(7 + which)
            block = p.chip(p.z, (p.a, 1 - p.a)[which], 1 - p.b)
            self.pass_on(13 + which, block, p.chip(p.z_pair, p.a, p.b))
        else:
            self.wait(*((), (3 + p.pair,), (9, 10), (11, 12, 13, 14))[which])


class Reduce(Hops):
    def __init__(self, place, terms, landed, chunk, *rest):
        super().__init__(place, *rest)
        self.terms, self.landed, self.chunk = terms, landed, chunk

    def sum_into(self, block, ks, store):
        for k in ks:
            self.arrived(k, self.landed(k))
        term = self.terms(block)
        landed = [self.landed(k) for k in ks]
        rows = term.shape[0]

        def some(n):
            at = rows_at(n, self.chunk)
            total = term[at].astype(F32)
            for each in landed:
                total += each[at].astype(F32)
            store(n, total)

        if rows == self.chunk:
            some(0)
        else:
            pl.loop(0, rows // self.chunk)(some)

    def add_and_send(self, k, block, ks, chip):
        term = self.terms(block)
        if ks:

            def store(n, total):
                term[rows_at(n, self.chunk)] = total.astype(term.dtype)

            self.sum_into(block, ks, store)
        self.send(k, term, self.landed(k), chip)

    def run(self, *hops):
        for hop in hops:
            self.take(hop)

    def take(self, name):
        p = self.place
        kind, which = name
        which = {PAIR: p.pair, OTHER: p.other}.get(which, which)
        if kind == P_:
            block = p.chip(p.z_pair, (p.a, 1 - p.a)[which], 1 - p.b)
            self.add_and_send(13 + which, block, (), p.chip(p.z_pair, p.a, p.b))
        elif kind == B:
            j = (0, 0, 2, 2, p.other, p.other)[which]
            block = p.chip(p.back(j), (p.a, 1 - p.a)[which % 2], 1 - p.b)
            landed = (13 + which,) if which < 2 else ()
            self.add_and_send(7 + which, block, landed, p.chip(p.z, p.a, 1 - p.b))
        elif kind == A:
            landed = {A0: (8,), A2: (10,), Ao: (12,), Ap: ()}[name]
            block = p.chip(p.back(which), 1 - p.a, p.b)
            self.add_and_send(3 + which, block, landed, p.chip(p.z, 1 - p.a, p.b))
        else:
            landed = {Z2: (9, 5), Zo: (11, 3 + p.other), Zp: (3 + p.pair,)}[name]
            owner = p.chip(p.back(which), p.a, p.b)
            self.add_and_send(3 - which, owner, landed, owner)

    def result(self, store):
        self.sum_into(self.place.me, (7, 3, 0, 1, 2), store)


class Across:
    def __init__(self, place, send_sem, recv_sem):
        self.place, self.send_sem, self.recv_sem = place, send_sem, recv_sem
        self.count = 0

    def copy(self, k, source, target):
        p = self.place
        return pltpu.make_async_remote_copy(
            src_ref=source,
            dst_ref=target,
            send_sem=self.send_sem.at[k],
            recv_sem=self.recv_sem.at[k],
            device_id=(p.me, 1 - p.core),
            device_id_type=MESH,
        )

    def send(self, source, target, here=None):
        k = self.count
        self.count += 1
        copy = self.copy(k, source, target)
        copy.start()
        landing = target if here is None else here
        return copy.wait_send, self.copy(k, landing, landing).wait_recv


def dot(left, right):
    return jnp.dot(left, right, preferred_element_type=F32)


def dot_left_t(left, right):
    return lax.dot_general(left, right, (((0,), (0,)), ((), ())), preferred_element_type=F32)


def dot_right_t(left, right):
    return lax.dot_general(left, right, (((1,), (1,)), ((), ())), preferred_element_type=F32)


def fold(values):
    rows, columns = values.shape
    return jnp.sum(values.reshape(rows // 8, 8, columns), axis=0)


def rows_at(index, size):
    if isinstance(index, int):
        return pl.ds(index * size, size)
    return pl.ds(pl.multiple_of(index * size, size), size)


Z, A, B, P_, E = range(5)
PAIR, OTHER = -1, -2
Z1, Z2, Z3, Zp, Zo = (Z, 1), (Z, 2), (Z, 3), (Z, PAIR), (Z, OTHER)
A0, A2, Ap, Ao = (A, 0), (A, 2), (A, PAIR), (A, OTHER)
B0, B1, B2, B3, B4, B5 = [(B, n) for n in range(6)]
P0, P1 = (P_, 0), (P_, 1)
E1, E2, E3 = (E, 1), (E, 2), (E, 3)
EARLY = (Z2, A0, B0, Z1, Z3)

SHORT = 8
BQ, BV, BO, G1, S1, BF, G2, S2 = range(SHORT)
EPSILON = 1e-12


def layer_kernel(
    tokens,
    lengths,
    cotangent,
    query_weight,
    key_weight,
    value_weight,
    output_weight,
    inner_weight,
    outer_weight,
    *rest,
):
    short_shards, rest = rest[: SHORT + 1], rest[SHORT + 1 :]
    layer_body(
        tokens,
        lengths,
        cotangent,
        query_weight,
        key_weight,
        value_weight,
        output_weight,
        inner_weight,
        outer_weight,
        short_shards,
        rest[-SHORT - 1 :],
        *rest[: -SHORT - 1],
    )


def layer_body(
    tokens,
    lengths,
    cotangent,
    query_weight,
    key_weight,
    value_weight,
    output_weight,
    inner_weight,
    outer_weight,
    short_shards,
    short_here,
    layer_out,
    token_grad,
    query_grad,
    key_grad,
    value_grad,
    output_grad,
    inner_grad,
    outer_grad,
    vec_grad,
    x_all,
    qkv,
    mix,
    acc,
    out_part,
    in_part,
    xhat,
    scale1,
    first,
    act,
    slope,
    dout,
    w_qkv,
    w_o,
    w_i,
    w_2,
    t_2,
    t_i,
    landed_2,
    landed_i,
    stage_q,
    stage_i,
    mask,
    vec_all,
    params,
    inner_bias,
    g_part,
    i_part,
    g_sum,
    g_other,
    v_terms,
    v_landed,
    v_stage,
    local_sem,
    core_send,
    core_recv,
    send_sem,
    recv_sem,
    ready_sem,
):
    f_s = (query_grad, key_grad, value_grad, output_grad)
    f_i, f_2, gbuf = inner_grad, outer_grad, layer_out
    p = Place()
    me, core = p.me, p.core
    peer = 1 - core
    across = Across(p, core_send, core_recv)
    pending = []

    own_rows = rows_at(core, 512)
    peer_rows = rows_at(peer, 512)

    def local(k, source, target):
        return pltpu.make_async_copy(source, target, local_sem.at[k])

    loads = [
        local(0, query_weight, f_s[0]),
        local(1, key_weight, f_s[1]),
        local(2, value_weight, f_s[2]),
        local(3, output_weight, f_s[3]),
        local(4, inner_weight, f_i),
        local(5, outer_weight, f_2),
        local(6, tokens, x_all.at[own_rows]),
        local(7, cotangent, gbuf),
    ]
    loads += [local(10 + n, short_shards[n], short_here[n]) for n in range(SHORT + 1)]
    for copy in loads:
        copy.start()

    places = lax.broadcasted_iota(jnp.int32, (8, 256), 1)
    seq_of = lax.broadcasted_iota(jnp.int32, (8, 256), 0)
    limit = jnp.where(seq_of == 0, lengths[0], lengths[1])
    mask[core] = jnp.where(places < limit, 1.0, 0.0).astype(F32)
    p.announce()
    v_stage[...] = jnp.zeros_like(v_stage)
    for copy in loads[8:]:
        copy.wait()
    for n in range(SHORT):
        v_stage[n : n + 1, 0:32] = short_here[n][...]
    v_stage[SHORT : SHORT + 1, :] = short_here[SHORT][...]
    piece = v_stage[...]
    four = piece + pltpu.roll(piece, 32, 1) + pltpu.roll(piece, 64, 1) + pltpu.roll(piece, 96, 1)
    is_short = lax.broadcasted_iota(jnp.int32, (16, 128), 0) < SHORT
    vec_all[core, me] = jnp.where(is_short, four, piece).astype(LOW)
    g_part[...] = jnp.zeros_like(g_part)
    i_part[...] = jnp.zeros_like(i_part)

    for copy in loads[:4]:
        copy.wait()
    my_rows = rows_at(core, 32)
    for n in range(3):
        w_qkv[me, my_rows, 512 * n : 512 * n + 512] = f_s[n][:, rows_at(core, 512)].astype(LOW)
        stage_q[:, 512 * n : 512 * n + 512] = f_s[n][:, rows_at(peer, 512)].astype(LOW)
    w_o[me, core] = f_s[3][...].astype(LOW)
    loads[5].wait()
    w_2[me] = f_2[...].astype(LOW)
    p.meet()
    sent_q, got_q = across.send(stage_q, w_qkv.at[me, my_rows], w_qkv.at[me, rows_at(peer, 32)])
    sent_m, got_m = across.send(mask.at[core], mask.at[core], mask.at[peer])
    gather_o = Gather(p, w_o.at[:, core], send_sem, recv_sem, COPIES)
    gather_v = Gather(p, vec_all.at[core], send_sem, recv_sem, 4 * COPIES)
    gather_q = Gather(p, w_qkv, send_sem, recv_sem, 0)
    gather_i = Gather(p, w_i, send_sem, recv_sem, 2 * COPIES)
    gather_2 = Gather(p, w_2, send_sem, recv_sem, 3 * COPIES)
    gather_o.run(*EARLY)
    gather_v.run(*EARLY)
    gather_2.run(A0, B0)
    loads[4].wait()
    for n in range(16):
        here, there = 2 * n + core, 2 * n + peer
        at = slice(128 * n, 128 * n + 128)
        w_i[me, my_rows, at] = f_i[:, rows_at(here, 128)].astype(LOW)
        stage_i[:, at] = f_i[:, rows_at(there, 128)].astype(LOW)
    sent_i, got_i = across.send(stage_i, w_i.at[me, my_rows], w_i.at[me, rows_at(peer, 32)])
    got_q()
    gather_q.run(*EARLY)
    loads[6].wait()
    sent_x, got_x = across.send(x_all.at[own_rows], x_all.at[own_rows], x_all.at[peer_rows])
    got_i()
    pending += [sent_q, sent_m, sent_i, sent_x]
    sent, got = {}, {}

    def exchange(name, source, target, here=None):
        sent[name], got[name] = across.send(source, target, here)

    def done(*names):
        for name in names:
            sent.pop(name)()

    def relay_output():
        mine = rows_at(core, 8)
        theirs = rows_at(peer, 8)
        exchange("o", w_o.at[theirs, core], w_o.at[theirs, core], w_o.at[mine, peer])
        exchange("v", vec_all.at[core], vec_all.at[core], vec_all.at[peer])

    def short_params():
        got["v"]()
        lane_group = lax.broadcasted_iota(jnp.int32, (16, 128), 1) // 32
        for t in range(8):
            pieces = [vec_all[i % 2, 2 * t + i // 2].astype(F32) for i in range(4)]
            tile = jnp.where(
                lane_group < 2,
                jnp.where(lane_group == 0, pieces[0], pieces[1]),
                jnp.where(lane_group == 2, pieces[2], pieces[3]),
            )
            params[:, 128 * t : 128 * t + 128] = tile
        for n in range(16):
            inner_bias[:, 128 * n : 128 * n + 128] = vec_all[core, n].astype(F32)[8:16]
        got_x()
        got_m()

    def param(n):
        return params[n : n + 1, :]

    def project(turn):
        owner = (core, peer)[turn]

        @pl.loop(0, 2)
        def _(half):
            rows = rows_at(2 * owner + half, 256)
            block = x_all[rows, :]
            for n in range(3):
                part = dot(block, w_qkv[:, :, 512 * n : 512 * n + 512].reshape(1024, 512))
                if n != 1:
                    part = part + params[BQ if n == 0 else BV, rows_at(core, 512)][None, :]
                qkv[rows, 512 * n : 512 * n + 512] = part.astype(LOW)

    left_half = lax.broadcasted_iota(jnp.int32, (256, 128), 1) < HD

    def heads_of(s, t):
        rows = rows_at(s, 256)
        return [qkv[rows, pl.ds(pl.multiple_of(512 * n + 128 * t, 128), 128)] for n in range(3)]

    def softmax(query_half, key, valid):
        raw = dot_right_t(query_half, key)
        raw = jnp.where(valid, raw, -1000000000.0)
        grown = jnp.exp(raw - jnp.max(raw, axis=-1, keepdims=True))
        return grown * (1.0 / jnp.sum(grown, axis=-1, keepdims=True))

    def halves(pair):
        none = jnp.zeros_like(pair)
        return jnp.where(left_half, pair, none), jnp.where(left_half, none, pair)

    scale = jnp.array(1.0 / math.sqrt(HD), LOW)

    def turn_of(turn):
        return (peer, peer, core, core)[turn], turn % 2

    def attention(turn, part):
        owner, n = turn_of(turn)
        s = 2 * owner + n
        valid = mask[owner, n : n + 1, :] > 0.5

        @pl.loop(2 * part, 2 * part + 2)
        def _(t):
            query, key, value = heads_of(s, t)
            outs = [
                dot(softmax(half, key, valid).astype(LOW), value) for half in halves(query * scale)
            ]
            both = jnp.where(left_half, outs[0], outs[1]).astype(LOW)
            mix[rows_at(s, 256), rows_at(t, 128)] = both

    def part_name(half):
        return "part0" if half == 0 else "part1"

    def pass_part(half):
        at = slice(256 * half, 256 * half + 256)
        exchange(part_name(half), out_part.at[at], in_part.at[at])

    def branch(turn):
        owner, n = turn_of(turn)
        if turn == 0:
            got["o"]()
        out_use = w_o[rows_at(core, 8)].reshape(512, 1024)
        part = dot(mix[rows_at(2 * owner + n, 256), :], out_use)
        at = slice(256 * n, 256 * n + 256)
        if turn < 2:
            out_part[at] = part
            pass_part(n)
        else:
            acc[at] = part

    def norm_of(hidden):
        center = hidden - jnp.mean(hidden, axis=-1, keepdims=True)
        spread = jnp.mean(center * center, axis=-1, keepdims=True)
        inverse = lax.rsqrt(spread + EPSILON)
        return center * inverse, inverse

    def norm_back(grown, normal, inverse):
        along = jnp.mean(grown * normal, axis=-1, keepdims=True)
        return inverse * (grown - jnp.mean(grown, axis=-1, keepdims=True) - normal * along)

    BLOCK = 128

    def tokens_of(owner, n):
        return pl.ds(pl.multiple_of(512 * owner + BLOCK * n, BLOCK), BLOCK)

    def half_of(owner, half):
        return pl.ds(pl.multiple_of(512 * owner + 256 * half, 256), 256)

    def share(name, whole, half):
        exchange(name + str(half), whole.at[half_of(core, half)], whole.at[half_of(core, half)], whole.at[half_of(peer, half)])

    def norm_first(half):
        got[part_name(half)]()

        @pl.loop(2 * half, 2 * half + 2)
        def _(n):
            at = rows_at(n, BLOCK)
            hidden = x_all[tokens_of(core, n), :].astype(F32) + acc[at] + in_part[at] + param(BO)
            normal, inverse = norm_of(hidden)
            xhat[rows_at(n, 4)] = normal.reshape(4, 32, 1024)
            scale1[at] = jnp.broadcast_to(inverse, (BLOCK, 128))
            first[pl.ds(8 * core + 2 * n, 2)] = (normal * param(G1) + param(S1)).astype(LOW).reshape(2, 2, 32, 1024)

        mine = pl.ds(8 * core + 4 * half, 4)
        theirs = pl.ds(8 * peer + 4 * half, 4)
        exchange("first" + str(half), first.at[mine], first.at[mine], first.at[theirs])
        if half == 1:
            done("part0", "part1")

    def inner(turn):
        owner, half = ((core, 0), (core, 1), (peer, 0), (peer, 1))[turn]
        if turn > 1:
            got["first" + str(half)]()
        rows64 = 8 * owner + 4 * half
        block = first[pl.ds(rows64, 4)].reshape(256, 1024)

        @pl.loop(0, 4)
        def _(n):
            columns = rows_at(n, 512)
            before = dot(block, w_i[:, :, columns].reshape(1024, 512)) + inner_bias[0:1, columns]
            error = lax.erf(before * (1.0 / math.sqrt(2.0)))
            chance = 0.5 * (1.0 + error)
            bell = jnp.exp(-0.5 * before * before) * (1.0 / math.sqrt(2.0 * math.pi))
            act[pl.ds(rows64, 4), :, columns] = (before * chance).astype(LOW).reshape(4, 64, 512)
            slope[pl.ds(rows64, 4), :, columns] = (chance + before * bell).astype(LOW).reshape(4, 64, 512)

    far = 1 - p.b

    def chips_of(group):
        if group < 2:
            a = (p.a, 1 - p.a)[group]
            return [p.chip(z, a, p.b) for z in range(4)]
        return [p.chip(p.back(j), a, far) for j in ((0, 2), (p.other, p.pair))[group - 2] for a in (p.a, 1 - p.a)]

    def outer_half(group, turn):
        owner, half = ((peer, 0), (peer, 1), (core, 0), (core, 1))[turn]
        target = out_part if turn < 2 else acc
        chips = chips_of(group)
        left = jnp.concatenate([act[pl.ds(8 * owner + 4 * half, 4), :, rows_at(chip, 128)].reshape(256, 128) for chip in chips], axis=1)
        at = slice(256 * half, 256 * half + 256)
        for n in range(2):
            columns = slice(512 * n, 512 * n + 512)
            right = jnp.concatenate([w_2[chip, :, columns] for chip in chips], axis=0)
            part = dot(left, right)
            if group > 0:
                part = target[at, columns] + part
            if group == 3 and turn < 2:
                t_2[2 * half : 2 * half + 2, :, columns] = part.astype(LOW).reshape(2, 128, 512)
            else:
                target[at, columns] = part
        if group == 3 and turn < 2:
            exchange(part_name(half), t_2.at[2 * half : 2 * half + 2], t_2.at[4 + 2 * half : 6 + 2 * half])

    def outer(group):
        for turn in range(4):
            outer_half(group, turn)

    def norm_second(half):
        got[part_name(half)]()
        if half == 0:
            loads[7].wait()
        for n in (2 * half, 2 * half + 1):
            at = rows_at(n, BLOCK)
            hidden = xhat[rows_at(n, 4)].reshape(BLOCK, 1024) * param(G1) + param(S1)
            hidden = hidden + acc[at] + t_2[4 + n].astype(F32) + param(BF)
            normal, inverse = norm_of(hidden)
            given = gbuf[at].astype(F32)
            gbuf[at] = (normal * param(G2) + param(S2)).astype(LOW)
            g_part[G2] += fold(given * normal)
            g_part[S2] += fold(given)
            down = norm_back(given * param(G2), normal, inverse)
            acc[at] = down
            low = down.astype(LOW)
            g_part[BF] += fold(low.astype(F32))
            dout[tokens_of(core, n), :] = low
            exchange("dout" + str(n), dout.at[tokens_of(core, n)], dout.at[tokens_of(core, n)], dout.at[tokens_of(peer, n)])
    planes = (p.z_pair, p.back(2), p.back(p.other), p.z)

    def outer_terms(step):
        if step == 0:
            for n in range(4):
                got["dout" + str(n)]()
            done("part0", "part1")
        z = planes[step]
        for half in range(2):
            left = act[:, :, pl.ds(pl.multiple_of(512 * z + 256 * half, 256), 256)].reshape(1024, 256)
            part = dot_left_t(left, dout[...])
            t_2[pl.ds(4 * z + 2 * half, 2)] = part.astype(LOW).reshape(2, 128, 1024)

    def d_inner(n):
        columns = rows_at(n, 512)

        @pl.loop(0, 4)
        def _(s):
            rows = rows_at(s, 256)
            back = dot_right_t(dout[rows, :], w_2[pl.ds(4 * n, 4)].reshape(512, 1024))
            bent = slope[pl.ds(4 * s, 4), :, columns].reshape(256, 512).astype(F32)
            low = (back * bent).astype(LOW)
            act[pl.ds(4 * s, 4), :, columns] = low.reshape(4, 64, 512)
            i_part[:, columns] += fold(low.astype(F32))

    def inner_terms(step):
        z = planes[step]
        for n in range(4):
            columns = slice(512 * n, 512 * n + 512)
            left = first[:, :, :, pl.ds(pl.multiple_of(256 * z, 256), 256)].reshape(1024, 256)
            part = dot_left_t(left, act[:, :, columns].reshape(1024, 512))
            t_i[pl.ds(4 * z, 4), :, columns] = part.astype(LOW).reshape(4, 64, 512)

    def d_first(turn):
        owner, half = ((peer, 0), (peer, 1), (core, 0), (core, 1))[turn]
        at = slice(256 * half, 256 * half + 256)
        for n in range(4):
            part = dot_right_t(act[pl.ds(8 * owner + 4 * half, 4)].reshape(256, 2048), w_i[4 * n : 4 * n + 4].reshape(256, 2048))
            columns = slice(256 * n, 256 * n + 256)
            if turn < 2:
                out_part[at, columns] = part
            else:
                acc[at, columns] += part
        if turn < 2:
            pass_part(half)
        if turn == 3:
            gather_i.finish()
            p.signal_peers(ready_sem)

    def norm_first_back(half):
        if half == 0:
            done("dout0", "dout1", "dout2", "dout3")
        got[part_name(half)]()

        @pl.loop(2 * half, 2 * half + 2)
        def _(n):
            at = rows_at(n, BLOCK)
            normal = xhat[rows_at(n, 4)].reshape(BLOCK, 1024)
            given = acc[at] + in_part[at]
            g_part[G1] += fold(given * normal)
            g_part[S1] += fold(given)
            down = norm_back(given * param(G1), normal, scale1[at, 0:1])
            acc[at] = down
            low = down.astype(LOW)
            g_part[BO] += fold(low.astype(F32))
            dout[tokens_of(core, n), :] = low

        share("dout", dout, half)

    def output_terms():
        got["dout0"]()
        got["dout1"]()
        for half in range(2):
            part = dot_left_t(mix[:, 256 * half : 256 * half + 256], dout[...])
            part = part.astype(LOW).reshape(4, 2, 32, 1024)
            low, high = part[:, 0], part[:, 1]
            mine, theirs = jnp.where(core == 0, low, high), jnp.where(core == 0, high, low)
            chips = pl.ds(8 * core + 4 * half, 4)
            for n in range(2):
                columns = slice(512 * n, 512 * n + 512)
                rows = slice(32 * n, 32 * n + 32)
                slope[chips, rows, 1536:2048] = mine[:, :, columns]
                act[4 * half : 4 * half + 4, rows, 0:512] = theirs[:, :, columns]
        last = pl.ds(1536, 512)
        exchange(
            "t",
            act.at[pl.ds(0, 8), :, pl.ds(0, 512)],
            slope.at[pl.ds(8 * core, 8), :, last],
            slope.at[pl.ds(8 * peer, 8), :, last],
        )

    def d_mixed():
        @pl.loop(0, 4)
        def _(s):
            rows = rows_at(s, 256)
            mix[rows, :] = dot_right_t(dout[rows, :], w_o[rows_at(core, 8)].reshape(512, 1024)).astype(LOW)

        got["t"]()
        pl.semaphore_wait(ready_sem, 5)

    def attention_back(turn, part):
        owner, n = turn_of(turn)
        s = 2 * owner + n
        valid = mask[owner, n : n + 1, :] > 0.5
        rows = rows_at(s, 256)

        @pl.loop(2 * part, 2 * part + 2)
        def _(t):
            query, key, value = heads_of(s, t)
            columns = rows_at(t, 128)
            d_mix = mix[rows, columns]
            scaled = query * scale
            d_query, d_key, d_value = [], [], []
            for q_half, m_half in zip(halves(scaled), halves(d_mix)):
                probs = softmax(q_half, key, valid)
                d_probs = dot_right_t(m_half, value)
                d_value.append(dot_left_t(probs.astype(LOW), d_mix))
                delta = jnp.sum(probs * d_probs, axis=-1, keepdims=True)
                d_scores = (probs * (d_probs - delta)).astype(LOW)
                d_query.append(dot(d_scores, key))
                d_key.append(dot_left_t(d_scores, scaled))
            low_q = (jnp.where(left_half, *d_query) * (1.0 / math.sqrt(HD))).astype(LOW)
            low_k = jnp.where(left_half, *d_key).astype(LOW)
            low_v = jnp.where(left_half, *d_value).astype(LOW)
            for n_part, low in enumerate((low_q, low_k, low_v)):
                qkv[rows, pl.ds(pl.multiple_of(512 * n_part + 128 * t, 128), 128)] = low
            here = pl.ds(pl.multiple_of(512 * core + 128 * t, 128), 128)
            g_part[BQ, :, here] += fold(low_q.astype(F32))
            g_part[BV, :, here] += fold(low_v.astype(F32))

    def query_terms(step):
        z = planes[step]
        for n in range(3):
            columns = slice(512 * n, 512 * n + 512)
            left = x_all[:, pl.ds(pl.multiple_of(256 * z, 256), 256)]
            part = dot_left_t(left, qkv[:, columns])
            slope[pl.ds(4 * z, 4), :, columns] = part.astype(LOW).reshape(4, 64, 512)

    def short_sums():
        for n in range(SHORT):
            g_sum[n : n + 1, :] = jnp.sum(g_part[n], axis=0, keepdims=True)
        exchange("g", g_sum, g_other)

    def short_terms():
        got["g"]()
        v_terms[...] = jnp.zeros_like(v_terms)
        for n in range(16):
            t = n // 2
            at = slice(128 * t, 128 * t + 128)
            v_terms[n, 0:8] = g_sum[:, at] + g_other[:, at]
            v_terms[n, 8:9] = jnp.sum(i_part[:, 128 * n : 128 * n + 128], axis=0, keepdims=True)

    def d_tokens(turn):
        owner, half = ((peer, 0), (peer, 1), (core, 0), (core, 1))[turn]
        if turn == 0:
            done("part0", "part1")
        at = slice(256 * half, 256 * half + 256)
        for n in range(4):
            part = dot_right_t(qkv[half_of(owner, half), :], w_qkv[4 * n : 4 * n + 4].reshape(256, 1536))
            columns = slice(256 * n, 256 * n + 256)
            if turn < 2:
                out_part[at, columns] = part
            else:
                acc[at, columns] += part
        if turn < 2:
            pass_part(half)

    def tokens_out():
        for half in range(2):
            got[part_name(half)]()

            @pl.loop(2 * half, 2 * half + 2)
            def _(n):
                at = rows_at(n, BLOCK)
                token_grad[at] = (acc[at] + in_part[at]).astype(LOW)

    reduce_2 = Reduce(p, lambda i: t_2.at[i], lambda k: landed_2.at[k], 32, send_sem, recv_sem, 5 * COPIES)
    reduce_i = Reduce(p, lambda i: t_i.at[i], lambda k: landed_i.at[k], 32, send_sem, recv_sem, 6 * COPIES)
    reduce_o = Reduce(p, lambda i: slope.at[i, :, pl.ds(1536, 512)], lambda k: w_i.at[k, :, pl.ds(1536, 512)], 32, send_sem, recv_sem, 7 * COPIES)
    reduce_q = Reduce(
        p,
        lambda i: slope.at[i, :, pl.ds(0, 1536)],
        lambda k: w_i.at[k, :, pl.ds(0, 1536)],
        32,
        send_sem,
        recv_sem,
        8 * COPIES,
    )
    reduce_v = Reduce(p, lambda i: v_terms.at[i], lambda k: v_landed.at[k], 16, send_sem, recv_sem, 9 * COPIES)

    def result_2():
        def put(n, total):
            f_2[rows_at(n, 32)] = total

        reduce_2.result(put)

    def halves_to(first_block):
        def put(n, total):
            xhat[first_block + 2 * n] = total[:, :1024]
            xhat[first_block + 2 * n + 1, :, : total.shape[1] - 1024] = total[:, 1024:]

        return put

    def column(block, n):
        return xhat[block + n // 8, :, 128 * (n % 8) : 128 * (n % 8) + 128]

    def result_i():
        reduce_i.result(halves_to(0))
        exchange("i", xhat.at[pl.ds(2 * peer, 2)], xhat.at[4:6])

    def result_i_out():
        got["i"]()
        for n in range(16):
            f_i[:, rows_at(2 * n + core, 128)] = column(2 * core, n)
            f_i[:, rows_at(2 * n + peer, 128)] = column(4, n)

    def result_o():
        def put(n, total):
            f_s[3][:, rows_at(n, 512)] = total

        reduce_o.result(put)

    def result_v():
        def put(n, total):
            group = 2 * lax.rem(me, 2) + core
            turned = total
            for n_group in (1, 2, 3):
                turned = jnp.where(group == n_group, pltpu.roll(total, 128 - 32 * n_group, 1), turned)
            is_short = lax.broadcasted_iota(jnp.int32, (16, 128), 0) < SHORT
            vec_grad[...] = jnp.where(is_short, turned, total)

        reduce_v.result(put)

    def result_q():
        reduce_q.result(halves_to(8))
        exchange("q", xhat.at[pl.ds(8 + 2 * peer, 2)], xhat.at[12:14])

    def result_q_out():
        got["q"]()
        for n in range(3):
            for owner, block in ((core, 8 + 2 * core), (peer, 12)):
                f_s[n][:, rows_at(owner, 512)] = xhat[block + n // 2, :, 512 * (n % 2) : 512 * (n % 2) + 512]

    gather_v.run(B1, P0)
    gather_o.run(A2)
    gather_i.run(A0)
    gather_q.run(B1)
    gather_o.run(B1)
    gather_i.run(B0)
    gather_q.run(P0)
    gather_o.run(P0, P1)
    gather_q.run(A2)
    gather_i.run(B1)
    gather_q.run(Ap)
    gather_v.run(A2)
    gather_q.run(P1)
    gather_v.run(P1, Ap)
    gather_q.run(B2)
    gather_i.run(Z1, Z2)
    gather_v.run(Ao, B3)
    gather_i.run(Z3)
    gather_o.run(Ap)
    gather_q.run(B3)
    gather_o.run(Ao)
    gather_q.run(Ao)
    gather_v.run(E1)
    gather_i.run(P1)
    gather_v.run(B4)
    gather_o.run(B2)
    gather_q.run(B4)
    gather_o.run(B4, E1)
    gather_2.run(Z2)
    gather_q.run(E2)
    gather_v.run(B2)
    gather_q.run(E1)
    gather_o.run(B3)
    gather_v.run(B5)
    gather_q.run(B5)
    gather_i.run(P0)
    gather_v.run(E2)
    gather_o.run(B5, E2)
    gather_2.run(Z1)
    gather_i.run(A2, B2)
    gather_2.run(Z3)
    gather_v.run(E3)
    gather_o.run(E3)
    gather_q.run(E3)
    relay_output()
    gather_2.run(B1)
    short_params()
    gather_i.run(Ao)
    project(1)
    gather_i.run(B3)
    project(0)
    attention(0, 0)
    gather_i.run(B4)
    attention(0, 1)
    branch(0)
    attention(1, 0)
    gather_2.run(A2)
    attention(1, 1)
    gather_i.run(B5)
    branch(1)
    attention(2, 0)
    gather_2.run(B2)
    gather_i.run(Ap)
    attention(2, 1)
    branch(2)
    attention(3, 0)
    attention(3, 1)
    gather_2.run(P1, B3)
    gather_i.run(E3)
    branch(3)
    norm_first(0)
    norm_first(1)
    gather_2.run(P0)
    gather_i.run(E2)
    gather_2.run(Ao)
    gather_i.run(E1)
    inner(0)
    gather_2.run(B4)
    inner(1)
    gather_2.run(Ap)
    inner(2)
    inner(3)
    gather_2.run(B5)
    outer(0)
    gather_2.run(E2, E1)
    outer(1)
    outer(2)
    gather_2.run(E3)
    outer(3)
    norm_second(0)
    norm_second(1)
    outer_terms(0)
    reduce_2.run(Ap)
    outer_terms(1)
    reduce_2.run(P0)
    outer_terms(2)
    reduce_2.run(P1, B5)
    outer_terms(3)
    reduce_2.run(B3, B4, B2)
    d_inner(0)
    d_inner(1)
    d_inner(2)
    d_inner(3)
    inner_terms(0)
    reduce_i.run(P0)
    reduce_2.run(A2)
    inner_terms(1)
    reduce_2.run(Ao)
    reduce_i.run(P1)
    inner_terms(2)
    inner_terms(3)
    reduce_i.run(B5)
    reduce_2.run(B1)
    d_first(0)
    reduce_2.run(Z2)
    reduce_i.run(B3)
    d_first(1)
    d_first(2)
    reduce_2.run(Zo)
    reduce_i.run(B4)
    d_first(3)
    norm_first_back(0)
    norm_first_back(1)
    reduce_i.run(Ao, B0, Ap, B2)
    reduce_2.run(Zp, A0)
    reduce_i.run(B1)
    output_terms()
    reduce_2.run(B0)
    reduce_i.run(A2)
    d_mixed()
    reduce_o.run(P1)
    attention_back(0, 0)
    attention_back(0, 1)
    reduce_i.run(Zo)
    attention_back(1, 0)
    reduce_o.run(P0)
    attention_back(1, 1)
    reduce_o.run(B3)
    attention_back(2, 0)
    reduce_i.run(Zp)
    reduce_o.run(B1, B4)
    attention_back(2, 1)
    reduce_o.run(B5)
    reduce_i.run(Z2)
    attention_back(3, 0)
    reduce_i.run(A0)
    reduce_o.run(B2)
    attention_back(3, 1)
    query_terms(0)
    reduce_q.run(P0)
    reduce_o.run(A2)
    query_terms(1)
    reduce_o.run(Ao, A0)
    query_terms(2)
    reduce_q.run(B5)
    reduce_o.run(Z2)
    query_terms(3)
    reduce_q.run(B4)
    reduce_o.run(Zo)
    d_tokens(0)
    reduce_q.run(Ao)
    result_2()
    reduce_q.run(Ap)
    d_tokens(1)
    reduce_q.run(P1)
    d_tokens(2)
    d_tokens(3)
    reduce_q.run(Zo, B3, B2)
    short_sums()
    short_terms()
    reduce_v.run(P1)
    reduce_q.run(A2)
    reduce_v.run(P0, B5)
    reduce_q.run(Zp)
    reduce_o.run(Ap)
    reduce_v.run(B2, B3, Ao)
    reduce_q.run(B1, Z2)
    reduce_v.run(B4, Ap, B1)
    reduce_q.run(B0)
    reduce_o.run(Zp)
    result_i()
    reduce_v.run(Zo, Zp, A2)
    reduce_q.run(A0)
    reduce_v.run(Z2)
    result_i_out()
    tokens_out()
    reduce_v.run(A0, B0)
    reduce_o.run(B0)
    result_q()
    result_o()
    result_v()
    result_q_out()

    for each in (gather_q, gather_o, gather_i, gather_2, gather_v):
        each.finish()
    for each in (reduce_q, reduce_o, reduce_i, reduce_2, reduce_v):
        each.finish()
    for each in pending + list(sent.values()):
        each()


def layer(*arrays):
    def low(*shape):
        return pltpu.VMEM(shape, LOW)

    def full(*shape):
        return pltpu.VMEM(shape, F32)

    hbm = pl.BlockSpec(memory_space=pl.ANY)
    vmem = pl.BlockSpec(memory_space=pltpu.VMEM)
    smem = pl.BlockSpec(memory_space=pltpu.SMEM)
    scratch = [
        low(1024, 1024),
        low(1024, 1536),
        low(1024, 512),
        full(512, 1024),
        full(512, 1024),
        full(512, 1024),
        full(16, 32, 1024),
        full(512, 128),
        low(16, 2, 32, 1024),
        low(16, 64, 2048),
        low(16, 64, 2048),
        low(1024, 1024),
        low(16, 64, 1536),
        low(16, 2, 32, 1024),
        low(16, 64, 2048),
        low(16, 128, 1024),
        low(16, 128, 1024),
        low(16, 64, 2048),
        low(COPIES, 128, 1024),
        low(COPIES, 64, 2048),
        low(32, 1536),
        low(32, 2048),
        full(2, 8, 256),
        low(2, 16, 16, 128),
        full(16, 1024),
        full(8, 2048),
        full(SHORT, 8, 1024),
        full(8, 2048),
        full(8, 1024),
        full(8, 1024),
        full(16, 16, 128),
        full(COPIES, 16, 128),
        full(16, 128),
        pltpu.SemaphoreType.DMA((19,)),
        pltpu.SemaphoreType.DMA((26,)),
        pltpu.SemaphoreType.DMA((26,)),
        pltpu.SemaphoreType.DMA((10 * COPIES,)),
        pltpu.SemaphoreType.DMA((10 * COPIES,)),
        pltpu.SemaphoreType.REGULAR,
    ] + [full(1, 32)] * SHORT + [full(1, 128)]
    shape = jax.ShapeDtypeStruct
    return pl.pallas_call(
        layer_kernel,
        out_shape=(
            pltpu.VMEM((512, 1024), LOW),
            pltpu.VMEM((512, 1024), LOW),
            pltpu.VMEM((32, 1024), F32),
            pltpu.VMEM((32, 1024), F32),
            pltpu.VMEM((32, 1024), F32),
            pltpu.VMEM((32, 1024), F32),
            pltpu.VMEM((32, 4096), F32),
            pltpu.VMEM((128, 1024), F32),
            pltpu.VMEM((16, 128), F32),
        ),
        in_specs=[hbm, smem] + [hbm] * (7 + SHORT + 1),
        out_specs=(vmem,) * 9,
        scratch_shapes=scratch,
        compiler_params=pltpu.CompilerParams(
            collective_id=0, has_side_effects=True, vmem_limit_bytes=VMEM_BYTES
        ),
        cost_estimate=pl.CostEstimate(flops=40_000_000_000, bytes_accessed=8 << 20, transcendentals=0),
    )(*arrays)


VMEM_BYTES = 60 << 20


def hand_over_kernel(*refs):
    sources, vec, targets, parts, sems = refs[:8], refs[8], refs[9:17], refs[17 : 17 + SHORT + 1], refs[-1]
    stores = [pltpu.make_async_copy(sources[n], targets[n], sems.at[n]) for n in range(8)]
    for store in stores:
        store.start()
    for n in range(SHORT):
        parts[n][...] = vec[n : n + 1, 0:32]
    parts[SHORT][...] = vec[SHORT : SHORT + 1, :]
    for store in stores:
        store.wait()


def hand_over(*results):
    hbm = pl.BlockSpec(memory_space=pl.ANY)
    vmem = pl.BlockSpec(memory_space=pltpu.VMEM)
    shape = jax.ShapeDtypeStruct
    return pl.pallas_call(
        hand_over_kernel,
        out_shape=tuple(shape(each.shape, each.dtype) for each in results[:8])
        + (shape((1, 32), F32),) * SHORT
        + (shape((1, 128), F32),),
        in_specs=[vmem] * 9,
        out_specs=(hbm,) * 8 + (vmem,) * (SHORT + 1),
        scratch_shapes=[pltpu.SemaphoreType.DMA((8,))],
        compiler_params=pltpu.CompilerParams(vmem_limit_bytes=8 << 20),
    )(*results)


def one_kernel_device(
    tokens,
    lengths,
    cotangent,
    query_weight,
    key_weight,
    value_weight,
    output_weight,
    query_bias,
    value_bias,
    output_bias,
    first_gain,
    first_shift,
    inner_weight,
    inner_bias,
    outer_weight,
    outer_bias,
    second_gain,
    second_shift,
):
    count, seq, width = tokens.shape
    rows = count * seq
    short = (query_bias, value_bias, output_bias, first_gain, first_shift, outer_bias, second_gain, second_shift)
    outs = layer(
        tokens.reshape(rows, width),
        lengths,
        cotangent.reshape(rows, width),
        query_weight,
        key_weight,
        value_weight,
        output_weight,
        inner_weight,
        outer_weight,
        *[each.reshape(1, -1) for each in short + (inner_bias,)],
    )
    outs = hand_over(*outs)
    layer_rows, token_grad, query_g, key_g, value_g, output_g, inner_g, outer_g, *part = outs
    part = [each.reshape(-1) for each in part]
    return (
        layer_rows.reshape(count, seq, width),
        token_grad.reshape(count, seq, width),
        query_g,
        key_g,
        value_g,
        output_g,
        part[BQ],
        part[BV],
        part[BO],
        part[G1],
        part[S1],
        inner_g,
        part[SHORT],
        outer_g,
        part[BF],
        part[G2],
        part[S2],
    )


epsilon = 1e-12


def normalize(hidden, gain, shift):
    center = hidden - jnp.mean(hidden, axis=-1, keepdims=True)
    spread = jnp.mean(center * center, axis=-1, keepdims=True)
    return center * lax.rsqrt(spread + epsilon) * gain + shift


def gelu_exact(inner):
    return jax.nn.gelu(inner, approximate=False)


def matmul(left, right):
    return jnp.dot(left, right, preferred_element_type=jnp.float32)


def matmul_left_t(left, right):
    return lax.dot_general(
        left, right, (((0,), (0,)), ((), ())), preferred_element_type=jnp.float32
    )


def matmul_right_t(left, right):
    return lax.dot_general(
        left, right, (((1,), (1,)), ((), ())), preferred_element_type=jnp.float32
    )


def row_sum(values):
    return jnp.sum(values.astype(jnp.float32), axis=0)


def per_device(
    tokens,
    lengths,
    cotangent,
    query_weight,
    key_weight,
    value_weight,
    output_weight,
    query_bias,
    value_bias,
    output_bias,
    first_gain,
    first_shift,
    inner_weight,
    inner_bias,
    outer_weight,
    outer_bias,
    second_gain,
    second_shift,
):
    attn_master = (
        query_weight,
        key_weight,
        value_weight,
        output_weight,
        query_bias,
        value_bias,
        output_bias,
        first_gain,
        first_shift,
    )
    ffn_master = (inner_weight, inner_bias, outer_weight, outer_bias, second_gain, second_shift)
    attn_half = [param.astype(jnp.bfloat16) for param in attn_master]
    ffn_half = [param.astype(jnp.bfloat16) for param in ffn_master]
    micro_count, rows, width = tokens.shape
    heads = width // HD
    owners = lax.axis_size(("dp", "fsdp"))
    scale = 1.0 / math.sqrt(HD)
    positions = jnp.arange(rows, dtype=jnp.int32)
    attn_totals = [
        jnp.zeros((param.shape[0] * owners,) + param.shape[1:], jnp.float32)
        for param in attn_master
    ]
    ffn_totals = [
        jnp.zeros((param.shape[0] * owners,) + param.shape[1:], jnp.float32) for param in ffn_master
    ]
    outputs_list = []
    token_grads_list = []
    for micro in range(micro_count):
        token_rows = tokens[micro]
        cot_rows = cotangent[micro].astype(jnp.float32)
        valid_keys = positions < lengths[micro]
        attn_full = (
            lax.all_gather(attn_half[0], ("dp", "fsdp"), axis=0, tiled=True),
            lax.all_gather(attn_half[1], ("dp", "fsdp"), axis=0, tiled=True),
            lax.all_gather(attn_half[2], ("dp", "fsdp"), axis=0, tiled=True),
            lax.all_gather(attn_half[3], ("dp", "fsdp"), axis=0, tiled=True),
            lax.all_gather(attn_half[4], ("dp", "fsdp"), axis=0, tiled=True),
            lax.all_gather(attn_half[5], ("dp", "fsdp"), axis=0, tiled=True),
            lax.all_gather(attn_half[6], ("dp", "fsdp"), axis=0, tiled=True),
            lax.all_gather(attn_half[7], ("dp", "fsdp"), axis=0, tiled=True),
            lax.all_gather(attn_half[8], ("dp", "fsdp"), axis=0, tiled=True),
        )
        query_use, key_use, value_use, output_use = (
            attn_full[0],
            attn_full[1],
            attn_full[2],
            attn_full[3],
        )
        bias_query = attn_full[4].astype(jnp.float32)
        bias_value = attn_full[5].astype(jnp.float32)
        bias_output = attn_full[6].astype(jnp.float32)
        gain_first = attn_full[7].astype(jnp.float32)
        shift_first = attn_full[8].astype(jnp.float32)
        query_rows = (matmul(token_rows, query_use) + bias_query).astype(jnp.bfloat16)
        key_rows = matmul(token_rows, key_use).astype(jnp.bfloat16)
        value_rows = (matmul(token_rows, value_use) + bias_value).astype(jnp.bfloat16)
        query_heads = query_rows.reshape(rows, heads, HD)
        key_heads = key_rows.reshape(rows, heads, HD)
        value_heads = value_rows.reshape(rows, heads, HD)

        def attention_scores():
            raw_scores = (
                jnp.einsum(
                    "qhd,khd->hqk", query_heads, key_heads, preferred_element_type=jnp.float32
                )
                * scale
            )
            return jnp.where(valid_keys[None, None, :], raw_scores, -1000000000.0)

        scores = attention_scores()
        peak = jnp.max(scores, axis=-1, keepdims=True)
        log_total = peak + jnp.log(jnp.sum(jnp.exp(scores - peak), axis=-1, keepdims=True))
        probs_low = jnp.exp(scores - log_total).astype(jnp.bfloat16)
        mixed = (
            jnp.einsum("hqk,khd->qhd", probs_low, value_heads, preferred_element_type=jnp.float32)
            .reshape(rows, width)
            .astype(jnp.bfloat16)
        )
        residual = token_rows.astype(jnp.float32) + matmul(mixed, output_use) + bias_output
        first = normalize(residual, gain_first, shift_first)
        first_low = first.astype(jnp.bfloat16)
        ffn_full = (
            lax.all_gather(ffn_half[0], ("dp", "fsdp"), axis=0, tiled=True),
            lax.all_gather(ffn_half[1], ("dp", "fsdp"), axis=0, tiled=True),
            lax.all_gather(ffn_half[2], ("dp", "fsdp"), axis=0, tiled=True),
            lax.all_gather(ffn_half[3], ("dp", "fsdp"), axis=0, tiled=True),
            lax.all_gather(ffn_half[4], ("dp", "fsdp"), axis=0, tiled=True),
            lax.all_gather(ffn_half[5], ("dp", "fsdp"), axis=0, tiled=True),
        )
        inner = matmul(first_low, ffn_full[0]) + ffn_full[1].astype(jnp.float32)
        active = gelu_exact(inner).astype(jnp.bfloat16)
        second_in = first + matmul(active, ffn_full[2]) + ffn_full[3].astype(jnp.float32)
        gain_second = ffn_full[4].astype(jnp.float32)
        shift_second = ffn_full[5].astype(jnp.float32)
        layer_rows, pull_second = jax.vjp(normalize, second_in, gain_second, shift_second)
        outputs_list.append(layer_rows.astype(jnp.bfloat16))
        ffn_full = (
            lax.all_gather(ffn_half[0], ("dp", "fsdp"), axis=0, tiled=True),
            lax.all_gather(ffn_half[1], ("dp", "fsdp"), axis=0, tiled=True),
            lax.all_gather(ffn_half[2], ("dp", "fsdp"), axis=0, tiled=True),
            lax.all_gather(ffn_half[3], ("dp", "fsdp"), axis=0, tiled=True),
            lax.all_gather(ffn_half[4], ("dp", "fsdp"), axis=0, tiled=True),
            lax.all_gather(ffn_half[5], ("dp", "fsdp"), axis=0, tiled=True),
        )
        d_second, d_gain_second, d_shift_second = pull_second(cot_rows)
        d_outer = d_second.astype(jnp.bfloat16)
        ffn_totals[2] = ffn_totals[2] + matmul_left_t(active, d_outer)
        ffn_totals[3] = ffn_totals[3] + row_sum(d_outer)
        ffn_totals[4] = ffn_totals[4] + d_gain_second
        ffn_totals[5] = ffn_totals[5] + d_shift_second
        d_active = matmul_right_t(d_outer, ffn_full[2])
        gelu_value, pull_gelu = jax.vjp(gelu_exact, inner)
        (d_inner,) = pull_gelu(d_active)
        d_inner_low = d_inner.astype(jnp.bfloat16)
        ffn_totals[0] = ffn_totals[0] + matmul_left_t(first_low, d_inner_low)
        ffn_totals[1] = ffn_totals[1] + row_sum(d_inner_low)
        d_first = matmul_right_t(d_inner_low, ffn_full[0]) + d_second
        attn_full = (
            lax.all_gather(attn_half[0], ("dp", "fsdp"), axis=0, tiled=True),
            lax.all_gather(attn_half[1], ("dp", "fsdp"), axis=0, tiled=True),
            lax.all_gather(attn_half[2], ("dp", "fsdp"), axis=0, tiled=True),
            lax.all_gather(attn_half[3], ("dp", "fsdp"), axis=0, tiled=True),
            lax.all_gather(attn_half[4], ("dp", "fsdp"), axis=0, tiled=True),
            lax.all_gather(attn_half[5], ("dp", "fsdp"), axis=0, tiled=True),
            lax.all_gather(attn_half[6], ("dp", "fsdp"), axis=0, tiled=True),
            lax.all_gather(attn_half[7], ("dp", "fsdp"), axis=0, tiled=True),
            lax.all_gather(attn_half[8], ("dp", "fsdp"), axis=0, tiled=True),
        )
        query_use, key_use, value_use, output_use = (
            attn_full[0],
            attn_full[1],
            attn_full[2],
            attn_full[3],
        )
        norm_value, pull_first = jax.vjp(
            normalize, residual, attn_full[7].astype(jnp.float32), attn_full[8].astype(jnp.float32)
        )
        d_residual, d_gain_first, d_shift_first = pull_first(d_first)
        attn_totals[7] = attn_totals[7] + d_gain_first
        attn_totals[8] = attn_totals[8] + d_shift_first
        d_branch = d_residual.astype(jnp.bfloat16)
        attn_totals[3] = attn_totals[3] + matmul_left_t(mixed, d_branch)
        attn_totals[6] = attn_totals[6] + row_sum(d_branch)
        d_mixed = matmul_right_t(d_branch, output_use).astype(jnp.bfloat16).reshape(rows, heads, HD)
        scores = attention_scores()
        probs = jnp.exp(scores - log_total)
        probs_low = probs.astype(jnp.bfloat16)
        d_probs = jnp.einsum(
            "qhd,khd->hqk", d_mixed, value_heads, preferred_element_type=jnp.float32
        )
        d_values = jnp.einsum(
            "hqk,qhd->khd", probs_low, d_mixed, preferred_element_type=jnp.float32
        ).reshape(rows, width)
        delta_rows = jnp.sum(probs * d_probs, axis=-1, keepdims=True)
        d_scores = (probs * (d_probs - delta_rows)).astype(jnp.bfloat16)
        d_queries = (
            (
                jnp.einsum("hqk,khd->qhd", d_scores, key_heads, preferred_element_type=jnp.float32)
                * scale
            )
            .reshape(rows, width)
            .astype(jnp.bfloat16)
        )
        d_keys = (
            jnp.einsum(
                "hqk,qhd->khd", d_scores, query_heads, preferred_element_type=jnp.float32
            ).reshape(rows, width)
            * scale
        )
        key_low = d_keys.astype(jnp.bfloat16)
        value_low = d_values.astype(jnp.bfloat16)
        attn_totals[0] = attn_totals[0] + matmul_left_t(token_rows, d_queries)
        attn_totals[1] = attn_totals[1] + matmul_left_t(token_rows, key_low)
        attn_totals[2] = attn_totals[2] + matmul_left_t(token_rows, value_low)
        attn_totals[4] = attn_totals[4] + row_sum(d_queries)
        attn_totals[5] = attn_totals[5] + row_sum(value_low)
        token_grad = (
            d_residual
            + matmul_right_t(d_queries, query_use)
            + matmul_right_t(key_low, key_use)
            + matmul_right_t(value_low, value_use)
        )
        token_grads_list.append(token_grad.astype(jnp.bfloat16))
    attn_shards = (
        lax.psum_scatter(attn_totals[0], ("dp", "fsdp"), scatter_dimension=0, tiled=True),
        lax.psum_scatter(attn_totals[1], ("dp", "fsdp"), scatter_dimension=0, tiled=True),
        lax.psum_scatter(attn_totals[2], ("dp", "fsdp"), scatter_dimension=0, tiled=True),
        lax.psum_scatter(attn_totals[3], ("dp", "fsdp"), scatter_dimension=0, tiled=True),
        lax.psum_scatter(attn_totals[4], ("dp", "fsdp"), scatter_dimension=0, tiled=True),
        lax.psum_scatter(attn_totals[5], ("dp", "fsdp"), scatter_dimension=0, tiled=True),
        lax.psum_scatter(attn_totals[6], ("dp", "fsdp"), scatter_dimension=0, tiled=True),
        lax.psum_scatter(attn_totals[7], ("dp", "fsdp"), scatter_dimension=0, tiled=True),
        lax.psum_scatter(attn_totals[8], ("dp", "fsdp"), scatter_dimension=0, tiled=True),
    )
    ffn_shards = (
        lax.psum_scatter(ffn_totals[0], ("dp", "fsdp"), scatter_dimension=0, tiled=True),
        lax.psum_scatter(ffn_totals[1], ("dp", "fsdp"), scatter_dimension=0, tiled=True),
        lax.psum_scatter(ffn_totals[2], ("dp", "fsdp"), scatter_dimension=0, tiled=True),
        lax.psum_scatter(ffn_totals[3], ("dp", "fsdp"), scatter_dimension=0, tiled=True),
        lax.psum_scatter(ffn_totals[4], ("dp", "fsdp"), scatter_dimension=0, tiled=True),
        lax.psum_scatter(ffn_totals[5], ("dp", "fsdp"), scatter_dimension=0, tiled=True),
    )
    return (
        jnp.stack(outputs_list),
        jnp.stack(token_grads_list),
        attn_shards[0],
        attn_shards[1],
        attn_shards[2],
        attn_shards[3],
        attn_shards[4],
        attn_shards[5],
        attn_shards[6],
        attn_shards[7],
        attn_shards[8],
        ffn_shards[0],
        ffn_shards[1],
        ffn_shards[2],
        ffn_shards[3],
        ffn_shards[4],
        ffn_shards[5],
    )


def solution(mesh):
    in_specs = (
        P(("dp", "fsdp"), None, None),
        P(("dp", "fsdp")),
        P(("dp", "fsdp"), None, None),
        P(("dp", "fsdp"), None),
        P(("dp", "fsdp"), None),
        P(("dp", "fsdp"), None),
        P(("dp", "fsdp"), None),
        P(("dp", "fsdp")),
        P(("dp", "fsdp")),
        P(("dp", "fsdp")),
        P(("dp", "fsdp")),
        P(("dp", "fsdp")),
        P(("dp", "fsdp"), None),
        P(("dp", "fsdp")),
        P(("dp", "fsdp"), None),
        P(("dp", "fsdp")),
        P(("dp", "fsdp")),
        P(("dp", "fsdp")),
    )
    out_specs = (
        P(("dp", "fsdp"), None, None),
        P(("dp", "fsdp"), None, None),
        P(("dp", "fsdp"), None),
        P(("dp", "fsdp"), None),
        P(("dp", "fsdp"), None),
        P(("dp", "fsdp"), None),
        P(("dp", "fsdp")),
        P(("dp", "fsdp")),
        P(("dp", "fsdp")),
        P(("dp", "fsdp")),
        P(("dp", "fsdp")),
        P(("dp", "fsdp"), None),
        P(("dp", "fsdp")),
        P(("dp", "fsdp"), None),
        P(("dp", "fsdp")),
        P(("dp", "fsdp")),
        P(("dp", "fsdp")),
    )
    one_kernel = dict(mesh.shape) == {"dp": 16, "fsdp": 2}
    device = one_kernel_device if one_kernel else per_device
    return jax.shard_map(
        device, mesh=mesh, in_specs=in_specs, out_specs=out_specs, check_vma=False
    )
```

```python
import functools
import math

import jax
import jax.numpy as jnp
from jax import lax
from jax.experimental import pallas as pl
from jax.experimental.pallas import tpu as pltpu
from jax.sharding import PartitionSpec as P

MESH = pl.DeviceIdType.MESH
COPIES = 15
HD = 64
LOW = jnp.bfloat16
F32 = jnp.float32


class Place:
    def __init__(self):
        self.me = lax.axis_index("dp")
        self.core = lax.axis_index("fsdp")
        x, y, self.z = lax.rem(self.me, 2), lax.rem(self.me // 2, 2), self.me // 4
        self.a = x + self.core * (y - x)
        self.b = y + self.core * (x - y)
        odd = lax.rem(self.z, 2)
        self.pair, self.other = 3 - 2 * odd, 1 + 2 * odd
        self.z_pair = self.z + 1 - 2 * odd

    def chip(self, z, a, b):
        return z * 4 + (b + self.core * (a - b)) * 2 + (a + self.core * (b - a))

    def back(self, j):
        return lax.rem(self.z - j + 4, 4)

    def peers(self):
        along_z = [self.chip(lax.rem(self.z + k, 4), self.a, self.b) for k in (1, 2, 3)]
        return along_z + [self.chip(self.z, 1 - self.a, self.b), self.chip(self.z, self.a, 1 - self.b)]

    def signal_peers(self, sem):
        for chip in self.peers():
            pl.semaphore_signal(sem, inc=1, device_id=(chip, self.core), device_id_type=MESH)

    def announce(self):
        sem = pltpu.get_barrier_semaphore()
        self.signal_peers(sem)
        pl.semaphore_signal(sem, inc=1, device_id=(self.me, 1 - self.core), device_id_type=MESH)

    def meet(self):
        pl.semaphore_wait(pltpu.get_barrier_semaphore(), 6)


class Hops:
    def __init__(self, place, send_sem, recv_sem, base):
        self.place, self.send_sem, self.recv_sem, self.base = place, send_sem, recv_sem, base
        self.started = []

    def send(self, k, source, target, chip):
        copy = pltpu.make_async_remote_copy(
            src_ref=source,
            dst_ref=target,
            send_sem=self.send_sem.at[self.base + k],
            recv_sem=self.recv_sem.at[self.base + k],
            device_id=(chip, self.place.core),
            device_id_type=MESH,
        )
        copy.start()
        self.started.append(copy)

    def arrived(self, k, block):
        pltpu.make_async_remote_copy(
            src_ref=block,
            dst_ref=block,
            send_sem=self.send_sem.at[self.base + k],
            recv_sem=self.recv_sem.at[self.base + k],
            device_id=(self.place.me, self.place.core),
            device_id_type=MESH,
        ).wait_recv()

    def finish(self):
        for copy in self.started:
            copy.wait_send()
        self.started = []


class Gather(Hops):
    def __init__(self, place, held, *rest):
        super().__init__(place, *rest)
        self.held = held

    def pass_on(self, k, block, chip):
        self.send(k, self.held.at[block], self.held.at[block], chip)

    def wait(self, *copies):
        for k in copies:
            self.arrived(k, self.held.at[self.place.me])

    def run(self, *hops):
        for hop in hops:
            self.take(hop)

    def take(self, name):
        p = self.place
        kind, which = name
        which = {PAIR: p.pair, OTHER: p.other}.get(which, which)
        if kind == Z:
            self.pass_on(which - 1, p.me, p.chip(lax.rem(p.z + which, 4), p.a, p.b))
        elif kind == A:
            if name != A0:
                self.wait(which - 1)
            self.pass_on(3 + which, p.chip(p.back(which), p.a, p.b), p.chip(p.z, 1 - p.a, p.b))
        elif kind == B:
            j = (0, 0, 2, 2, p.other, p.other)[which]
            if which % 2:
                self.wait(3 + j)
            block = p.chip(p.back(j), (p.a, 1 - p.a)[which % 2], p.b)
            self.pass_on(7 + which, block, p.chip(p.z, p.a, 1 - p.b))
        elif kind == P_:
            self.wait(7 + which)
            block = p.chip(p.z, (p.a, 1 - p.a)[which], 1 - p.b)
            self.pass_on(13 + which, block, p.chip(p.z_pair, p.a, p.b))
        else:
            self.wait(*((), (3 + p.pair,), (9, 10), (11, 12, 13, 14))[which])


class Reduce(Hops):
    def __init__(self, place, terms, landed, chunk, *rest):
        super().__init__(place, *rest)
        self.terms, self.landed, self.chunk = terms, landed, chunk

    def sum_into(self, block, ks, store):
        for k in ks:
            self.arrived(k, self.landed(k))
        term = self.terms(block)
        landed = [self.landed(k) for k in ks]
        rows = term.shape[0]

        def some(n):
            at = rows_at(n, self.chunk)
            total = term[at].astype(F32)
            for each in landed:
                total += each[at].astype(F32)
            store(n, total)

        if rows == self.chunk:
            some(0)
        else:
            pl.loop(0, rows // self.chunk)(some)

    def add_and_send(self, k, block, ks, chip):
        term = self.terms(block)
        if ks:

            def store(n, total):
                term[rows_at(n, self.chunk)] = total.astype(term.dtype)

            self.sum_into(block, ks, store)
        self.send(k, term, self.landed(k), chip)

    def run(self, *hops):
        for hop in hops:
            self.take(hop)

    def take(self, name):
        p = self.place
        kind, which = name
        which = {PAIR: p.pair, OTHER: p.other}.get(which, which)
        if kind == P_:
            block = p.chip(p.z_pair, (p.a, 1 - p.a)[which], 1 - p.b)
            self.add_and_send(13 + which, block, (), p.chip(p.z_pair, p.a, p.b))
        elif kind == B:
            j = (0, 0, 2, 2, p.other, p.other)[which]
            block = p.chip(p.back(j), (p.a, 1 - p.a)[which % 2], 1 - p.b)
            landed = (13 + which,) if which < 2 else ()
            self.add_and_send(7 + which, block, landed, p.chip(p.z, p.a, 1 - p.b))
        elif kind == A:
            landed = {A0: (8,), A2: (10,), Ao: (12,), Ap: ()}[name]
            block = p.chip(p.back(which), 1 - p.a, p.b)
            self.add_and_send(3 + which, block, landed, p.chip(p.z, 1 - p.a, p.b))
        else:
            landed = {Z2: (9, 5), Zo: (11, 3 + p.other), Zp: (3 + p.pair,)}[name]
            owner = p.chip(p.back(which), p.a, p.b)
            self.add_and_send(3 - which, owner, landed, owner)

    def result(self, store):
        self.sum_into(self.place.me, (7, 3, 0, 1, 2), store)


class Across:
    def __init__(self, place, send_sem, recv_sem):
        self.place, self.send_sem, self.recv_sem = place, send_sem, recv_sem
        self.count = 0

    def copy(self, k, source, target):
        p = self.place
        return pltpu.make_async_remote_copy(
            src_ref=source,
            dst_ref=target,
            send_sem=self.send_sem.at[k],
            recv_sem=self.recv_sem.at[k],
            device_id=(p.me, 1 - p.core),
            device_id_type=MESH,
        )

    def send(self, source, target, here=None):
        k = self.count
        self.count += 1
        copy = self.copy(k, source, target)
        copy.start()
        landing = target if here is None else here
        return copy.wait_send, self.copy(k, landing, landing).wait_recv


def dot(left, right):
    return jnp.dot(left, right, preferred_element_type=F32)


def dot_left_t(left, right):
    return lax.dot_general(left, right, (((0,), (0,)), ((), ())), preferred_element_type=F32)


def dot_right_t(left, right):
    return lax.dot_general(left, right, (((1,), (1,)), ((), ())), preferred_element_type=F32)


def fold(values):
    rows, columns = values.shape
    return jnp.sum(values.reshape(rows // 8, 8, columns), axis=0)


def rows_at(index, size):
    if isinstance(index, int):
        return pl.ds(index * size, size)
    return pl.ds(pl.multiple_of(index * size, size), size)


Z, A, B, P_, E = range(5)
PAIR, OTHER = -1, -2
Z1, Z2, Z3, Zp, Zo = (Z, 1), (Z, 2), (Z, 3), (Z, PAIR), (Z, OTHER)
A0, A2, Ap, Ao = (A, 0), (A, 2), (A, PAIR), (A, OTHER)
B0, B1, B2, B3, B4, B5 = [(B, n) for n in range(6)]
P0, P1 = (P_, 0), (P_, 1)
E1, E2, E3 = (E, 1), (E, 2), (E, 3)
EARLY = (Z2, A0, B0, Z1, Z3)

SHORT = 8
BQ, BV, BO, G1, S1, BF, G2, S2 = range(SHORT)
EPSILON = 1e-12


def layer_kernel(
    tokens,
    lengths,
    cotangent,
    query_weight,
    key_weight,
    value_weight,
    output_weight,
    inner_weight,
    outer_weight,
    *rest,
):
    short_shards, rest = rest[: SHORT + 1], rest[SHORT + 1 :]
    layer_body(
        tokens,
        lengths,
        cotangent,
        query_weight,
        key_weight,
        value_weight,
        output_weight,
        inner_weight,
        outer_weight,
        short_shards,
        rest[-SHORT - 1 :],
        *rest[: -SHORT - 1],
    )


def layer_body(
    tokens,
    lengths,
    cotangent,
    query_weight,
    key_weight,
    value_weight,
    output_weight,
    inner_weight,
    outer_weight,
    short_shards,
    short_here,
    layer_out,
    token_grad,
    query_grad,
    key_grad,
    value_grad,
    output_grad,
    inner_grad,
    outer_grad,
    vec_grad,
    x_all,
    qkv,
    mix,
    acc,
    out_part,
    in_part,
    xhat,
    scale1,
    first,
    act,
    slope,
    dout,
    w_qkv,
    w_o,
    w_i,
    w_2,
    t_2,
    t_i,
    landed_2,
    landed_i,
    stage_q,
    stage_i,
    mask,
    vec_all,
    params,
    inner_bias,
    g_part,
    i_part,
    g_sum,
    g_other,
    v_terms,
    v_landed,
    v_stage,
    local_sem,
    core_send,
    core_recv,
    send_sem,
    recv_sem,
    ready_sem,
):
    f_s = (query_grad, key_grad, value_grad, output_grad)
    f_i, f_2, gbuf = inner_grad, outer_grad, layer_out
    p = Place()
    me, core = p.me, p.core
    peer = 1 - core
    across = Across(p, core_send, core_recv)
    pending = []

    own_rows = rows_at(core, 512)
    peer_rows = rows_at(peer, 512)

    def local(k, source, target):
        return pltpu.make_async_copy(source, target, local_sem.at[k])

    p.announce()
    loads = [
        local(0, query_weight, f_s[0]),
        local(1, key_weight, f_s[1]),
        local(2, value_weight, f_s[2]),
        local(3, output_weight, f_s[3]),
        local(4, inner_weight, f_i),
        local(5, outer_weight, f_2),
        local(6, tokens, x_all.at[own_rows]),
        local(7, cotangent, gbuf),
    ]
    short_loads = [local(10 + n, short_shards[n], short_here[n]) for n in range(SHORT + 1)]
    for copy in loads[:4] + [loads[5]] + short_loads + [loads[4]] + loads[6:]:
        copy.start()

    gather_o = Gather(p, w_o.at[:, core], send_sem, recv_sem, COPIES)
    gather_v = Gather(p, vec_all.at[core], send_sem, recv_sem, 4 * COPIES)
    gather_q = Gather(p, w_qkv, send_sem, recv_sem, 0)
    gather_i = Gather(p, w_i, send_sem, recv_sem, 2 * COPIES)
    gather_2 = Gather(p, w_2, send_sem, recv_sem, 3 * COPIES)
    for copy in loads[:4]:
        copy.wait()
    my_rows = rows_at(core, 32)
    for n in range(3):
        stage_q[:, 512 * n : 512 * n + 512] = f_s[n][:, rows_at(peer, 512)].astype(LOW)
    w_o[me, core] = f_s[3][...].astype(LOW)
    p.meet()
    sent_q, got_q = across.send(stage_q, w_qkv.at[me, my_rows], w_qkv.at[me, rows_at(peer, 32)])
    gather_o.run(*EARLY)
    for n in range(3):
        w_qkv[me, my_rows, 512 * n : 512 * n + 512] = f_s[n][:, rows_at(core, 512)].astype(LOW)
    loads[5].wait()
    w_2[me] = f_2[...].astype(LOW)
    gather_2.run(A0, B0)
    got_q()
    gather_q.run(*EARLY)
    for copy in short_loads:
        copy.wait()
    v_stage[...] = jnp.zeros_like(v_stage)
    for n in range(SHORT):
        v_stage[n : n + 1, 0:32] = short_here[n][...]
    v_stage[SHORT : SHORT + 1, :] = short_here[SHORT][...]
    piece = v_stage[...]
    four = piece + pltpu.roll(piece, 32, 1) + pltpu.roll(piece, 64, 1) + pltpu.roll(piece, 96, 1)
    is_short = lax.broadcasted_iota(jnp.int32, (16, 128), 0) < SHORT
    vec_all[core, me] = jnp.where(is_short, four, piece).astype(LOW)
    gather_v.run(*EARLY)
    loads[4].wait()
    for n in range(16):
        here, there = 2 * n + core, 2 * n + peer
        at = slice(128 * n, 128 * n + 128)
        w_i[me, my_rows, at] = f_i[:, rows_at(here, 128)].astype(LOW)
        stage_i[:, at] = f_i[:, rows_at(there, 128)].astype(LOW)
    sent_i, got_i = across.send(stage_i, w_i.at[me, my_rows], w_i.at[me, rows_at(peer, 32)])
    places = lax.broadcasted_iota(jnp.int32, (8, 256), 1)
    seq_of = lax.broadcasted_iota(jnp.int32, (8, 256), 0)
    limit = jnp.where(seq_of == 0, lengths[0], lengths[1])
    mask[core] = jnp.where(places < limit, 1.0, 0.0).astype(F32)
    sent_m, got_m = across.send(mask.at[core], mask.at[core], mask.at[peer])
    loads[6].wait()
    sent_x, got_x = across.send(x_all.at[own_rows], x_all.at[own_rows], x_all.at[peer_rows])
    g_part[...] = jnp.zeros_like(g_part)
    i_part[...] = jnp.zeros_like(i_part)
    got_i()
    pending += [sent_q, sent_m, sent_i, sent_x]
    sent, got = {}, {}

    def exchange(name, source, target, here=None):
        sent[name], got[name] = across.send(source, target, here)

    def done(*names):
        for name in names:
            sent.pop(name)()

    def relay_output():
        mine = rows_at(core, 8)
        theirs = rows_at(peer, 8)
        exchange("o", w_o.at[theirs, core], w_o.at[theirs, core], w_o.at[mine, peer])
        exchange("v", vec_all.at[core], vec_all.at[core], vec_all.at[peer])

    def short_params():
        got["v"]()
        lane_group = lax.broadcasted_iota(jnp.int32, (16, 128), 1) // 32
        for t in range(8):
            pieces = [vec_all[i % 2, 2 * t + i // 2].astype(F32) for i in range(4)]
            tile = jnp.where(
                lane_group < 2,
                jnp.where(lane_group == 0, pieces[0], pieces[1]),
                jnp.where(lane_group == 2, pieces[2], pieces[3]),
            )
            params[:, 128 * t : 128 * t + 128] = tile
        for n in range(16):
            inner_bias[:, 128 * n : 128 * n + 128] = vec_all[core, n].astype(F32)[8:16]
        got_x()
        got_m()

    def param(n):
        return params[n : n + 1, :]

    def project(turn):
        owner = (core, peer)[turn]

        @pl.loop(0, 2)
        def _(half):
            rows = rows_at(2 * owner + half, 256)
            block = x_all[rows, :]
            for n in range(3):
                part = dot(block, w_qkv[:, :, 512 * n : 512 * n + 512].reshape(1024, 512))
                if n != 1:
                    part = part + params[BQ if n == 0 else BV, rows_at(core, 512)][None, :]
                qkv[rows, 512 * n : 512 * n + 512] = part.astype(LOW)

    left_half = lax.broadcasted_iota(jnp.int32, (256, 128), 1) < HD

    def heads_of(s, t):
        rows = rows_at(s, 256)
        return [qkv[rows, pl.ds(pl.multiple_of(512 * n + 128 * t, 128), 128)] for n in range(3)]

    def softmax(query_half, key, valid):
        raw = dot_right_t(query_half, key)
        raw = jnp.where(valid, raw, -1000000000.0)
        grown = jnp.exp(raw - jnp.max(raw, axis=-1, keepdims=True))
        return grown * (1.0 / jnp.sum(grown, axis=-1, keepdims=True))

    def halves(pair):
        none = jnp.zeros_like(pair)
        return jnp.where(left_half, pair, none), jnp.where(left_half, none, pair)

    scale = jnp.array(1.0 / math.sqrt(HD), LOW)

    def turn_of(turn):
        return (peer, peer, core, core)[turn], turn % 2

    def attention(turn, part):
        owner, n = turn_of(turn)
        s = 2 * owner + n
        valid = mask[owner, n : n + 1, :] > 0.5

        @pl.loop(2 * part, 2 * part + 2)
        def _(t):
            query, key, value = heads_of(s, t)
            outs = [
                dot(softmax(half, key, valid).astype(LOW), value) for half in halves(query * scale)
            ]
            both = jnp.where(left_half, outs[0], outs[1]).astype(LOW)
            mix[rows_at(s, 256), rows_at(t, 128)] = both

    def part_name(half):
        return "part0" if half == 0 else "part1"

    def pass_part(half):
        at = slice(256 * half, 256 * half + 256)
        exchange(part_name(half), out_part.at[at], in_part.at[at])

    def branch(turn):
        owner, n = turn_of(turn)
        if turn == 0:
            got["o"]()
        out_use = w_o[rows_at(core, 8)].reshape(512, 1024)
        part = dot(mix[rows_at(2 * owner + n, 256), :], out_use)
        at = slice(256 * n, 256 * n + 256)
        if turn < 2:
            out_part[at] = part
            pass_part(n)
        else:
            acc[at] = part

    def norm_of(hidden):
        center = hidden - jnp.mean(hidden, axis=-1, keepdims=True)
        spread = jnp.mean(center * center, axis=-1, keepdims=True)
        inverse = lax.rsqrt(spread + EPSILON)
        return center * inverse, inverse

    def norm_back(grown, normal, inverse):
        along = jnp.mean(grown * normal, axis=-1, keepdims=True)
        return inverse * (grown - jnp.mean(grown, axis=-1, keepdims=True) - normal * along)

    BLOCK = 128

    def tokens_of(owner, n):
        return pl.ds(pl.multiple_of(512 * owner + BLOCK * n, BLOCK), BLOCK)

    def half_of(owner, half):
        return pl.ds(pl.multiple_of(512 * owner + 256 * half, 256), 256)

    def share(name, whole, half):
        exchange(name + str(half), whole.at[half_of(core, half)], whole.at[half_of(core, half)], whole.at[half_of(peer, half)])

    def norm_first(half):
        got[part_name(half)]()

        @pl.loop(2 * half, 2 * half + 2)
        def _(n):
            at = rows_at(n, BLOCK)
            hidden = x_all[tokens_of(core, n), :].astype(F32) + acc[at] + in_part[at] + param(BO)
            normal, inverse = norm_of(hidden)
            xhat[rows_at(n, 4)] = normal.reshape(4, 32, 1024)
            scale1[at] = jnp.broadcast_to(inverse, (BLOCK, 128))
            first[pl.ds(8 * core + 2 * n, 2)] = (normal * param(G1) + param(S1)).astype(LOW).reshape(2, 2, 32, 1024)

        mine = pl.ds(8 * core + 4 * half, 4)
        theirs = pl.ds(8 * peer + 4 * half, 4)
        exchange("first" + str(half), first.at[mine], first.at[mine], first.at[theirs])
        if half == 1:
            done("part0", "part1")

    def inner(turn):
        owner, half = ((core, 0), (core, 1), (peer, 0), (peer, 1))[turn]
        if turn > 1:
            got["first" + str(half)]()
        rows64 = 8 * owner + 4 * half
        block = first[pl.ds(rows64, 4)].reshape(256, 1024)

        @pl.loop(0, 4)
        def _(n):
            columns = rows_at(n, 512)
            before = dot(block, w_i[:, :, columns].reshape(1024, 512)) + inner_bias[0:1, columns]
            error = lax.erf(before * (1.0 / math.sqrt(2.0)))
            chance = 0.5 * (1.0 + error)
            bell = jnp.exp(-0.5 * before * before) * (1.0 / math.sqrt(2.0 * math.pi))
            act[pl.ds(rows64, 4), :, columns] = (before * chance).astype(LOW).reshape(4, 64, 512)
            slope[pl.ds(rows64, 4), :, columns] = (chance + before * bell).astype(LOW).reshape(4, 64, 512)

    far = 1 - p.b

    def chips_of(group):
        if group < 2:
            a = (p.a, 1 - p.a)[group]
            return [p.chip(z, a, p.b) for z in range(4)]
        return [p.chip(p.back(j), a, far) for j in ((0, 2), (p.other, p.pair))[group - 2] for a in (p.a, 1 - p.a)]

    def outer_half(group, turn):
        owner, half = ((peer, 0), (peer, 1), (core, 0), (core, 1))[turn]
        target = out_part if turn < 2 else acc
        chips = chips_of(group)
        left = jnp.concatenate([act[pl.ds(8 * owner + 4 * half, 4), :, rows_at(chip, 128)].reshape(256, 128) for chip in chips], axis=1)
        at = slice(256 * half, 256 * half + 256)
        for n in range(2):
            columns = slice(512 * n, 512 * n + 512)
            right = jnp.concatenate([w_2[chip, :, columns] for chip in chips], axis=0)
            part = dot(left, right)
            if group > 0:
                part = target[at, columns] + part
            if group == 3 and turn < 2:
                t_2[2 * half : 2 * half + 2, :, columns] = part.astype(LOW).reshape(2, 128, 512)
            else:
                target[at, columns] = part
        if group == 3 and turn < 2:
            exchange(part_name(half), t_2.at[2 * half : 2 * half + 2], t_2.at[4 + 2 * half : 6 + 2 * half])

    def outer(group):
        for turn in range(4):
            outer_half(group, turn)

    def norm_second(half):
        got[part_name(half)]()
        if half == 0:
            loads[7].wait()
        for n in (2 * half, 2 * half + 1):
            at = rows_at(n, BLOCK)
            hidden = xhat[rows_at(n, 4)].reshape(BLOCK, 1024) * param(G1) + param(S1)
            hidden = hidden + acc[at] + t_2[4 + n].astype(F32) + param(BF)
            normal, inverse = norm_of(hidden)
            given = gbuf[at].astype(F32)
            gbuf[at] = (normal * param(G2) + param(S2)).astype(LOW)
            g_part[G2] += fold(given * normal)
            g_part[S2] += fold(given)
            down = norm_back(given * param(G2), normal, inverse)
            acc[at] = down
            low = down.astype(LOW)
            g_part[BF] += fold(low.astype(F32))
            dout[tokens_of(core, n), :] = low
            exchange("dout" + str(n), dout.at[tokens_of(core, n)], dout.at[tokens_of(core, n)], dout.at[tokens_of(peer, n)])
    planes = (p.z_pair, p.back(2), p.back(p.other), p.z)

    def outer_terms(step, part=None):
        if step == 0 and part == 0:
            for n in range(4):
                got["dout" + str(n)]()
            done("part0", "part1")
        z = planes[step]
        y = jnp.where(core == 0, p.b, 1 - p.a)
        for half in (0, 1) if part is None else (y if part == 0 else 1 - y,):
            left = act[:, :, pl.ds(pl.multiple_of(512 * z + 256 * half, 256), 256)].reshape(1024, 256)
            block = dot_left_t(left, dout[...])
            t_2[pl.ds(4 * z + 2 * half, 2)] = block.astype(LOW).reshape(2, 128, 1024)

    def d_inner(n):
        columns = rows_at(n, 512)

        @pl.loop(0, 4)
        def _(s):
            rows = rows_at(s, 256)
            back = dot_right_t(dout[rows, :], w_2[pl.ds(4 * n, 4)].reshape(512, 1024))
            bent = slope[pl.ds(4 * s, 4), :, columns].reshape(256, 512).astype(F32)
            low = (back * bent).astype(LOW)
            act[pl.ds(4 * s, 4), :, columns] = low.reshape(4, 64, 512)
            i_part[:, columns] += fold(low.astype(F32))

    def inner_terms(step):
        z = planes[step]
        for n in range(4):
            columns = slice(512 * n, 512 * n + 512)
            left = first[:, :, :, pl.ds(pl.multiple_of(256 * z, 256), 256)].reshape(1024, 256)
            part = dot_left_t(left, act[:, :, columns].reshape(1024, 512))
            t_i[pl.ds(4 * z, 4), :, columns] = part.astype(LOW).reshape(4, 64, 512)

    def d_first(turn):
        owner, half = ((peer, 0), (peer, 1), (core, 0), (core, 1))[turn]
        at = slice(256 * half, 256 * half + 256)
        for n in range(4):
            part = dot_right_t(act[pl.ds(8 * owner + 4 * half, 4)].reshape(256, 2048), w_i[4 * n : 4 * n + 4].reshape(256, 2048))
            columns = slice(256 * n, 256 * n + 256)
            if turn < 2:
                out_part[at, columns] = part
            else:
                acc[at, columns] += part
        if turn < 2:
            pass_part(half)
        if turn == 3:
            gather_i.finish()
            p.signal_peers(ready_sem)

    def norm_first_back(half):
        if half == 0:
            done("dout0", "dout1", "dout2", "dout3")
        got[part_name(half)]()

        @pl.loop(2 * half, 2 * half + 2)
        def _(n):
            at = rows_at(n, BLOCK)
            normal = xhat[rows_at(n, 4)].reshape(BLOCK, 1024)
            given = acc[at] + in_part[at]
            g_part[G1] += fold(given * normal)
            g_part[S1] += fold(given)
            down = norm_back(given * param(G1), normal, scale1[at, 0:1])
            acc[at] = down
            low = down.astype(LOW)
            g_part[BO] += fold(low.astype(F32))
            dout[tokens_of(core, n), :] = low

        share("dout", dout, half)

    def output_terms():
        got["dout0"]()
        got["dout1"]()
        for half in range(2):
            part = dot_left_t(mix[:, 256 * half : 256 * half + 256], dout[...])
            part = part.astype(LOW).reshape(4, 2, 32, 1024)
            low, high = part[:, 0], part[:, 1]
            mine, theirs = jnp.where(core == 0, low, high), jnp.where(core == 0, high, low)
            chips = pl.ds(8 * core + 4 * half, 4)
            for n in range(2):
                columns = slice(512 * n, 512 * n + 512)
                rows = slice(32 * n, 32 * n + 32)
                slope[chips, rows, 1536:2048] = mine[:, :, columns]
                act[4 * half : 4 * half + 4, rows, 0:512] = theirs[:, :, columns]
        last = pl.ds(1536, 512)
        exchange(
            "t",
            act.at[pl.ds(0, 8), :, pl.ds(0, 512)],
            slope.at[pl.ds(8 * core, 8), :, last],
            slope.at[pl.ds(8 * peer, 8), :, last],
        )

    def d_mixed():
        @pl.loop(0, 4)
        def _(s):
            rows = rows_at(s, 256)
            mix[rows, :] = dot_right_t(dout[rows, :], w_o[rows_at(core, 8)].reshape(512, 1024)).astype(LOW)

        got["t"]()
        pl.semaphore_wait(ready_sem, 5)

    def attention_back(turn, part):
        owner, n = turn_of(turn)
        s = 2 * owner + n
        valid = mask[owner, n : n + 1, :] > 0.5
        rows = rows_at(s, 256)

        @pl.loop(2 * part, 2 * part + 2)
        def _(t):
            query, key, value = heads_of(s, t)
            columns = rows_at(t, 128)
            d_mix = mix[rows, columns]
            scaled = query * scale
            d_query, d_key, d_value = [], [], []
            for q_half, m_half in zip(halves(scaled), halves(d_mix)):
                probs = softmax(q_half, key, valid)
                d_probs = dot_right_t(m_half, value)
                d_value.append(dot_left_t(probs.astype(LOW), d_mix))
                delta = jnp.sum(probs * d_probs, axis=-1, keepdims=True)
                d_scores = (probs * (d_probs - delta)).astype(LOW)
                d_query.append(dot(d_scores, key))
                d_key.append(dot_left_t(d_scores, scaled))
            low_q = (jnp.where(left_half, *d_query) * (1.0 / math.sqrt(HD))).astype(LOW)
            low_k = jnp.where(left_half, *d_key).astype(LOW)
            low_v = jnp.where(left_half, *d_value).astype(LOW)
            for n_part, low in enumerate((low_q, low_k, low_v)):
                qkv[rows, pl.ds(pl.multiple_of(512 * n_part + 128 * t, 128), 128)] = low
            here = pl.ds(pl.multiple_of(512 * core + 128 * t, 128), 128)
            g_part[BQ, :, here] += fold(low_q.astype(F32))
            g_part[BV, :, here] += fold(low_v.astype(F32))

    def query_terms(step):
        z = planes[step]
        for n in range(3):
            columns = slice(512 * n, 512 * n + 512)
            left = x_all[:, pl.ds(pl.multiple_of(256 * z, 256), 256)]
            part = dot_left_t(left, qkv[:, columns])
            slope[pl.ds(4 * z, 4), :, columns] = part.astype(LOW).reshape(4, 64, 512)

    def short_sums():
        for n in range(SHORT):
            g_sum[n : n + 1, :] = jnp.sum(g_part[n], axis=0, keepdims=True)
        exchange("g", g_sum, g_other)

    def short_terms():
        got["g"]()
        v_terms[...] = jnp.zeros_like(v_terms)
        for n in range(16):
            t = n // 2
            at = slice(128 * t, 128 * t + 128)
            v_terms[n, 0:8] = g_sum[:, at] + g_other[:, at]
            v_terms[n, 8:9] = jnp.sum(i_part[:, 128 * n : 128 * n + 128], axis=0, keepdims=True)

    def d_tokens(turn):
        owner, half = ((peer, 0), (peer, 1), (core, 0), (core, 1))[turn]
        if turn == 0:
            done("part0", "part1")
        at = slice(256 * half, 256 * half + 256)
        for n in range(4):
            part = dot_right_t(qkv[half_of(owner, half), :], w_qkv[4 * n : 4 * n + 4].reshape(256, 1536))
            columns = slice(256 * n, 256 * n + 256)
            if turn < 2:
                out_part[at, columns] = part
            else:
                acc[at, columns] += part
        if turn < 2:
            pass_part(half)

    def tokens_out():
        for half in range(2):
            got[part_name(half)]()

            @pl.loop(2 * half, 2 * half + 2)
            def _(n):
                at = rows_at(n, BLOCK)
                token_grad[at] = (acc[at] + in_part[at]).astype(LOW)

    reduce_2 = Reduce(p, lambda i: t_2.at[i], lambda k: landed_2.at[k], 32, send_sem, recv_sem, 5 * COPIES)
    reduce_i = Reduce(p, lambda i: t_i.at[i], lambda k: landed_i.at[k], 32, send_sem, recv_sem, 6 * COPIES)
    reduce_o = Reduce(p, lambda i: slope.at[i, :, pl.ds(1536, 512)], lambda k: w_i.at[k, :, pl.ds(1536, 512)], 32, send_sem, recv_sem, 7 * COPIES)
    reduce_q = Reduce(
        p,
        lambda i: slope.at[i, :, pl.ds(0, 1536)],
        lambda k: w_i.at[k, :, pl.ds(0, 1536)],
        32,
        send_sem,
        recv_sem,
        8 * COPIES,
    )
    reduce_v = Reduce(p, lambda i: v_terms.at[i], lambda k: v_landed.at[k], 16, send_sem, recv_sem, 9 * COPIES)

    def result_2():
        def put(n, total):
            f_2[rows_at(n, 32)] = total

        reduce_2.result(put)

    def halves_to(first_block):
        def put(n, total):
            xhat[first_block + 2 * n] = total[:, :1024]
            xhat[first_block + 2 * n + 1, :, : total.shape[1] - 1024] = total[:, 1024:]

        return put

    def column(block, n):
        return xhat[block + n // 8, :, 128 * (n % 8) : 128 * (n % 8) + 128]

    def result_i():
        reduce_i.result(halves_to(0))
        exchange("i", xhat.at[pl.ds(2 * peer, 2)], xhat.at[4:6])

    def result_i_out():
        got["i"]()
        for n in range(16):
            f_i[:, rows_at(2 * n + core, 128)] = column(2 * core, n)
            f_i[:, rows_at(2 * n + peer, 128)] = column(4, n)

    def result_o():
        def put(n, total):
            f_s[3][:, rows_at(n, 512)] = total

        reduce_o.result(put)

    def result_v():
        def put(n, total):
            group = 2 * lax.rem(me, 2) + core
            turned = total
            for n_group in (1, 2, 3):
                turned = jnp.where(group == n_group, pltpu.roll(total, 128 - 32 * n_group, 1), turned)
            is_short = lax.broadcasted_iota(jnp.int32, (16, 128), 0) < SHORT
            vec_grad[...] = jnp.where(is_short, turned, total)

        reduce_v.result(put)

    def result_q():
        reduce_q.result(halves_to(8))
        exchange("q", xhat.at[pl.ds(8 + 2 * peer, 2)], xhat.at[12:14])

    def result_q_out():
        got["q"]()
        for n in range(3):
            for owner, block in ((core, 8 + 2 * core), (peer, 12)):
                f_s[n][:, rows_at(owner, 512)] = xhat[block + n // 2, :, 512 * (n % 2) : 512 * (n % 2) + 512]

    gather_v.run(B1)
    gather_o.run(A2)
    gather_i.run(A0)
    gather_q.run(B1)
    gather_v.run(P0)
    gather_q.run(P0)
    gather_o.run(P0, B1)
    gather_v.run(P1)
    gather_i.run(B0)
    gather_o.run(P1)
    gather_q.run(P1, A2)
    gather_v.run(Ap)
    gather_i.run(B1)
    gather_q.run(Ap)
    gather_v.run(A2)
    gather_i.run(Z1)
    gather_q.run(B2)
    gather_v.run(Ao)
    gather_i.run(Z2, Z3)
    gather_v.run(B3)
    gather_o.run(B2)
    gather_q.run(Ao)
    gather_i.run(P1)
    gather_q.run(E1)
    gather_o.run(Ap)
    gather_q.run(B3)
    gather_o.run(Ao, B4)
    gather_v.run(B5)
    gather_q.run(B4)
    gather_v.run(B4)
    gather_2.run(Z2)
    gather_q.run(E2)
    gather_o.run(B3)
    gather_q.run(B5)
    gather_v.run(B2)
    gather_i.run(P0)
    gather_o.run(E2)
    gather_v.run(E1)
    gather_o.run(B5)
    gather_2.run(Z1, B1)
    gather_o.run(E1)
    gather_i.run(A2)
    gather_2.run(Z3)
    gather_i.run(B2)
    gather_o.run(E3)
    gather_v.run(E3, E2)
    relay_output()
    gather_q.run(E3)
    short_params()
    project(1)
    gather_i.run(Ao, B3)
    project(0)
    attention(0, 0)
    attention(0, 1)
    gather_i.run(B4)
    branch(0)
    attention(1, 0)
    gather_2.run(A2)
    attention(1, 1)
    gather_i.run(B5)
    gather_2.run(B2)
    branch(1)
    attention(2, 0)
    gather_i.run(Ap)
    attention(2, 1)
    branch(2)
    gather_i.run(E2)
    attention(3, 0)
    attention(3, 1)
    gather_2.run(B3, P1)
    branch(3)
    gather_2.run(P0)
    norm_first(0)
    norm_first(1)
    gather_2.run(Ao)
    gather_i.run(E3, E1)
    gather_2.run(B4)
    inner(0)
    inner(1)
    gather_2.run(Ap)
    inner(2)
    inner(3)
    gather_2.run(E2, B5)
    outer(0)
    gather_2.run(E1)
    outer(1)
    outer(2)
    gather_2.run(E3)
    outer(3)
    norm_second(0)
    norm_second(1)
    outer_terms(0, 0)
    reduce_2.run(Ap)
    outer_terms(0, 1)
    outer_terms(1)
    reduce_2.run(P0)
    outer_terms(2)
    reduce_2.run(P1, B5)
    outer_terms(3)
    reduce_2.run(B3, B4)
    d_inner(0)
    d_inner(1)
    reduce_2.run(B2)
    d_inner(2)
    d_inner(3)
    inner_terms(0)
    reduce_i.run(P0)
    reduce_2.run(A2, Ao)
    reduce_i.run(P1)
    inner_terms(1)
    inner_terms(2)
    inner_terms(3)
    reduce_i.run(B5)
    d_first(0)
    reduce_2.run(Z2)
    d_first(1)
    reduce_2.run(B1)
    d_first(2)
    reduce_i.run(B3, B4)
    reduce_2.run(Zo)
    d_first(3)
    norm_first_back(0)
    norm_first_back(1)
    reduce_i.run(Ao, B0)
    reduce_2.run(Zp, A0)
    reduce_i.run(Ap, B2)
    output_terms()
    reduce_i.run(B1)
    reduce_2.run(B0)
    reduce_i.run(A2)
    d_mixed()
    attention_back(0, 0)
    reduce_o.run(P1)
    attention_back(0, 1)
    reduce_i.run(Zo)
    attention_back(1, 0)
    reduce_o.run(P0, B3, B5)
    attention_back(1, 1)
    attention_back(2, 0)
    reduce_i.run(Zp)
    reduce_o.run(B4)
    attention_back(2, 1)
    reduce_o.run(B1)
    reduce_i.run(Z2)
    reduce_o.run(B2)
    attention_back(3, 0)
    reduce_i.run(A0)
    attention_back(3, 1)
    query_terms(0)
    reduce_q.run(P0)
    reduce_o.run(A2)
    query_terms(1)
    reduce_o.run(Ao, A0)
    query_terms(2)
    reduce_q.run(B5)
    query_terms(3)
    reduce_q.run(B4)
    reduce_o.run(Z2, Zo)
    d_tokens(0)
    reduce_q.run(Ao)
    d_tokens(1)
    reduce_q.run(P1, Ap)
    result_2()
    d_tokens(2)
    d_tokens(3)
    reduce_q.run(Zo, B3, B2)
    short_sums()
    short_terms()
    reduce_v.run(B5, P1)
    reduce_q.run(A2)
    reduce_v.run(P0)
    reduce_q.run(Zp)
    reduce_v.run(B2)
    result_i()
    reduce_o.run(Ap)
    reduce_v.run(Ao, B3)
    reduce_q.run(B1)
    reduce_v.run(B4, Ap)
    reduce_q.run(Z2, B0)
    reduce_o.run(Zp)
    reduce_v.run(Zo, B1, A2)
    reduce_q.run(A0)
    tokens_out()
    reduce_v.run(Z2)
    result_i_out()
    reduce_v.run(A0, Zp)
    reduce_o.run(B0)
    reduce_v.run(B0)
    result_q()
    result_o()
    result_v()
    result_q_out()

    for each in (gather_q, gather_o, gather_i, gather_2, gather_v):
        each.finish()
    for each in (reduce_q, reduce_o, reduce_i, reduce_2, reduce_v):
        each.finish()
    for each in pending + list(sent.values()):
        each()


def layer(*arrays):
    def low(*shape):
        return pltpu.VMEM(shape, LOW)

    def full(*shape):
        return pltpu.VMEM(shape, F32)

    hbm = pl.BlockSpec(memory_space=pl.ANY)
    vmem = pl.BlockSpec(memory_space=pltpu.VMEM)
    smem = pl.BlockSpec(memory_space=pltpu.SMEM)
    scratch = [
        low(1024, 1024),
        low(1024, 1536),
        low(1024, 512),
        full(512, 1024),
        full(512, 1024),
        full(512, 1024),
        full(16, 32, 1024),
        full(512, 128),
        low(16, 2, 32, 1024),
        low(16, 64, 2048),
        low(16, 64, 2048),
        low(1024, 1024),
        low(16, 64, 1536),
        low(16, 2, 32, 1024),
        low(16, 64, 2048),
        low(16, 128, 1024),
        low(16, 128, 1024),
        low(16, 64, 2048),
        low(COPIES, 128, 1024),
        low(COPIES, 64, 2048),
        low(32, 1536),
        low(32, 2048),
        full(2, 8, 256),
        low(2, 16, 16, 128),
        full(16, 1024),
        full(8, 2048),
        full(SHORT, 8, 1024),
        full(8, 2048),
        full(8, 1024),
        full(8, 1024),
        full(16, 16, 128),
        full(COPIES, 16, 128),
        full(16, 128),
        pltpu.SemaphoreType.DMA((19,)),
        pltpu.SemaphoreType.DMA((26,)),
        pltpu.SemaphoreType.DMA((26,)),
        pltpu.SemaphoreType.DMA((10 * COPIES,)),
        pltpu.SemaphoreType.DMA((10 * COPIES,)),
        pltpu.SemaphoreType.REGULAR,
    ] + [full(1, 32)] * SHORT + [full(1, 128)]
    shape = jax.ShapeDtypeStruct
    return pl.pallas_call(
        layer_kernel,
        out_shape=(
            pltpu.VMEM((512, 1024), LOW),
            pltpu.VMEM((512, 1024), LOW),
            pltpu.VMEM((32, 1024), F32),
            pltpu.VMEM((32, 1024), F32),
            pltpu.VMEM((32, 1024), F32),
            pltpu.VMEM((32, 1024), F32),
            pltpu.VMEM((32, 4096), F32),
            pltpu.VMEM((128, 1024), F32),
            pltpu.VMEM((16, 128), F32),
        ),
        in_specs=[hbm, smem] + [hbm] * (7 + SHORT + 1),
        out_specs=(vmem,) * 9,
        scratch_shapes=scratch,
        compiler_params=pltpu.CompilerParams(
            collective_id=0, has_side_effects=True, vmem_limit_bytes=VMEM_BYTES
        ),
        cost_estimate=pl.CostEstimate(flops=40_000_000_000, bytes_accessed=8 << 20, transcendentals=0),
    )(*arrays)


VMEM_BYTES = 60 << 20


def hand_over_kernel(*refs):
    sources, vec, targets, parts, sems = refs[:8], refs[8], refs[9:17], refs[17 : 17 + SHORT + 1], refs[-1]
    stores = [pltpu.make_async_copy(sources[n], targets[n], sems.at[n]) for n in range(8)]
    for store in stores:
        store.start()
    for n in range(SHORT):
        parts[n][...] = vec[n : n + 1, 0:32]
    parts[SHORT][...] = vec[SHORT : SHORT + 1, :]
    for store in stores:
        store.wait()


def hand_over(*results):
    hbm = pl.BlockSpec(memory_space=pl.ANY)
    vmem = pl.BlockSpec(memory_space=pltpu.VMEM)
    shape = jax.ShapeDtypeStruct
    return pl.pallas_call(
        hand_over_kernel,
        out_shape=tuple(shape(each.shape, each.dtype) for each in results[:8])
        + (shape((1, 32), F32),) * SHORT
        + (shape((1, 128), F32),),
        in_specs=[vmem] * 9,
        out_specs=(hbm,) * 8 + (vmem,) * (SHORT + 1),
        scratch_shapes=[pltpu.SemaphoreType.DMA((8,))],
        compiler_params=pltpu.CompilerParams(vmem_limit_bytes=8 << 20),
    )(*results)


def one_kernel_device(
    tokens,
    lengths,
    cotangent,
    query_weight,
    key_weight,
    value_weight,
    output_weight,
    query_bias,
    value_bias,
    output_bias,
    first_gain,
    first_shift,
    inner_weight,
    inner_bias,
    outer_weight,
    outer_bias,
    second_gain,
    second_shift,
):
    count, seq, width = tokens.shape
    rows = count * seq
    short = (query_bias, value_bias, output_bias, first_gain, first_shift, outer_bias, second_gain, second_shift)
    outs = layer(
        tokens.reshape(rows, width),
        lengths,
        cotangent.reshape(rows, width),
        query_weight,
        key_weight,
        value_weight,
        output_weight,
        inner_weight,
        outer_weight,
        *[each.reshape(1, -1) for each in short + (inner_bias,)],
    )
    outs = hand_over(*outs)
    layer_rows, token_grad, query_g, key_g, value_g, output_g, inner_g, outer_g, *part = outs
    part = [each.reshape(-1) for each in part]
    return (
        layer_rows.reshape(count, seq, width),
        token_grad.reshape(count, seq, width),
        query_g,
        key_g,
        value_g,
        output_g,
        part[BQ],
        part[BV],
        part[BO],
        part[G1],
        part[S1],
        inner_g,
        part[SHORT],
        outer_g,
        part[BF],
        part[G2],
        part[S2],
    )


epsilon = 1e-12


def normalize(hidden, gain, shift):
    center = hidden - jnp.mean(hidden, axis=-1, keepdims=True)
    spread = jnp.mean(center * center, axis=-1, keepdims=True)
    return center * lax.rsqrt(spread + epsilon) * gain + shift


def gelu_exact(inner):
    return jax.nn.gelu(inner, approximate=False)


def matmul(left, right):
    return jnp.dot(left, right, preferred_element_type=jnp.float32)


def matmul_left_t(left, right):
    return lax.dot_general(
        left, right, (((0,), (0,)), ((), ())), preferred_element_type=jnp.float32
    )


def matmul_right_t(left, right):
    return lax.dot_general(
        left, right, (((1,), (1,)), ((), ())), preferred_element_type=jnp.float32
    )


def row_sum(values):
    return jnp.sum(values.astype(jnp.float32), axis=0)


def per_device(
    tokens,
    lengths,
    cotangent,
    query_weight,
    key_weight,
    value_weight,
    output_weight,
    query_bias,
    value_bias,
    output_bias,
    first_gain,
    first_shift,
    inner_weight,
    inner_bias,
    outer_weight,
    outer_bias,
    second_gain,
    second_shift,
):
    attn_master = (
        query_weight,
        key_weight,
        value_weight,
        output_weight,
        query_bias,
        value_bias,
        output_bias,
        first_gain,
        first_shift,
    )
    ffn_master = (inner_weight, inner_bias, outer_weight, outer_bias, second_gain, second_shift)
    attn_half = [param.astype(jnp.bfloat16) for param in attn_master]
    ffn_half = [param.astype(jnp.bfloat16) for param in ffn_master]
    micro_count, rows, width = tokens.shape
    heads = width // HD
    owners = lax.axis_size(("dp", "fsdp"))
    scale = 1.0 / math.sqrt(HD)
    positions = jnp.arange(rows, dtype=jnp.int32)
    attn_totals = [
        jnp.zeros((param.shape[0] * owners,) + param.shape[1:], jnp.float32)
        for param in attn_master
    ]
    ffn_totals = [
        jnp.zeros((param.shape[0] * owners,) + param.shape[1:], jnp.float32) for param in ffn_master
    ]
    outputs_list = []
    token_grads_list = []
    for micro in range(micro_count):
        token_rows = tokens[micro]
        cot_rows = cotangent[micro].astype(jnp.float32)
        valid_keys = positions < lengths[micro]
        attn_full = (
            lax.all_gather(attn_half[0], ("dp", "fsdp"), axis=0, tiled=True),
            lax.all_gather(attn_half[1], ("dp", "fsdp"), axis=0, tiled=True),
            lax.all_gather(attn_half[2], ("dp", "fsdp"), axis=0, tiled=True),
            lax.all_gather(attn_half[3], ("dp", "fsdp"), axis=0, tiled=True),
            lax.all_gather(attn_half[4], ("dp", "fsdp"), axis=0, tiled=True),
            lax.all_gather(attn_half[5], ("dp", "fsdp"), axis=0, tiled=True),
            lax.all_gather(attn_half[6], ("dp", "fsdp"), axis=0, tiled=True),
            lax.all_gather(attn_half[7], ("dp", "fsdp"), axis=0, tiled=True),
            lax.all_gather(attn_half[8], ("dp", "fsdp"), axis=0, tiled=True),
        )
        query_use, key_use, value_use, output_use = (
            attn_full[0],
            attn_full[1],
            attn_full[2],
            attn_full[3],
        )
        bias_query = attn_full[4].astype(jnp.float32)
        bias_value = attn_full[5].astype(jnp.float32)
        bias_output = attn_full[6].astype(jnp.float32)
        gain_first = attn_full[7].astype(jnp.float32)
        shift_first = attn_full[8].astype(jnp.float32)
        query_rows = (matmul(token_rows, query_use) + bias_query).astype(jnp.bfloat16)
        key_rows = matmul(token_rows, key_use).astype(jnp.bfloat16)
        value_rows = (matmul(token_rows, value_use) + bias_value).astype(jnp.bfloat16)
        query_heads = query_rows.reshape(rows, heads, HD)
        key_heads = key_rows.reshape(rows, heads, HD)
        value_heads = value_rows.reshape(rows, heads, HD)

        def attention_scores():
            raw_scores = (
                jnp.einsum(
                    "qhd,khd->hqk", query_heads, key_heads, preferred_element_type=jnp.float32
                )
                * scale
            )
            return jnp.where(valid_keys[None, None, :], raw_scores, -1000000000.0)

        scores = attention_scores()
        peak = jnp.max(scores, axis=-1, keepdims=True)
        log_total = peak + jnp.log(jnp.sum(jnp.exp(scores - peak), axis=-1, keepdims=True))
        probs_low = jnp.exp(scores - log_total).astype(jnp.bfloat16)
        mixed = (
            jnp.einsum("hqk,khd->qhd", probs_low, value_heads, preferred_element_type=jnp.float32)
            .reshape(rows, width)
            .astype(jnp.bfloat16)
        )
        residual = token_rows.astype(jnp.float32) + matmul(mixed, output_use) + bias_output
        first = normalize(residual, gain_first, shift_first)
        first_low = first.astype(jnp.bfloat16)
        ffn_full = (
            lax.all_gather(ffn_half[0], ("dp", "fsdp"), axis=0, tiled=True),
            lax.all_gather(ffn_half[1], ("dp", "fsdp"), axis=0, tiled=True),
            lax.all_gather(ffn_half[2], ("dp", "fsdp"), axis=0, tiled=True),
            lax.all_gather(ffn_half[3], ("dp", "fsdp"), axis=0, tiled=True),
            lax.all_gather(ffn_half[4], ("dp", "fsdp"), axis=0, tiled=True),
            lax.all_gather(ffn_half[5], ("dp", "fsdp"), axis=0, tiled=True),
        )
        inner = matmul(first_low, ffn_full[0]) + ffn_full[1].astype(jnp.float32)
        active = gelu_exact(inner).astype(jnp.bfloat16)
        second_in = first + matmul(active, ffn_full[2]) + ffn_full[3].astype(jnp.float32)
        gain_second = ffn_full[4].astype(jnp.float32)
        shift_second = ffn_full[5].astype(jnp.float32)
        layer_rows, pull_second = jax.vjp(normalize, second_in, gain_second, shift_second)
        outputs_list.append(layer_rows.astype(jnp.bfloat16))
        ffn_full = (
            lax.all_gather(ffn_half[0], ("dp", "fsdp"), axis=0, tiled=True),
            lax.all_gather(ffn_half[1], ("dp", "fsdp"), axis=0, tiled=True),
            lax.all_gather(ffn_half[2], ("dp", "fsdp"), axis=0, tiled=True),
            lax.all_gather(ffn_half[3], ("dp", "fsdp"), axis=0, tiled=True),
            lax.all_gather(ffn_half[4], ("dp", "fsdp"), axis=0, tiled=True),
            lax.all_gather(ffn_half[5], ("dp", "fsdp"), axis=0, tiled=True),
        )
        d_second, d_gain_second, d_shift_second = pull_second(cot_rows)
        d_outer = d_second.astype(jnp.bfloat16)
        ffn_totals[2] = ffn_totals[2] + matmul_left_t(active, d_outer)
        ffn_totals[3] = ffn_totals[3] + row_sum(d_outer)
        ffn_totals[4] = ffn_totals[4] + d_gain_second
        ffn_totals[5] = ffn_totals[5] + d_shift_second
        d_active = matmul_right_t(d_outer, ffn_full[2])
        gelu_value, pull_gelu = jax.vjp(gelu_exact, inner)
        (d_inner,) = pull_gelu(d_active)
        d_inner_low = d_inner.astype(jnp.bfloat16)
        ffn_totals[0] = ffn_totals[0] + matmul_left_t(first_low, d_inner_low)
        ffn_totals[1] = ffn_totals[1] + row_sum(d_inner_low)
        d_first = matmul_right_t(d_inner_low, ffn_full[0]) + d_second
        attn_full = (
            lax.all_gather(attn_half[0], ("dp", "fsdp"), axis=0, tiled=True),
            lax.all_gather(attn_half[1], ("dp", "fsdp"), axis=0, tiled=True),
            lax.all_gather(attn_half[2], ("dp", "fsdp"), axis=0, tiled=True),
            lax.all_gather(attn_half[3], ("dp", "fsdp"), axis=0, tiled=True),
            lax.all_gather(attn_half[4], ("dp", "fsdp"), axis=0, tiled=True),
            lax.all_gather(attn_half[5], ("dp", "fsdp"), axis=0, tiled=True),
            lax.all_gather(attn_half[6], ("dp", "fsdp"), axis=0, tiled=True),
            lax.all_gather(attn_half[7], ("dp", "fsdp"), axis=0, tiled=True),
            lax.all_gather(attn_half[8], ("dp", "fsdp"), axis=0, tiled=True),
        )
        query_use, key_use, value_use, output_use = (
            attn_full[0],
            attn_full[1],
            attn_full[2],
            attn_full[3],
        )
        norm_value, pull_first = jax.vjp(
            normalize, residual, attn_full[7].astype(jnp.float32), attn_full[8].astype(jnp.float32)
        )
        d_residual, d_gain_first, d_shift_first = pull_first(d_first)
        attn_totals[7] = attn_totals[7] + d_gain_first
        attn_totals[8] = attn_totals[8] + d_shift_first
        d_branch = d_residual.astype(jnp.bfloat16)
        attn_totals[3] = attn_totals[3] + matmul_left_t(mixed, d_branch)
        attn_totals[6] = attn_totals[6] + row_sum(d_branch)
        d_mixed = matmul_right_t(d_branch, output_use).astype(jnp.bfloat16).reshape(rows, heads, HD)
        scores = attention_scores()
        probs = jnp.exp(scores - log_total)
        probs_low = probs.astype(jnp.bfloat16)
        d_probs = jnp.einsum(
            "qhd,khd->hqk", d_mixed, value_heads, preferred_element_type=jnp.float32
        )
        d_values = jnp.einsum(
            "hqk,qhd->khd", probs_low, d_mixed, preferred_element_type=jnp.float32
        ).reshape(rows, width)
        delta_rows = jnp.sum(probs * d_probs, axis=-1, keepdims=True)
        d_scores = (probs * (d_probs - delta_rows)).astype(jnp.bfloat16)
        d_queries = (
            (
                jnp.einsum("hqk,khd->qhd", d_scores, key_heads, preferred_element_type=jnp.float32)
                * scale
            )
            .reshape(rows, width)
            .astype(jnp.bfloat16)
        )
        d_keys = (
            jnp.einsum(
                "hqk,qhd->khd", d_scores, query_heads, preferred_element_type=jnp.float32
            ).reshape(rows, width)
            * scale
        )
        key_low = d_keys.astype(jnp.bfloat16)
        value_low = d_values.astype(jnp.bfloat16)
        attn_totals[0] = attn_totals[0] + matmul_left_t(token_rows, d_queries)
        attn_totals[1] = attn_totals[1] + matmul_left_t(token_rows, key_low)
        attn_totals[2] = attn_totals[2] + matmul_left_t(token_rows, value_low)
        attn_totals[4] = attn_totals[4] + row_sum(d_queries)
        attn_totals[5] = attn_totals[5] + row_sum(value_low)
        token_grad = (
            d_residual
            + matmul_right_t(d_queries, query_use)
            + matmul_right_t(key_low, key_use)
            + matmul_right_t(value_low, value_use)
        )
        token_grads_list.append(token_grad.astype(jnp.bfloat16))
    attn_shards = (
        lax.psum_scatter(attn_totals[0], ("dp", "fsdp"), scatter_dimension=0, tiled=True),
        lax.psum_scatter(attn_totals[1], ("dp", "fsdp"), scatter_dimension=0, tiled=True),
        lax.psum_scatter(attn_totals[2], ("dp", "fsdp"), scatter_dimension=0, tiled=True),
        lax.psum_scatter(attn_totals[3], ("dp", "fsdp"), scatter_dimension=0, tiled=True),
        lax.psum_scatter(attn_totals[4], ("dp", "fsdp"), scatter_dimension=0, tiled=True),
        lax.psum_scatter(attn_totals[5], ("dp", "fsdp"), scatter_dimension=0, tiled=True),
        lax.psum_scatter(attn_totals[6], ("dp", "fsdp"), scatter_dimension=0, tiled=True),
        lax.psum_scatter(attn_totals[7], ("dp", "fsdp"), scatter_dimension=0, tiled=True),
        lax.psum_scatter(attn_totals[8], ("dp", "fsdp"), scatter_dimension=0, tiled=True),
    )
    ffn_shards = (
        lax.psum_scatter(ffn_totals[0], ("dp", "fsdp"), scatter_dimension=0, tiled=True),
        lax.psum_scatter(ffn_totals[1], ("dp", "fsdp"), scatter_dimension=0, tiled=True),
        lax.psum_scatter(ffn_totals[2], ("dp", "fsdp"), scatter_dimension=0, tiled=True),
        lax.psum_scatter(ffn_totals[3], ("dp", "fsdp"), scatter_dimension=0, tiled=True),
        lax.psum_scatter(ffn_totals[4], ("dp", "fsdp"), scatter_dimension=0, tiled=True),
        lax.psum_scatter(ffn_totals[5], ("dp", "fsdp"), scatter_dimension=0, tiled=True),
    )
    return (
        jnp.stack(outputs_list),
        jnp.stack(token_grads_list),
        attn_shards[0],
        attn_shards[1],
        attn_shards[2],
        attn_shards[3],
        attn_shards[4],
        attn_shards[5],
        attn_shards[6],
        attn_shards[7],
        attn_shards[8],
        ffn_shards[0],
        ffn_shards[1],
        ffn_shards[2],
        ffn_shards[3],
        ffn_shards[4],
        ffn_shards[5],
    )


def solution(mesh):
    in_specs = (
        P(("dp", "fsdp"), None, None),
        P(("dp", "fsdp")),
        P(("dp", "fsdp"), None, None),
        P(("dp", "fsdp"), None),
        P(("dp", "fsdp"), None),
        P(("dp", "fsdp"), None),
        P(("dp", "fsdp"), None),
        P(("dp", "fsdp")),
        P(("dp", "fsdp")),
        P(("dp", "fsdp")),
        P(("dp", "fsdp")),
        P(("dp", "fsdp")),
        P(("dp", "fsdp"), None),
        P(("dp", "fsdp")),
        P(("dp", "fsdp"), None),
        P(("dp", "fsdp")),
        P(("dp", "fsdp")),
        P(("dp", "fsdp")),
    )
    out_specs = (
        P(("dp", "fsdp"), None, None),
        P(("dp", "fsdp"), None, None),
        P(("dp", "fsdp"), None),
        P(("dp", "fsdp"), None),
        P(("dp", "fsdp"), None),
        P(("dp", "fsdp"), None),
        P(("dp", "fsdp")),
        P(("dp", "fsdp")),
        P(("dp", "fsdp")),
        P(("dp", "fsdp")),
        P(("dp", "fsdp")),
        P(("dp", "fsdp"), None),
        P(("dp", "fsdp")),
        P(("dp", "fsdp"), None),
        P(("dp", "fsdp")),
        P(("dp", "fsdp")),
        P(("dp", "fsdp")),
    )
    one_kernel = dict(mesh.shape) == {"dp": 16, "fsdp": 2}
    device = one_kernel_device if one_kernel else per_device
    return jax.shard_map(
        device, mesh=mesh, in_specs=in_specs, out_specs=out_specs, check_vma=False
    )
```

```python
import functools
import math

import jax
import jax.numpy as jnp
from jax import lax
from jax.experimental import pallas as pl
from jax.experimental.pallas import tpu as pltpu
from jax.sharding import PartitionSpec as P

MESH = pl.DeviceIdType.MESH
COPIES = 15
HD = 64
LOW = jnp.bfloat16
F32 = jnp.float32


class Place:
    def __init__(self):
        self.me = lax.axis_index("dp")
        self.core = lax.axis_index("fsdp")
        x, y, self.z = lax.rem(self.me, 2), lax.rem(self.me // 2, 2), self.me // 4
        self.a = x + self.core * (y - x)
        self.b = y + self.core * (x - y)
        odd = lax.rem(self.z, 2)
        self.pair, self.other = 3 - 2 * odd, 1 + 2 * odd
        self.z_pair = self.z + 1 - 2 * odd

    def chip(self, z, a, b):
        return z * 4 + (b + self.core * (a - b)) * 2 + (a + self.core * (b - a))

    def back(self, j):
        return lax.rem(self.z - j + 4, 4)

    def peers(self):
        along_z = [self.chip(lax.rem(self.z + k, 4), self.a, self.b) for k in (1, 2, 3)]
        return along_z + [self.chip(self.z, 1 - self.a, self.b), self.chip(self.z, self.a, 1 - self.b)]

    def signal_peers(self, sem):
        for chip in self.peers():
            pl.semaphore_signal(sem, inc=1, device_id=(chip, self.core), device_id_type=MESH)

    def announce(self):
        sem = pltpu.get_barrier_semaphore()
        self.signal_peers(sem)
        pl.semaphore_signal(sem, inc=1, device_id=(self.me, 1 - self.core), device_id_type=MESH)

    def meet(self):
        pl.semaphore_wait(pltpu.get_barrier_semaphore(), 6)


class Hops:
    def __init__(self, place, send_sem, recv_sem, base):
        self.place, self.send_sem, self.recv_sem, self.base = place, send_sem, recv_sem, base
        self.started = []

    def send(self, k, source, target, chip):
        copy = pltpu.make_async_remote_copy(
            src_ref=source,
            dst_ref=target,
            send_sem=self.send_sem.at[self.base + k],
            recv_sem=self.recv_sem.at[self.base + k],
            device_id=(chip, self.place.core),
            device_id_type=MESH,
        )
        copy.start()
        self.started.append(copy)

    def arrived(self, k, block):
        pltpu.make_async_remote_copy(
            src_ref=block,
            dst_ref=block,
            send_sem=self.send_sem.at[self.base + k],
            recv_sem=self.recv_sem.at[self.base + k],
            device_id=(self.place.me, self.place.core),
            device_id_type=MESH,
        ).wait_recv()

    def finish(self):
        for copy in self.started:
            copy.wait_send()
        self.started = []


class Gather(Hops):
    def __init__(self, place, held, *rest):
        super().__init__(place, *rest)
        self.held = held

    def pass_on(self, k, block, chip):
        self.send(k, self.held.at[block], self.held.at[block], chip)

    def wait(self, *copies):
        for k in copies:
            self.arrived(k, self.held.at[self.place.me])

    def run(self, *hops):
        for hop in hops:
            self.take(hop)

    def take(self, name):
        p = self.place
        kind, which = name
        which = {PAIR: p.pair, OTHER: p.other}.get(which, which)
        if kind == Z:
            self.pass_on(which - 1, p.me, p.chip(lax.rem(p.z + which, 4), p.a, p.b))
        elif kind == A:
            if name != A0:
                self.wait(which - 1)
            self.pass_on(3 + which, p.chip(p.back(which), p.a, p.b), p.chip(p.z, 1 - p.a, p.b))
        elif kind == B:
            j = (0, 0, 2, 2, p.other, p.other)[which]
            if which % 2:
                self.wait(3 + j)
            block = p.chip(p.back(j), (p.a, 1 - p.a)[which % 2], p.b)
            self.pass_on(7 + which, block, p.chip(p.z, p.a, 1 - p.b))
        elif kind == P_:
            self.wait(7 + which)
            block = p.chip(p.z, (p.a, 1 - p.a)[which], 1 - p.b)
            self.pass_on(13 + which, block, p.chip(p.z_pair, p.a, p.b))
        else:
            self.wait(*((), (3 + p.pair,), (9, 10), (11, 12, 13, 14))[which])


class Reduce(Hops):
    def __init__(self, place, terms, landed, chunk, *rest):
        super().__init__(place, *rest)
        self.terms, self.landed, self.chunk = terms, landed, chunk

    def sum_into(self, block, ks, store):
        for k in ks:
            self.arrived(k, self.landed(k))
        term = self.terms(block)
        landed = [self.landed(k) for k in ks]
        rows = term.shape[0]

        def some(n):
            at = rows_at(n, self.chunk)
            total = term[at].astype(F32)
            for each in landed:
                total += each[at].astype(F32)
            store(n, total)

        if rows == self.chunk:
            some(0)
        else:
            pl.loop(0, rows // self.chunk)(some)

    def add_and_send(self, k, block, ks, chip):
        term = self.terms(block)
        if ks:

            def store(n, total):
                term[rows_at(n, self.chunk)] = total.astype(term.dtype)

            self.sum_into(block, ks, store)
        self.send(k, term, self.landed(k), chip)

    def run(self, *hops):
        for hop in hops:
            self.take(hop)

    def take(self, name):
        p = self.place
        kind, which = name
        which = {PAIR: p.pair, OTHER: p.other}.get(which, which)
        if kind == P_:
            block = p.chip(p.z_pair, (p.a, 1 - p.a)[which], 1 - p.b)
            self.add_and_send(13 + which, block, (), p.chip(p.z_pair, p.a, p.b))
        elif kind == B:
            j = (0, 0, 2, 2, p.other, p.other)[which]
            block = p.chip(p.back(j), (p.a, 1 - p.a)[which % 2], 1 - p.b)
            landed = (13 + which,) if which < 2 else ()
            self.add_and_send(7 + which, block, landed, p.chip(p.z, p.a, 1 - p.b))
        elif kind == A:
            landed = {A0: (8,), A2: (10,), Ao: (12,), Ap: ()}[name]
            block = p.chip(p.back(which), 1 - p.a, p.b)
            self.add_and_send(3 + which, block, landed, p.chip(p.z, 1 - p.a, p.b))
        else:
            landed = {Z2: (9, 5), Zo: (11, 3 + p.other), Zp: (3 + p.pair,)}[name]
            owner = p.chip(p.back(which), p.a, p.b)
            self.add_and_send(3 - which, owner, landed, owner)

    def result(self, store):
        self.sum_into(self.place.me, (7, 3, 0, 1, 2), store)


class Across:
    def __init__(self, place, send_sem, recv_sem):
        self.place, self.send_sem, self.recv_sem = place, send_sem, recv_sem
        self.count = 0

    def copy(self, k, source, target):
        p = self.place
        return pltpu.make_async_remote_copy(
            src_ref=source,
            dst_ref=target,
            send_sem=self.send_sem.at[k],
            recv_sem=self.recv_sem.at[k],
            device_id=(p.me, 1 - p.core),
            device_id_type=MESH,
        )

    def send(self, source, target, here=None):
        k = self.count
        self.count += 1
        copy = self.copy(k, source, target)
        copy.start()
        landing = target if here is None else here
        return copy.wait_send, self.copy(k, landing, landing).wait_recv


def dot(left, right):
    return jnp.dot(left, right, preferred_element_type=F32)


def dot_left_t(left, right):
    return lax.dot_general(left, right, (((0,), (0,)), ((), ())), preferred_element_type=F32)


def dot_right_t(left, right):
    return lax.dot_general(left, right, (((1,), (1,)), ((), ())), preferred_element_type=F32)


def fold(values):
    rows, columns = values.shape
    return jnp.sum(values.reshape(rows // 8, 8, columns), axis=0)


def rows_at(index, size):
    if isinstance(index, int):
        return pl.ds(index * size, size)
    return pl.ds(pl.multiple_of(index * size, size), size)


Z, A, B, P_, E = range(5)
PAIR, OTHER = -1, -2
Z1, Z2, Z3, Zp, Zo = (Z, 1), (Z, 2), (Z, 3), (Z, PAIR), (Z, OTHER)
A0, A2, Ap, Ao = (A, 0), (A, 2), (A, PAIR), (A, OTHER)
B0, B1, B2, B3, B4, B5 = [(B, n) for n in range(6)]
P0, P1 = (P_, 0), (P_, 1)
E1, E2, E3 = (E, 1), (E, 2), (E, 3)
EARLY = (Z2, A0, B0, Z1, Z3)

SHORT = 8
BQ, BV, BO, G1, S1, BF, G2, S2 = range(SHORT)
EPSILON = 1e-12


def layer_kernel(
    tokens,
    lengths,
    cotangent,
    query_weight,
    key_weight,
    value_weight,
    output_weight,
    inner_weight,
    outer_weight,
    *rest,
):
    short_shards, rest = rest[: SHORT + 1], rest[SHORT + 1 :]
    layer_body(
        tokens,
        lengths,
        cotangent,
        query_weight,
        key_weight,
        value_weight,
        output_weight,
        inner_weight,
        outer_weight,
        short_shards,
        rest[-SHORT - 1 :],
        *rest[: -SHORT - 1],
    )


def layer_body(
    tokens,
    lengths,
    cotangent,
    query_weight,
    key_weight,
    value_weight,
    output_weight,
    inner_weight,
    outer_weight,
    short_shards,
    short_here,
    layer_out,
    token_grad,
    query_grad,
    key_grad,
    value_grad,
    output_grad,
    inner_grad,
    outer_grad,
    vec_grad,
    x_all,
    qkv,
    mix,
    acc,
    out_part,
    in_part,
    xhat,
    scale1,
    first,
    act,
    slope,
    dout,
    w_qkv,
    w_o,
    w_i,
    w_2,
    t_2,
    t_i,
    landed_2,
    landed_i,
    stage_q,
    stage_i,
    mask,
    vec_all,
    params,
    inner_bias,
    g_part,
    i_part,
    g_sum,
    g_other,
    v_terms,
    v_landed,
    v_stage,
    local_sem,
    core_send,
    core_recv,
    send_sem,
    recv_sem,
    ready_sem,
):
    f_s = (query_grad, key_grad, value_grad, output_grad)
    f_i, f_2, gbuf = inner_grad, outer_grad, layer_out
    p = Place()
    me, core = p.me, p.core
    peer = 1 - core
    across = Across(p, core_send, core_recv)
    pending = []

    own_rows = rows_at(core, 512)
    peer_rows = rows_at(peer, 512)

    def local(k, source, target):
        return pltpu.make_async_copy(source, target, local_sem.at[k])

    p.announce()
    loads = [
        local(0, query_weight, f_s[0]),
        local(1, key_weight, f_s[1]),
        local(2, value_weight, f_s[2]),
        local(3, output_weight, f_s[3]),
        local(4, inner_weight, f_i),
        local(5, outer_weight, f_2),
        local(6, tokens, x_all.at[own_rows]),
        local(7, cotangent, gbuf),
    ]
    short_loads = [local(10 + n, short_shards[n], short_here[n]) for n in range(SHORT + 1)]
    for copy in loads[:4] + [loads[5]] + short_loads + [loads[4]] + loads[6:]:
        copy.start()

    gather_o = Gather(p, w_o.at[:, core], send_sem, recv_sem, COPIES)
    gather_v = Gather(p, vec_all.at[core], send_sem, recv_sem, 4 * COPIES)
    gather_q = Gather(p, w_qkv, send_sem, recv_sem, 0)
    gather_i = Gather(p, w_i, send_sem, recv_sem, 2 * COPIES)
    gather_2 = Gather(p, w_2, send_sem, recv_sem, 3 * COPIES)
    for copy in loads[:4]:
        copy.wait()
    my_rows = rows_at(core, 32)
    for n in range(3):
        stage_q[:, 512 * n : 512 * n + 512] = f_s[n][:, rows_at(peer, 512)].astype(LOW)
    w_o[me, core] = f_s[3][...].astype(LOW)
    p.meet()
    sent_q, got_q = across.send(stage_q, w_qkv.at[me, my_rows], w_qkv.at[me, rows_at(peer, 32)])
    gather_o.run(*EARLY)
    for n in range(3):
        w_qkv[me, my_rows, 512 * n : 512 * n + 512] = f_s[n][:, rows_at(core, 512)].astype(LOW)
    loads[5].wait()
    w_2[me] = f_2[...].astype(LOW)
    gather_2.run(A0, B0)
    got_q()
    gather_q.run(*EARLY)
    for copy in short_loads:
        copy.wait()
    v_stage[...] = jnp.zeros_like(v_stage)
    for n in range(SHORT):
        v_stage[n : n + 1, 0:32] = short_here[n][...]
    v_stage[SHORT : SHORT + 1, :] = short_here[SHORT][...]
    piece = v_stage[...]
    four = piece + pltpu.roll(piece, 32, 1) + pltpu.roll(piece, 64, 1) + pltpu.roll(piece, 96, 1)
    is_short = lax.broadcasted_iota(jnp.int32, (16, 128), 0) < SHORT
    vec_all[core, me] = jnp.where(is_short, four, piece).astype(LOW)
    gather_v.run(*EARLY)
    loads[4].wait()
    for n in range(16):
        here, there = 2 * n + core, 2 * n + peer
        at = slice(128 * n, 128 * n + 128)
        w_i[me, my_rows, at] = f_i[:, rows_at(here, 128)].astype(LOW)
        stage_i[:, at] = f_i[:, rows_at(there, 128)].astype(LOW)
    sent_i, got_i = across.send(stage_i, w_i.at[me, my_rows], w_i.at[me, rows_at(peer, 32)])
    places = lax.broadcasted_iota(jnp.int32, (8, 256), 1)
    seq_of = lax.broadcasted_iota(jnp.int32, (8, 256), 0)
    limit = jnp.where(seq_of == 0, lengths[0], lengths[1])
    mask[core] = jnp.where(places < limit, 1.0, 0.0).astype(F32)
    sent_m, got_m = across.send(mask.at[core], mask.at[core], mask.at[peer])
    loads[6].wait()
    sent_x, got_x = across.send(x_all.at[own_rows], x_all.at[own_rows], x_all.at[peer_rows])
    g_part[...] = jnp.zeros_like(g_part)
    i_part[...] = jnp.zeros_like(i_part)
    got_i()
    pending += [sent_q, sent_m, sent_i, sent_x]
    sent, got = {}, {}

    def exchange(name, source, target, here=None):
        sent[name], got[name] = across.send(source, target, here)

    def done(*names):
        for name in names:
            sent.pop(name)()

    def relay_output():
        mine = rows_at(core, 8)
        theirs = rows_at(peer, 8)
        exchange("o", w_o.at[theirs, core], w_o.at[theirs, core], w_o.at[mine, peer])
        exchange("v", vec_all.at[core], vec_all.at[core], vec_all.at[peer])

    def short_params():
        got["v"]()
        lane_group = lax.broadcasted_iota(jnp.int32, (16, 128), 1) // 32
        for t in range(8):
            pieces = [vec_all[i % 2, 2 * t + i // 2].astype(F32) for i in range(4)]
            tile = jnp.where(
                lane_group < 2,
                jnp.where(lane_group == 0, pieces[0], pieces[1]),
                jnp.where(lane_group == 2, pieces[2], pieces[3]),
            )
            params[:, 128 * t : 128 * t + 128] = tile
        for n in range(16):
            inner_bias[:, 128 * n : 128 * n + 128] = vec_all[core, n].astype(F32)[8:16]
        got_x()
        got_m()

    def param(n):
        return params[n : n + 1, :]

    def project(turn):
        owner = (core, peer)[turn]

        @pl.loop(0, 2)
        def _(half):
            rows = rows_at(2 * owner + half, 256)
            block = x_all[rows, :]
            for n in range(3):
                part = dot(block, w_qkv[:, :, 512 * n : 512 * n + 512].reshape(1024, 512))
                if n != 1:
                    part = part + params[BQ if n == 0 else BV, rows_at(core, 512)][None, :]
                qkv[rows, 512 * n : 512 * n + 512] = part.astype(LOW)

    left_half = lax.broadcasted_iota(jnp.int32, (256, 128), 1) < HD

    def heads_of(s, t):
        rows = rows_at(s, 256)
        return [qkv[rows, pl.ds(pl.multiple_of(512 * n + 128 * t, 128), 128)] for n in range(3)]

    def softmax(query_half, key, valid):
        raw = dot_right_t(query_half, key)
        raw = jnp.where(valid, raw, -1000000000.0)
        grown = jnp.exp(raw - jnp.max(raw, axis=-1, keepdims=True))
        return grown * (1.0 / jnp.sum(grown, axis=-1, keepdims=True))

    def halves(pair):
        none = jnp.zeros_like(pair)
        return jnp.where(left_half, pair, none), jnp.where(left_half, none, pair)

    scale = jnp.array(1.0 / math.sqrt(HD), LOW)

    def turn_of(turn):
        return (peer, peer, core, core)[turn], turn % 2

    def attention(turn, part):
        owner, n = turn_of(turn)
        s = 2 * owner + n
        valid = mask[owner, n : n + 1, :] > 0.5

        @pl.loop(2 * part, 2 * part + 2)
        def _(t):
            query, key, value = heads_of(s, t)
            outs = [
                dot(softmax(half, key, valid).astype(LOW), value) for half in halves(query * scale)
            ]
            both = jnp.where(left_half, outs[0], outs[1]).astype(LOW)
            mix[rows_at(s, 256), rows_at(t, 128)] = both

    def part_name(half):
        return "part0" if half == 0 else "part1"

    def pass_part(half):
        at = slice(256 * half, 256 * half + 256)
        exchange(part_name(half), out_part.at[at], in_part.at[at])

    def branch(turn):
        owner, n = turn_of(turn)
        if turn == 0:
            got["o"]()
        out_use = w_o[rows_at(core, 8)].reshape(512, 1024)
        part = dot(mix[rows_at(2 * owner + n, 256), :], out_use)
        at = slice(256 * n, 256 * n + 256)
        if turn < 2:
            out_part[at] = part
            pass_part(n)
        else:
            acc[at] = part

    def norm_of(hidden):
        center = hidden - jnp.mean(hidden, axis=-1, keepdims=True)
        spread = jnp.mean(center * center, axis=-1, keepdims=True)
        inverse = lax.rsqrt(spread + EPSILON)
        return center * inverse, inverse

    def norm_back(grown, normal, inverse):
        along = jnp.mean(grown * normal, axis=-1, keepdims=True)
        return inverse * (grown - jnp.mean(grown, axis=-1, keepdims=True) - normal * along)

    BLOCK = 128

    def tokens_of(owner, n):
        return pl.ds(pl.multiple_of(512 * owner + BLOCK * n, BLOCK), BLOCK)

    def half_of(owner, half):
        return pl.ds(pl.multiple_of(512 * owner + 256 * half, 256), 256)

    def share(name, whole, half):
        exchange(name + str(half), whole.at[half_of(core, half)], whole.at[half_of(core, half)], whole.at[half_of(peer, half)])

    def norm_first(half):
        got[part_name(half)]()

        @pl.loop(2 * half, 2 * half + 2)
        def _(n):
            at = rows_at(n, BLOCK)
            hidden = x_all[tokens_of(core, n), :].astype(F32) + acc[at] + in_part[at] + param(BO)
            normal, inverse = norm_of(hidden)
            xhat[rows_at(n, 4)] = normal.reshape(4, 32, 1024)
            scale1[at] = jnp.broadcast_to(inverse, (BLOCK, 128))
            first[pl.ds(8 * core + 2 * n, 2)] = (normal * param(G1) + param(S1)).astype(LOW).reshape(2, 2, 32, 1024)

        mine = pl.ds(8 * core + 4 * half, 4)
        theirs = pl.ds(8 * peer + 4 * half, 4)
        exchange("first" + str(half), first.at[mine], first.at[mine], first.at[theirs])
        if half == 1:
            done("part0", "part1")

    def inner(turn):
        owner, half = ((core, 0), (core, 1), (peer, 0), (peer, 1))[turn]
        if turn > 1:
            got["first" + str(half)]()
        rows64 = 8 * owner + 4 * half
        block = first[pl.ds(rows64, 4)].reshape(256, 1024)

        @pl.loop(0, 4)
        def _(n):
            columns = rows_at(n, 512)
            before = dot(block, w_i[:, :, columns].reshape(1024, 512)) + inner_bias[0:1, columns]
            error = lax.erf(before * (1.0 / math.sqrt(2.0)))
            chance = 0.5 * (1.0 + error)
            bell = jnp.exp(-0.5 * before * before) * (1.0 / math.sqrt(2.0 * math.pi))
            act[pl.ds(rows64, 4), :, columns] = (before * chance).astype(LOW).reshape(4, 64, 512)
            slope[pl.ds(rows64, 4), :, columns] = (chance + before * bell).astype(LOW).reshape(4, 64, 512)

    far = 1 - p.b

    def chips_of(group):
        if group < 2:
            a = (p.a, 1 - p.a)[group]
            return [p.chip(z, a, p.b) for z in range(4)]
        return [p.chip(p.back(j), a, far) for j in ((0, 2), (p.other, p.pair))[group - 2] for a in (p.a, 1 - p.a)]

    def outer_half(group, turn):
        owner, half = ((peer, 0), (peer, 1), (core, 0), (core, 1))[turn]
        target = out_part if turn < 2 else acc
        chips = chips_of(group)
        left = jnp.concatenate([act[pl.ds(8 * owner + 4 * half, 4), :, rows_at(chip, 128)].reshape(256, 128) for chip in chips], axis=1)
        at = slice(256 * half, 256 * half + 256)
        for n in range(2):
            columns = slice(512 * n, 512 * n + 512)
            right = jnp.concatenate([w_2[chip, :, columns] for chip in chips], axis=0)
            part = dot(left, right)
            if group > 0:
                part = target[at, columns] + part
            if group == 3 and turn < 2:
                t_2[2 * half : 2 * half + 2, :, columns] = part.astype(LOW).reshape(2, 128, 512)
            else:
                target[at, columns] = part
        if group == 3 and turn < 2:
            exchange(part_name(half), t_2.at[2 * half : 2 * half + 2], t_2.at[4 + 2 * half : 6 + 2 * half])

    def outer(group):
        for turn in range(4):
            outer_half(group, turn)

    def norm_second(half):
        got[part_name(half)]()
        if half == 0:
            loads[7].wait()
        for n in (2 * half, 2 * half + 1):
            at = rows_at(n, BLOCK)
            hidden = xhat[rows_at(n, 4)].reshape(BLOCK, 1024) * param(G1) + param(S1)
            hidden = hidden + acc[at] + t_2[4 + n].astype(F32) + param(BF)
            normal, inverse = norm_of(hidden)
            given = gbuf[at].astype(F32)
            gbuf[at] = (normal * param(G2) + param(S2)).astype(LOW)
            g_part[G2] += fold(given * normal)
            g_part[S2] += fold(given)
            down = norm_back(given * param(G2), normal, inverse)
            acc[at] = down
            low = down.astype(LOW)
            g_part[BF] += fold(low.astype(F32))
            dout[tokens_of(core, n), :] = low
            exchange("dout" + str(n), dout.at[tokens_of(core, n)], dout.at[tokens_of(core, n)], dout.at[tokens_of(peer, n)])
    planes = (p.z_pair, p.back(2), p.back(p.other), p.z)

    def outer_terms(step, part=None):
        if step == 0 and part == 0:
            for n in range(4):
                got["dout" + str(n)]()
            done("part0", "part1")
        z = planes[step]
        y = jnp.where(core == 0, p.b, 1 - p.a)
        for half in (0, 1) if part is None else (y if part == 0 else 1 - y,):
            left = act[:, :, pl.ds(pl.multiple_of(512 * z + 256 * half, 256), 256)].reshape(1024, 256)
            block = dot_left_t(left, dout[...])
            t_2[pl.ds(4 * z + 2 * half, 2)] = block.astype(LOW).reshape(2, 128, 1024)

    def d_inner(n):
        columns = rows_at(n, 512)

        @pl.loop(0, 4)
        def _(s):
            rows = rows_at(s, 256)
            back = dot_right_t(dout[rows, :], w_2[pl.ds(4 * n, 4)].reshape(512, 1024))
            bent = slope[pl.ds(4 * s, 4), :, columns].reshape(256, 512).astype(F32)
            low = (back * bent).astype(LOW)
            act[pl.ds(4 * s, 4), :, columns] = low.reshape(4, 64, 512)
            i_part[:, columns] += fold(low.astype(F32))

    def inner_terms(step):
        z = planes[step]
        for n in range(4):
            columns = slice(512 * n, 512 * n + 512)
            left = first[:, :, :, pl.ds(pl.multiple_of(256 * z, 256), 256)].reshape(1024, 256)
            part = dot_left_t(left, act[:, :, columns].reshape(1024, 512))
            t_i[pl.ds(4 * z, 4), :, columns] = part.astype(LOW).reshape(4, 64, 512)

    def d_first(turn):
        owner, half = ((peer, 0), (peer, 1), (core, 0), (core, 1))[turn]
        at = slice(256 * half, 256 * half + 256)
        for n in range(4):
            part = dot_right_t(act[pl.ds(8 * owner + 4 * half, 4)].reshape(256, 2048), w_i[4 * n : 4 * n + 4].reshape(256, 2048))
            columns = slice(256 * n, 256 * n + 256)
            if turn < 2:
                out_part[at, columns] = part
            else:
                acc[at, columns] += part
        if turn < 2:
            pass_part(half)
        if turn == 3:
            gather_i.finish()
            p.signal_peers(ready_sem)

    def norm_first_back(half):
        if half == 0:
            done("dout0", "dout1", "dout2", "dout3")
        got[part_name(half)]()

        @pl.loop(2 * half, 2 * half + 2)
        def _(n):
            at = rows_at(n, BLOCK)
            normal = xhat[rows_at(n, 4)].reshape(BLOCK, 1024)
            given = acc[at] + in_part[at]
            g_part[G1] += fold(given * normal)
            g_part[S1] += fold(given)
            down = norm_back(given * param(G1), normal, scale1[at, 0:1])
            acc[at] = down
            low = down.astype(LOW)
            g_part[BO] += fold(low.astype(F32))
            dout[tokens_of(core, n), :] = low

        share("dout", dout, half)

    def output_terms():
        got["dout0"]()
        got["dout1"]()
        for half in range(2):
            part = dot_left_t(mix[:, 256 * half : 256 * half + 256], dout[...])
            part = part.astype(LOW).reshape(4, 2, 32, 1024)
            low, high = part[:, 0], part[:, 1]
            mine, theirs = jnp.where(core == 0, low, high), jnp.where(core == 0, high, low)
            chips = pl.ds(8 * core + 4 * half, 4)
            for n in range(2):
                columns = slice(512 * n, 512 * n + 512)
                rows = slice(32 * n, 32 * n + 32)
                slope[chips, rows, 1536:2048] = mine[:, :, columns]
                act[4 * half : 4 * half + 4, rows, 0:512] = theirs[:, :, columns]
        last = pl.ds(1536, 512)
        exchange(
            "t",
            act.at[pl.ds(0, 8), :, pl.ds(0, 512)],
            slope.at[pl.ds(8 * core, 8), :, last],
            slope.at[pl.ds(8 * peer, 8), :, last],
        )

    def d_mixed():
        @pl.loop(0, 4)
        def _(s):
            rows = rows_at(s, 256)
            mix[rows, :] = dot_right_t(dout[rows, :], w_o[rows_at(core, 8)].reshape(512, 1024)).astype(LOW)

        got["t"]()
        pl.semaphore_wait(ready_sem, 5)

    def attention_back(turn, part):
        owner, n = turn_of(turn)
        s = 2 * owner + n
        valid = mask[owner, n : n + 1, :] > 0.5
        rows = rows_at(s, 256)

        @pl.loop(2 * part, 2 * part + 2)
        def _(t):
            query, key, value = heads_of(s, t)
            columns = rows_at(t, 128)
            d_mix = mix[rows, columns]
            scaled = query * scale
            d_query, d_key, d_value = [], [], []
            for q_half, m_half in zip(halves(scaled), halves(d_mix)):
                probs = softmax(q_half, key, valid)
                d_probs = dot_right_t(m_half, value)
                d_value.append(dot_left_t(probs.astype(LOW), d_mix))
                delta = jnp.sum(probs * d_probs, axis=-1, keepdims=True)
                d_scores = (probs * (d_probs - delta)).astype(LOW)
                d_query.append(dot(d_scores, key))
                d_key.append(dot_left_t(d_scores, scaled))
            low_q = (jnp.where(left_half, *d_query) * (1.0 / math.sqrt(HD))).astype(LOW)
            low_k = jnp.where(left_half, *d_key).astype(LOW)
            low_v = jnp.where(left_half, *d_value).astype(LOW)
            for n_part, low in enumerate((low_q, low_k, low_v)):
                qkv[rows, pl.ds(pl.multiple_of(512 * n_part + 128 * t, 128), 128)] = low
            here = pl.ds(pl.multiple_of(512 * core + 128 * t, 128), 128)
            g_part[BQ, :, here] += fold(low_q.astype(F32))
            g_part[BV, :, here] += fold(low_v.astype(F32))

    def query_terms(step):
        z = planes[step]
        for n in range(3):
            columns = slice(512 * n, 512 * n + 512)
            left = x_all[:, pl.ds(pl.multiple_of(256 * z, 256), 256)]
            part = dot_left_t(left, qkv[:, columns])
            slope[pl.ds(4 * z, 4), :, columns] = part.astype(LOW).reshape(4, 64, 512)

    def short_sums():
        for n in range(SHORT):
            g_sum[n : n + 1, :] = jnp.sum(g_part[n], axis=0, keepdims=True)
        exchange("g", g_sum, g_other)

    def short_terms():
        got["g"]()
        v_terms[...] = jnp.zeros_like(v_terms)
        for n in range(16):
            t = n // 2
            at = slice(128 * t, 128 * t + 128)
            v_terms[n, 0:8] = g_sum[:, at] + g_other[:, at]
            v_terms[n, 8:9] = jnp.sum(i_part[:, 128 * n : 128 * n + 128], axis=0, keepdims=True)

    def d_tokens(turn):
        owner, half = ((peer, 0), (peer, 1), (core, 0), (core, 1))[turn]
        if turn == 0:
            done("part0", "part1")
        at = slice(256 * half, 256 * half + 256)
        for n in range(4):
            part = dot_right_t(qkv[half_of(owner, half), :], w_qkv[4 * n : 4 * n + 4].reshape(256, 1536))
            columns = slice(256 * n, 256 * n + 256)
            if turn < 2:
                out_part[at, columns] = part
            else:
                acc[at, columns] += part
        if turn < 2:
            pass_part(half)

    def tokens_out():
        for half in range(2):
            got[part_name(half)]()

            @pl.loop(2 * half, 2 * half + 2)
            def _(n):
                at = rows_at(n, BLOCK)
                token_grad[at] = (acc[at] + in_part[at]).astype(LOW)

    reduce_2 = Reduce(p, lambda i: t_2.at[i], lambda k: landed_2.at[k], 32, send_sem, recv_sem, 5 * COPIES)
    reduce_i = Reduce(p, lambda i: t_i.at[i], lambda k: landed_i.at[k], 32, send_sem, recv_sem, 6 * COPIES)
    reduce_o = Reduce(p, lambda i: slope.at[i, :, pl.ds(1536, 512)], lambda k: w_i.at[k, :, pl.ds(1536, 512)], 32, send_sem, recv_sem, 7 * COPIES)
    reduce_q = Reduce(
        p,
        lambda i: slope.at[i, :, pl.ds(0, 1536)],
        lambda k: w_i.at[k, :, pl.ds(0, 1536)],
        32,
        send_sem,
        recv_sem,
        8 * COPIES,
    )
    reduce_v = Reduce(p, lambda i: v_terms.at[i], lambda k: v_landed.at[k], 16, send_sem, recv_sem, 9 * COPIES)

    def result_2():
        def put(n, total):
            f_2[rows_at(n, 32)] = total

        reduce_2.result(put)

    def halves_to(first_block):
        def put(n, total):
            xhat[first_block + 2 * n] = total[:, :1024]
            xhat[first_block + 2 * n + 1, :, : total.shape[1] - 1024] = total[:, 1024:]

        return put

    def column(block, n):
        return xhat[block + n // 8, :, 128 * (n % 8) : 128 * (n % 8) + 128]

    def result_i():
        reduce_i.result(halves_to(0))
        exchange("i", xhat.at[pl.ds(2 * peer, 2)], xhat.at[4:6])

    def result_i_out():
        got["i"]()
        for n in range(16):
            f_i[:, rows_at(2 * n + core, 128)] = column(2 * core, n)
            f_i[:, rows_at(2 * n + peer, 128)] = column(4, n)

    def result_o():
        def put(n, total):
            f_s[3][:, rows_at(n, 512)] = total

        reduce_o.result(put)

    def result_v():
        def put(n, total):
            group = 2 * lax.rem(me, 2) + core
            turned = total
            for n_group in (1, 2, 3):
                turned = jnp.where(group == n_group, pltpu.roll(total, 128 - 32 * n_group, 1), turned)
            is_short = lax.broadcasted_iota(jnp.int32, (16, 128), 0) < SHORT
            vec_grad[...] = jnp.where(is_short, turned, total)

        reduce_v.result(put)

    def result_q():
        reduce_q.result(halves_to(8))
        exchange("q", xhat.at[pl.ds(8 + 2 * peer, 2)], xhat.at[12:14])

    def result_q_out():
        got["q"]()
        for n in range(3):
            for owner, block in ((core, 8 + 2 * core), (peer, 12)):
                f_s[n][:, rows_at(owner, 512)] = xhat[block + n // 2, :, 512 * (n % 2) : 512 * (n % 2) + 512]

    gather_v.run(B1)
    gather_o.run(A2)
    gather_i.run(A0)
    gather_q.run(B1, P0)
    gather_o.run(P0, B1)
    gather_v.run(P0)
    gather_i.run(B0)
    gather_o.run(P1)
    gather_q.run(Ap, A2)
    gather_v.run(A2)
    gather_i.run(B1)
    gather_v.run(P1)
    gather_q.run(P1)
    gather_v.run(Ao)
    gather_q.run(B2)
    gather_i.run(Z1, Z2)
    gather_v.run(Ap, B3)
    gather_i.run(Z3)
    gather_v.run(E1)
    gather_o.run(Ap)
    gather_v.run(B4, B2)
    gather_o.run(Ao)
    gather_q.run(Ao)
    gather_o.run(B4, B2)
    gather_v.run(B5)
    gather_q.run(B3)
    gather_i.run(P1)
    gather_q.run(B4, E1)
    gather_o.run(B3)
    gather_q.run(B5, E2)
    gather_o.run(B5)
    gather_2.run(Z2)
    gather_i.run(P0)
    gather_o.run(E2)
    gather_2.run(Z1)
    gather_i.run(A2)
    gather_o.run(E1)
    gather_i.run(B2)
    gather_v.run(E3)
    gather_2.run(Z3)
    gather_v.run(E2)
    gather_o.run(E3)
    relay_output()
    gather_2.run(B1)
    short_params()
    gather_i.run(Ao)
    gather_q.run(E3)
    gather_i.run(B4)
    project(1)
    gather_i.run(B3)
    project(0)
    attention(0, 0)
    attention(0, 1)
    branch(0)
    attention(1, 0)
    gather_2.run(A2)
    attention(1, 1)
    gather_i.run(B5)
    branch(1)
    attention(2, 0)
    gather_2.run(B2)
    gather_i.run(Ap)
    attention(2, 1)
    gather_2.run(P1)
    branch(2)
    attention(3, 0)
    attention(3, 1)
    gather_2.run(B3)
    gather_i.run(E3)
    gather_2.run(P0)
    branch(3)
    norm_first(0)
    gather_i.run(E2)
    norm_first(1)
    gather_2.run(Ao, B4)
    gather_i.run(E1)
    inner(0)
    inner(1)
    gather_2.run(Ap)
    inner(2)
    inner(3)
    gather_2.run(B5)
    outer(0)
    gather_2.run(E1)
    outer(1)
    gather_2.run(E2)
    outer(2)
    gather_2.run(E3)
    outer(3)
    norm_second(0)
    norm_second(1)
    outer_terms(0, 0)
    reduce_2.run(Ap)
    outer_terms(0, 1)
    outer_terms(1)
    reduce_2.run(P0)
    outer_terms(2)
    reduce_2.run(B5)
    outer_terms(3)
    reduce_2.run(B3, P1)
    d_inner(0)
    reduce_2.run(B4, B2)
    d_inner(1)
    d_inner(2)
    d_inner(3)
    inner_terms(0)
    reduce_i.run(P0)
    reduce_2.run(A2)
    inner_terms(1)
    reduce_i.run(P1)
    reduce_2.run(Ao)
    inner_terms(2)
    inner_terms(3)
    reduce_i.run(B5)
    d_first(0)
    reduce_2.run(Z2, B1)
    reduce_i.run(B3)
    d_first(1)
    d_first(2)
    reduce_2.run(Zo)
    d_first(3)
    norm_first_back(0)
    reduce_i.run(B4)
    norm_first_back(1)
    reduce_i.run(Ao, B0, B2)
    reduce_2.run(Zp)
    reduce_i.run(Ap)
    reduce_2.run(A0)
    reduce_i.run(B1)
    output_terms()
    reduce_2.run(B0)
    d_mixed()
    reduce_i.run(A2)
    attention_back(0, 0)
    reduce_o.run(B3, P1)
    attention_back(0, 1)
    attention_back(1, 0)
    reduce_i.run(Zo)
    reduce_o.run(P0, B5)
    attention_back(1, 1)
    attention_back(2, 0)
    reduce_i.run(Zp)
    reduce_o.run(B1, B4)
    attention_back(2, 1)
    reduce_i.run(Z2)
    attention_back(3, 0)
    reduce_i.run(A0)
    reduce_o.run(B2)
    attention_back(3, 1)
    query_terms(0)
    reduce_q.run(P0)
    reduce_o.run(A2)
    query_terms(1)
    reduce_o.run(Ao, A0)
    query_terms(2)
    reduce_q.run(B5, B4)
    reduce_o.run(Z2)
    query_terms(3)
    reduce_o.run(Zo)
    d_tokens(0)
    reduce_q.run(Ao)
    d_tokens(1)
    reduce_q.run(Ap)
    result_2()
    reduce_q.run(P1)
    d_tokens(2)
    d_tokens(3)
    reduce_q.run(Zo, B3, B2)
    short_sums()
    short_terms()
    reduce_v.run(P0, P1, B2)
    reduce_q.run(Zp)
    reduce_v.run(B5)
    reduce_q.run(A2)
    reduce_v.run(Ap, B3)
    reduce_o.run(Ap)
    result_i()
    reduce_v.run(Ao)
    reduce_q.run(B1, Z2)
    reduce_v.run(B4)
    reduce_q.run(B0)
    reduce_o.run(Zp)
    reduce_v.run(Zo, Zp, A2)
    reduce_q.run(A0)
    reduce_v.run(B1, Z2)
    tokens_out()
    result_i_out()
    reduce_v.run(A0, B0)
    reduce_o.run(B0)
    result_q()
    result_o()
    result_q_out()
    result_v()

    for each in (gather_q, gather_o, gather_i, gather_2, gather_v):
        each.finish()
    for each in (reduce_q, reduce_o, reduce_i, reduce_2, reduce_v):
        each.finish()
    for each in pending + list(sent.values()):
        each()


def layer(*arrays):
    def low(*shape):
        return pltpu.VMEM(shape, LOW)

    def full(*shape):
        return pltpu.VMEM(shape, F32)

    hbm = pl.BlockSpec(memory_space=pl.ANY)
    vmem = pl.BlockSpec(memory_space=pltpu.VMEM)
    smem = pl.BlockSpec(memory_space=pltpu.SMEM)
    scratch = [
        low(1024, 1024),
        low(1024, 1536),
        low(1024, 512),
        full(512, 1024),
        full(512, 1024),
        full(512, 1024),
        full(16, 32, 1024),
        full(512, 128),
        low(16, 2, 32, 1024),
        low(16, 64, 2048),
        low(16, 64, 2048),
        low(1024, 1024),
        low(16, 64, 1536),
        low(16, 2, 32, 1024),
        low(16, 64, 2048),
        low(16, 128, 1024),
        low(16, 128, 1024),
        low(16, 64, 2048),
        low(COPIES, 128, 1024),
        low(COPIES, 64, 2048),
        low(32, 1536),
        low(32, 2048),
        full(2, 8, 256),
        low(2, 16, 16, 128),
        full(16, 1024),
        full(8, 2048),
        full(SHORT, 8, 1024),
        full(8, 2048),
        full(8, 1024),
        full(8, 1024),
        full(16, 16, 128),
        full(COPIES, 16, 128),
        full(16, 128),
        pltpu.SemaphoreType.DMA((19,)),
        pltpu.SemaphoreType.DMA((26,)),
        pltpu.SemaphoreType.DMA((26,)),
        pltpu.SemaphoreType.DMA((10 * COPIES,)),
        pltpu.SemaphoreType.DMA((10 * COPIES,)),
        pltpu.SemaphoreType.REGULAR,
    ] + [full(1, 32)] * SHORT + [full(1, 128)]
    shape = jax.ShapeDtypeStruct
    return pl.pallas_call(
        layer_kernel,
        out_shape=(
            pltpu.VMEM((512, 1024), LOW),
            pltpu.VMEM((512, 1024), LOW),
            pltpu.VMEM((32, 1024), F32),
            pltpu.VMEM((32, 1024), F32),
            pltpu.VMEM((32, 1024), F32),
            pltpu.VMEM((32, 1024), F32),
            pltpu.VMEM((32, 4096), F32),
            pltpu.VMEM((128, 1024), F32),
            pltpu.VMEM((16, 128), F32),
        ),
        in_specs=[hbm, smem] + [hbm] * (7 + SHORT + 1),
        out_specs=(vmem,) * 9,
        scratch_shapes=scratch,
        compiler_params=pltpu.CompilerParams(
            collective_id=0, has_side_effects=True, vmem_limit_bytes=VMEM_BYTES
        ),
        cost_estimate=pl.CostEstimate(flops=40_000_000_000, bytes_accessed=8 << 20, transcendentals=0),
    )(*arrays)


VMEM_BYTES = 60 << 20


def hand_over_kernel(*refs):
    sources, vec, targets, parts, sems = refs[:8], refs[8], refs[9:17], refs[17 : 17 + SHORT + 1], refs[-1]
    stores = [pltpu.make_async_copy(sources[n], targets[n], sems.at[n]) for n in range(8)]
    for store in stores:
        store.start()
    for n in range(SHORT):
        parts[n][...] = vec[n : n + 1, 0:32]
    parts[SHORT][...] = vec[SHORT : SHORT + 1, :]
    for store in stores:
        store.wait()


def hand_over(*results):
    hbm = pl.BlockSpec(memory_space=pl.ANY)
    vmem = pl.BlockSpec(memory_space=pltpu.VMEM)
    shape = jax.ShapeDtypeStruct
    return pl.pallas_call(
        hand_over_kernel,
        out_shape=tuple(shape(each.shape, each.dtype) for each in results[:8])
        + (shape((1, 32), F32),) * SHORT
        + (shape((1, 128), F32),),
        in_specs=[vmem] * 9,
        out_specs=(hbm,) * 8 + (vmem,) * (SHORT + 1),
        scratch_shapes=[pltpu.SemaphoreType.DMA((8,))],
        compiler_params=pltpu.CompilerParams(vmem_limit_bytes=8 << 20),
    )(*results)


def one_kernel_device(
    tokens,
    lengths,
    cotangent,
    query_weight,
    key_weight,
    value_weight,
    output_weight,
    query_bias,
    value_bias,
    output_bias,
    first_gain,
    first_shift,
    inner_weight,
    inner_bias,
    outer_weight,
    outer_bias,
    second_gain,
    second_shift,
):
    count, seq, width = tokens.shape
    rows = count * seq
    short = (query_bias, value_bias, output_bias, first_gain, first_shift, outer_bias, second_gain, second_shift)
    outs = layer(
        tokens.reshape(rows, width),
        lengths,
        cotangent.reshape(rows, width),
        query_weight,
        key_weight,
        value_weight,
        output_weight,
        inner_weight,
        outer_weight,
        *[each.reshape(1, -1) for each in short + (inner_bias,)],
    )
    outs = hand_over(*outs)
    layer_rows, token_grad, query_g, key_g, value_g, output_g, inner_g, outer_g, *part = outs
    part = [each.reshape(-1) for each in part]
    return (
        layer_rows.reshape(count, seq, width),
        token_grad.reshape(count, seq, width),
        query_g,
        key_g,
        value_g,
        output_g,
        part[BQ],
        part[BV],
        part[BO],
        part[G1],
        part[S1],
        inner_g,
        part[SHORT],
        outer_g,
        part[BF],
        part[G2],
        part[S2],
    )


epsilon = 1e-12


def normalize(hidden, gain, shift):
    center = hidden - jnp.mean(hidden, axis=-1, keepdims=True)
    spread = jnp.mean(center * center, axis=-1, keepdims=True)
    return center * lax.rsqrt(spread + epsilon) * gain + shift


def gelu_exact(inner):
    return jax.nn.gelu(inner, approximate=False)


def matmul(left, right):
    return jnp.dot(left, right, preferred_element_type=jnp.float32)


def matmul_left_t(left, right):
    return lax.dot_general(
        left, right, (((0,), (0,)), ((), ())), preferred_element_type=jnp.float32
    )


def matmul_right_t(left, right):
    return lax.dot_general(
        left, right, (((1,), (1,)), ((), ())), preferred_element_type=jnp.float32
    )


def row_sum(values):
    return jnp.sum(values.astype(jnp.float32), axis=0)


def per_device(
    tokens,
    lengths,
    cotangent,
    query_weight,
    key_weight,
    value_weight,
    output_weight,
    query_bias,
    value_bias,
    output_bias,
    first_gain,
    first_shift,
    inner_weight,
    inner_bias,
    outer_weight,
    outer_bias,
    second_gain,
    second_shift,
):
    attn_master = (
        query_weight,
        key_weight,
        value_weight,
        output_weight,
        query_bias,
        value_bias,
        output_bias,
        first_gain,
        first_shift,
    )
    ffn_master = (inner_weight, inner_bias, outer_weight, outer_bias, second_gain, second_shift)
    attn_half = [param.astype(jnp.bfloat16) for param in attn_master]
    ffn_half = [param.astype(jnp.bfloat16) for param in ffn_master]
    micro_count, rows, width = tokens.shape
    heads = width // HD
    owners = lax.axis_size(("dp", "fsdp"))
    scale = 1.0 / math.sqrt(HD)
    positions = jnp.arange(rows, dtype=jnp.int32)
    attn_totals = [
        jnp.zeros((param.shape[0] * owners,) + param.shape[1:], jnp.float32)
        for param in attn_master
    ]
    ffn_totals = [
        jnp.zeros((param.shape[0] * owners,) + param.shape[1:], jnp.float32) for param in ffn_master
    ]
    outputs_list = []
    token_grads_list = []
    for micro in range(micro_count):
        token_rows = tokens[micro]
        cot_rows = cotangent[micro].astype(jnp.float32)
        valid_keys = positions < lengths[micro]
        attn_full = (
            lax.all_gather(attn_half[0], ("dp", "fsdp"), axis=0, tiled=True),
            lax.all_gather(attn_half[1], ("dp", "fsdp"), axis=0, tiled=True),
            lax.all_gather(attn_half[2], ("dp", "fsdp"), axis=0, tiled=True),
            lax.all_gather(attn_half[3], ("dp", "fsdp"), axis=0, tiled=True),
            lax.all_gather(attn_half[4], ("dp", "fsdp"), axis=0, tiled=True),
            lax.all_gather(attn_half[5], ("dp", "fsdp"), axis=0, tiled=True),
            lax.all_gather(attn_half[6], ("dp", "fsdp"), axis=0, tiled=True),
            lax.all_gather(attn_half[7], ("dp", "fsdp"), axis=0, tiled=True),
            lax.all_gather(attn_half[8], ("dp", "fsdp"), axis=0, tiled=True),
        )
        query_use, key_use, value_use, output_use = (
            attn_full[0],
            attn_full[1],
            attn_full[2],
            attn_full[3],
        )
        bias_query = attn_full[4].astype(jnp.float32)
        bias_value = attn_full[5].astype(jnp.float32)
        bias_output = attn_full[6].astype(jnp.float32)
        gain_first = attn_full[7].astype(jnp.float32)
        shift_first = attn_full[8].astype(jnp.float32)
        query_rows = (matmul(token_rows, query_use) + bias_query).astype(jnp.bfloat16)
        key_rows = matmul(token_rows, key_use).astype(jnp.bfloat16)
        value_rows = (matmul(token_rows, value_use) + bias_value).astype(jnp.bfloat16)
        query_heads = query_rows.reshape(rows, heads, HD)
        key_heads = key_rows.reshape(rows, heads, HD)
        value_heads = value_rows.reshape(rows, heads, HD)

        def attention_scores():
            raw_scores = (
                jnp.einsum(
                    "qhd,khd->hqk", query_heads, key_heads, preferred_element_type=jnp.float32
                )
                * scale
            )
            return jnp.where(valid_keys[None, None, :], raw_scores, -1000000000.0)

        scores = attention_scores()
        peak = jnp.max(scores, axis=-1, keepdims=True)
        log_total = peak + jnp.log(jnp.sum(jnp.exp(scores - peak), axis=-1, keepdims=True))
        probs_low = jnp.exp(scores - log_total).astype(jnp.bfloat16)
        mixed = (
            jnp.einsum("hqk,khd->qhd", probs_low, value_heads, preferred_element_type=jnp.float32)
            .reshape(rows, width)
            .astype(jnp.bfloat16)
        )
        residual = token_rows.astype(jnp.float32) + matmul(mixed, output_use) + bias_output
        first = normalize(residual, gain_first, shift_first)
        first_low = first.astype(jnp.bfloat16)
        ffn_full = (
            lax.all_gather(ffn_half[0], ("dp", "fsdp"), axis=0, tiled=True),
            lax.all_gather(ffn_half[1], ("dp", "fsdp"), axis=0, tiled=True),
            lax.all_gather(ffn_half[2], ("dp", "fsdp"), axis=0, tiled=True),
            lax.all_gather(ffn_half[3], ("dp", "fsdp"), axis=0, tiled=True),
            lax.all_gather(ffn_half[4], ("dp", "fsdp"), axis=0, tiled=True),
            lax.all_gather(ffn_half[5], ("dp", "fsdp"), axis=0, tiled=True),
        )
        inner = matmul(first_low, ffn_full[0]) + ffn_full[1].astype(jnp.float32)
        active = gelu_exact(inner).astype(jnp.bfloat16)
        second_in = first + matmul(active, ffn_full[2]) + ffn_full[3].astype(jnp.float32)
        gain_second = ffn_full[4].astype(jnp.float32)
        shift_second = ffn_full[5].astype(jnp.float32)
        layer_rows, pull_second = jax.vjp(normalize, second_in, gain_second, shift_second)
        outputs_list.append(layer_rows.astype(jnp.bfloat16))
        ffn_full = (
            lax.all_gather(ffn_half[0], ("dp", "fsdp"), axis=0, tiled=True),
            lax.all_gather(ffn_half[1], ("dp", "fsdp"), axis=0, tiled=True),
            lax.all_gather(ffn_half[2], ("dp", "fsdp"), axis=0, tiled=True),
            lax.all_gather(ffn_half[3], ("dp", "fsdp"), axis=0, tiled=True),
            lax.all_gather(ffn_half[4], ("dp", "fsdp"), axis=0, tiled=True),
            lax.all_gather(ffn_half[5], ("dp", "fsdp"), axis=0, tiled=True),
        )
        d_second, d_gain_second, d_shift_second = pull_second(cot_rows)
        d_outer = d_second.astype(jnp.bfloat16)
        ffn_totals[2] = ffn_totals[2] + matmul_left_t(active, d_outer)
        ffn_totals[3] = ffn_totals[3] + row_sum(d_outer)
        ffn_totals[4] = ffn_totals[4] + d_gain_second
        ffn_totals[5] = ffn_totals[5] + d_shift_second
        d_active = matmul_right_t(d_outer, ffn_full[2])
        gelu_value, pull_gelu = jax.vjp(gelu_exact, inner)
        (d_inner,) = pull_gelu(d_active)
        d_inner_low = d_inner.astype(jnp.bfloat16)
        ffn_totals[0] = ffn_totals[0] + matmul_left_t(first_low, d_inner_low)
        ffn_totals[1] = ffn_totals[1] + row_sum(d_inner_low)
        d_first = matmul_right_t(d_inner_low, ffn_full[0]) + d_second
        attn_full = (
            lax.all_gather(attn_half[0], ("dp", "fsdp"), axis=0, tiled=True),
            lax.all_gather(attn_half[1], ("dp", "fsdp"), axis=0, tiled=True),
            lax.all_gather(attn_half[2], ("dp", "fsdp"), axis=0, tiled=True),
            lax.all_gather(attn_half[3], ("dp", "fsdp"), axis=0, tiled=True),
            lax.all_gather(attn_half[4], ("dp", "fsdp"), axis=0, tiled=True),
            lax.all_gather(attn_half[5], ("dp", "fsdp"), axis=0, tiled=True),
            lax.all_gather(attn_half[6], ("dp", "fsdp"), axis=0, tiled=True),
            lax.all_gather(attn_half[7], ("dp", "fsdp"), axis=0, tiled=True),
            lax.all_gather(attn_half[8], ("dp", "fsdp"), axis=0, tiled=True),
        )
        query_use, key_use, value_use, output_use = (
            attn_full[0],
            attn_full[1],
            attn_full[2],
            attn_full[3],
        )
        norm_value, pull_first = jax.vjp(
            normalize, residual, attn_full[7].astype(jnp.float32), attn_full[8].astype(jnp.float32)
        )
        d_residual, d_gain_first, d_shift_first = pull_first(d_first)
        attn_totals[7] = attn_totals[7] + d_gain_first
        attn_totals[8] = attn_totals[8] + d_shift_first
        d_branch = d_residual.astype(jnp.bfloat16)
        attn_totals[3] = attn_totals[3] + matmul_left_t(mixed, d_branch)
        attn_totals[6] = attn_totals[6] + row_sum(d_branch)
        d_mixed = matmul_right_t(d_branch, output_use).astype(jnp.bfloat16).reshape(rows, heads, HD)
        scores = attention_scores()
        probs = jnp.exp(scores - log_total)
        probs_low = probs.astype(jnp.bfloat16)
        d_probs = jnp.einsum(
            "qhd,khd->hqk", d_mixed, value_heads, preferred_element_type=jnp.float32
        )
        d_values = jnp.einsum(
            "hqk,qhd->khd", probs_low, d_mixed, preferred_element_type=jnp.float32
        ).reshape(rows, width)
        delta_rows = jnp.sum(probs * d_probs, axis=-1, keepdims=True)
        d_scores = (probs * (d_probs - delta_rows)).astype(jnp.bfloat16)
        d_queries = (
            (
                jnp.einsum("hqk,khd->qhd", d_scores, key_heads, preferred_element_type=jnp.float32)
                * scale
            )
            .reshape(rows, width)
            .astype(jnp.bfloat16)
        )
        d_keys = (
            jnp.einsum(
                "hqk,qhd->khd", d_scores, query_heads, preferred_element_type=jnp.float32
            ).reshape(rows, width)
            * scale
        )
        key_low = d_keys.astype(jnp.bfloat16)
        value_low = d_values.astype(jnp.bfloat16)
        attn_totals[0] = attn_totals[0] + matmul_left_t(token_rows, d_queries)
        attn_totals[1] = attn_totals[1] + matmul_left_t(token_rows, key_low)
        attn_totals[2] = attn_totals[2] + matmul_left_t(token_rows, value_low)
        attn_totals[4] = attn_totals[4] + row_sum(d_queries)
        attn_totals[5] = attn_totals[5] + row_sum(value_low)
        token_grad = (
            d_residual
            + matmul_right_t(d_queries, query_use)
            + matmul_right_t(key_low, key_use)
            + matmul_right_t(value_low, value_use)
        )
        token_grads_list.append(token_grad.astype(jnp.bfloat16))
    attn_shards = (
        lax.psum_scatter(attn_totals[0], ("dp", "fsdp"), scatter_dimension=0, tiled=True),
        lax.psum_scatter(attn_totals[1], ("dp", "fsdp"), scatter_dimension=0, tiled=True),
        lax.psum_scatter(attn_totals[2], ("dp", "fsdp"), scatter_dimension=0, tiled=True),
        lax.psum_scatter(attn_totals[3], ("dp", "fsdp"), scatter_dimension=0, tiled=True),
        lax.psum_scatter(attn_totals[4], ("dp", "fsdp"), scatter_dimension=0, tiled=True),
        lax.psum_scatter(attn_totals[5], ("dp", "fsdp"), scatter_dimension=0, tiled=True),
        lax.psum_scatter(attn_totals[6], ("dp", "fsdp"), scatter_dimension=0, tiled=True),
        lax.psum_scatter(attn_totals[7], ("dp", "fsdp"), scatter_dimension=0, tiled=True),
        lax.psum_scatter(attn_totals[8], ("dp", "fsdp"), scatter_dimension=0, tiled=True),
    )
    ffn_shards = (
        lax.psum_scatter(ffn_totals[0], ("dp", "fsdp"), scatter_dimension=0, tiled=True),
        lax.psum_scatter(ffn_totals[1], ("dp", "fsdp"), scatter_dimension=0, tiled=True),
        lax.psum_scatter(ffn_totals[2], ("dp", "fsdp"), scatter_dimension=0, tiled=True),
        lax.psum_scatter(ffn_totals[3], ("dp", "fsdp"), scatter_dimension=0, tiled=True),
        lax.psum_scatter(ffn_totals[4], ("dp", "fsdp"), scatter_dimension=0, tiled=True),
        lax.psum_scatter(ffn_totals[5], ("dp", "fsdp"), scatter_dimension=0, tiled=True),
    )
    return (
        jnp.stack(outputs_list),
        jnp.stack(token_grads_list),
        attn_shards[0],
        attn_shards[1],
        attn_shards[2],
        attn_shards[3],
        attn_shards[4],
        attn_shards[5],
        attn_shards[6],
        attn_shards[7],
        attn_shards[8],
        ffn_shards[0],
        ffn_shards[1],
        ffn_shards[2],
        ffn_shards[3],
        ffn_shards[4],
        ffn_shards[5],
    )


def solution(mesh):
    in_specs = (
        P(("dp", "fsdp"), None, None),
        P(("dp", "fsdp")),
        P(("dp", "fsdp"), None, None),
        P(("dp", "fsdp"), None),
        P(("dp", "fsdp"), None),
        P(("dp", "fsdp"), None),
        P(("dp", "fsdp"), None),
        P(("dp", "fsdp")),
        P(("dp", "fsdp")),
        P(("dp", "fsdp")),
        P(("dp", "fsdp")),
        P(("dp", "fsdp")),
        P(("dp", "fsdp"), None),
        P(("dp", "fsdp")),
        P(("dp", "fsdp"), None),
        P(("dp", "fsdp")),
        P(("dp", "fsdp")),
        P(("dp", "fsdp")),
    )
    out_specs = (
        P(("dp", "fsdp"), None, None),
        P(("dp", "fsdp"), None, None),
        P(("dp", "fsdp"), None),
        P(("dp", "fsdp"), None),
        P(("dp", "fsdp"), None),
        P(("dp", "fsdp"), None),
        P(("dp", "fsdp")),
        P(("dp", "fsdp")),
        P(("dp", "fsdp")),
        P(("dp", "fsdp")),
        P(("dp", "fsdp")),
        P(("dp", "fsdp"), None),
        P(("dp", "fsdp")),
        P(("dp", "fsdp"), None),
        P(("dp", "fsdp")),
        P(("dp", "fsdp")),
        P(("dp", "fsdp")),
    )
    one_kernel = dict(mesh.shape) == {"dp": 16, "fsdp": 2}
    device = one_kernel_device if one_kernel else per_device
    return jax.shard_map(
        device, mesh=mesh, in_specs=in_specs, out_specs=out_specs, check_vma=False
    )
```
